32 devices in a mesh: mol: 2 (over x), pair: 8 (over z, y), aux: 2 (over core).
Axes of the slice: x: 2, y: 2, z: 4, core: 2. Of those that a mesh axis runs over, the one named last changes fastest.
Arguments:
- three_index: bfloat16 [224, 256, 4096], P(('mol', 'pair'), None, 'aux'), parts along dimension 0, may hold values from -0.03125 to 0.03125
- density: bfloat16 [224, 256, 256], P(('mol', 'pair')), parts along dimension 0, may hold values from -6 to 6
- screen: int32 [224, 256], P(('mol', 'pair')), parts along dimension 0, may hold values 0 or 1
- pair_shells: int32 [224, 2], P(('mol', 'pair')), parts along dimension 0, may hold values from 0 to 1249, as said below
- home_slot: int32 [224], P('mol'), parts along dimension 0, may hold values from 0 to 111, as said below
- mirror_slot: int32 [224], P('mol'), parts along dimension 0, may hold values from 0 to 111, as said below
Outputs:
- coulomb_rows: bfloat16 [224, 256, 256], P(('mol', 'pair'), None, 'aux'), parts along dimension 0
- coulomb_cols: bfloat16 [224, 256, 256], P(('mol', 'pair'), None, 'aux'), parts along dimension 0
The draws below stay inside these ranges and needn't reach their ends.
There are 2 independent parts, one for each index of `mol`. The reference program is written for one: setup_inputs(seed, part) draws one part's arguments, and reference() takes and returns one part's arrays. A program takes and returns all parts, laid end to end along the dimension named above; each array names one. Nothing has to cross between parts.
Inputs may be any that keep to these rules, and one draw needn't show every extreme that they name: `pair_shells`: the column shell is the row shell or one of the next two shells, modulo 1250. `home_slot`: a permutation; rows k * 14 to (k + 1) * 14 - 1 belong to device k, and of the 14 blocks of one device at most 3 have home rows on any one device, exactly 3 on some device. `mirror_slot`: as for home_slot.
All inputs are finite; a program needn't handle non-finite values. No bound on the sum of `screen` on one device may be relied on, other than what follows from the above.
Results may differ from the reference program's by a relative error of at most 0.0048.
Values may be sent and summed in bfloat16 or wider, within the bound.
No kernel may reach another device: no remote copies, remote signals or barrier semaphores. Data moves between devices by JAX's collectives and lax.ppermute only.
A program may use at most 192 MiB of HBM per device.

```python
import jax
import jax.numpy as jnp

SH = 16
FN = 256
SHELLS = 1250
AUX = 4096
NDENS = 256
PAIRS_DEV = 14
BLOCKS = 112
CAP = 3


def slot_table(key, salt):
    key = jax.random.fold_in(key, salt)
    key_spare, key_first, key_order, key_rows = jax.random.split(key, 4)
    devices = BLOCKS // PAIRS_DEV
    spare = jax.random.permutation(key_spare, jnp.tile(jnp.arange(1, devices, dtype=jnp.int32), CAP))
    first = jax.random.randint(key_first, (), 0, devices, dtype=jnp.int32)
    offsets = jnp.concatenate([jnp.full((CAP,), first, jnp.int32), (first + spare[:PAIRS_DEV - CAP]) % devices])
    offsets = jax.random.permutation(key_order, offsets)
    orders = jax.vmap(lambda one_key: jax.random.permutation(one_key, PAIRS_DEV))(jax.random.split(key_rows, devices))
    source = jnp.arange(devices, dtype=jnp.int32)[:, None]
    target = (source + offsets[None, :]) % devices
    within = orders[target, jnp.arange(PAIRS_DEV, dtype=jnp.int32)[None, :]].astype(jnp.int32)
    return (target * PAIRS_DEV + within).reshape(-1).astype(jnp.int32)


def draw_home_slot(key, part):
    return slot_table(key, 5)


def draw_mirror_slot(key, part):
    return slot_table(key, 7)


def draw_pair_shells(key, part):
    key = jax.random.fold_in(key, 11)
    key_row, key_step = jax.random.split(key)
    row_shell = jax.random.randint(key_row, (BLOCKS,), 0, SHELLS, dtype=jnp.int32)
    stride = jax.random.randint(key_step, (BLOCKS,), 0, 3, dtype=jnp.int32)
    return jnp.stack([row_shell, (row_shell + stride) % SHELLS], axis=1).astype(jnp.int32)


def with_ends(entries, stream_key, smallest, high):
    spot = [jax.random.randint(jax.random.fold_in(stream_key, axis), (), 0, length) for axis, length in enumerate(entries.shape)]
    longest = entries.shape.index(max(entries.shape))
    next_to = spot[:longest] + [(spot[longest] + 1) % entries.shape[longest]] + spot[longest + 1:]
    return entries.at[tuple(spot)].set(smallest).at[tuple(next_to)].set(high)


def levels(own_key, extent, cuts, least, top_value):
    def one(position, parts):
        heights = jax.random.uniform(jax.random.fold_in(jax.random.fold_in(own_key, 6), position), (parts,), jnp.float32, least / len(cuts), top_value / len(cuts))
        return jnp.repeat(jnp.exp(heights), extent[position] // parts).reshape((-1,) + (1,) * (len(extent) - position - 1))

    gain = one(*cuts[0])
    for cut in cuts[1:]:
        gain = gain * one(*cut)
    return gain


def noise(rng, extent, spread, most, shards=(), kind=jnp.bfloat16):
    entries = spread * jax.random.normal(rng, extent, jnp.float32)
    if shards:
        entries = entries * levels(rng, extent, shards, -0.22, 0.18)
    return jnp.clip(entries, -most, most).astype(kind)


def setup_inputs(seed: int = 0, part: int = 0) -> dict:
    key_of = jax.random.split(jax.random.key(seed), 7)
    own_keys = jax.random.split(jax.random.fold_in(key_of[6], part), 7)
    return {
        "three_index": noise(own_keys[0], (BLOCKS, FN, AUX), (BLOCKS * FN) ** -0.5, 0.03125, ((0, 8), (2, 2))),
        "density": noise(own_keys[1], (BLOCKS, FN, NDENS), 1.0, 6.0, ((0, 8),)),
        "screen": with_ends((jax.random.randint(own_keys[2], (BLOCKS, FN), 0, 4) < 3).astype(jnp.int32), jax.random.fold_in(own_keys[2], 1), 0, 1),
        "pair_shells": draw_pair_shells(jax.random.fold_in(jax.random.fold_in(key_of[6], part), 71), part),
        "home_slot": draw_home_slot(jax.random.fold_in(jax.random.fold_in(key_of[6], part), 71), part),
        "mirror_slot": draw_mirror_slot(jax.random.fold_in(jax.random.fold_in(key_of[6], part), 71), part),
    }


def reference(three_index, density, screen, pair_shells, home_slot, mirror_slot):
    weight = jnp.where(pair_shells[:, 0] != pair_shells[:, 1], 2.0, 1.0).astype(jnp.float32)
    gathered = density[home_slot]
    factor = screen.astype(jnp.float32) * weight[:, None]
    fitted = (gathered.astype(jnp.float32) * factor[:, :, None]).astype(jnp.bfloat16)
    flat_integrals = three_index.reshape(BLOCKS * FN, AUX)
    flat_fitted = fitted.reshape(BLOCKS * FN, NDENS)
    coef = jnp.dot(flat_integrals.T, flat_fitted, preferred_element_type=jnp.float32).astype(jnp.bfloat16)
    summed = jnp.dot(flat_integrals, coef, preferred_element_type=jnp.float32).reshape(BLOCKS, FN, NDENS)
    coulomb = (summed * screen.astype(jnp.float32)[:, :, None]).astype(jnp.bfloat16)
    turned = jnp.swapaxes(coulomb.reshape(BLOCKS, SH, SH, NDENS), 1, 2).reshape(BLOCKS, FN, NDENS)
    coulomb_rows = jnp.zeros_like(coulomb).at[home_slot].set(coulomb)
    coulomb_cols = jnp.zeros_like(coulomb).at[mirror_slot].set(turned)
    return coulomb_rows, coulomb_cols
```

```python
import functools
import math

import jax
import jax.numpy as jnp
from jax import lax
from jax.experimental import pallas as pl
from jax.experimental.pallas import tpu as pltpu
from jax.sharding import PartitionSpec as P

VMEM_BYTES = 48 * 1024 * 1024


def tables(slots, devices, blocks_dev, me):
    total = slots.shape[0]
    numbers = jnp.arange(total, dtype=jnp.int32)
    source = numbers // blocks_dev
    target = slots // blocks_dev
    joined = source * devices + target
    earlier = (joined[:, None] == joined[None, :]) & (numbers[None, :] < numbers[:, None])
    rank = jnp.sum(earlier.astype(jnp.int32), axis=1)
    own_target = lax.dynamic_slice_in_dim(target, me * blocks_dev, blocks_dev, 0)
    own_rank = lax.dynamic_slice_in_dim(rank, me * blocks_dev, blocks_dev, 0)
    rows = me * blocks_dev + jnp.arange(blocks_dev, dtype=jnp.int32)
    hot = slots[None, :] == rows[:, None]
    row_source = jnp.sum(jnp.where(hot, source[None, :], 0), axis=1)
    row_rank = jnp.sum(jnp.where(hot, rank[None, :], 0), axis=1)
    return own_target, own_rank, row_source, row_rank


def scatter_density_kernel(devices, blocks, width, table, density, *rest):
    sends, sems = rest[:devices], rest[devices]
    column = pl.multiple_of(table[2 * blocks] * width, width)

    def copy(row, step):
        return pltpu.make_async_copy(
            density.at[row, :, pl.ds(column, width)],
            sends[step].at[table[blocks + row]],
            sems.at[row],
        )

    for row in range(blocks):
        for step in range(devices):

            @pl.when(table[row] == step)
            def _():
                copy(row, step).start()

    for row in range(blocks):
        copy(row, 0).wait()


def gather_kernel(devices, blocks, groups, table, *rest):
    received, outs, sems = rest[:devices], rest[devices : devices + groups], rest[devices + groups]

    def copy(group, row, step):
        return pltpu.make_async_copy(
            received[step].at[table[(2 * group + 1) * blocks + row]],
            outs[group].at[row],
            sems.at[group, row],
        )

    for group in range(groups):
        for row in range(blocks):
            for step in range(devices):

                @pl.when(table[2 * group * blocks + row] == step)
                def _():
                    copy(group, row, step).start()

    for group in range(groups):
        for row in range(blocks):
            copy(group, row, 0).wait()


def fit_kernel(devices, some, steps, table, factor, own, other, integrals, *rest):
    own_part, sends, total = rest[0], rest[1:devices], rest[devices]
    step = pl.program_id(0)
    width = own_part.shape[1]

    @pl.when(step == 0)
    def _():
        total[...] = jnp.zeros_like(total)

    turned = []
    for b in range(some):
        both = jnp.concatenate([own[b], other[b]], axis=1)
        turned.append(both.T * factor[b])
    fitted = jnp.concatenate(turned, axis=1)
    flat = integrals.reshape(some * integrals.shape[1], integrals.shape[2])
    for chunk in range(devices):
        at = pl.ds(chunk * width, width)
        total[:, at] += jnp.dot(fitted, flat[:, at], preferred_element_type=jnp.float32)

    @pl.when(step == steps - 1)
    def _():
        for d in range(devices):
            chunk = lax.rem(table[0] + d, devices)
            value = total[:, pl.ds(pl.multiple_of(chunk * width, width), width)]
            if d == 0:
                own_part[...] = value
            else:
                sends[d - 1][...] = value.astype(jnp.bfloat16)


def apply_kernel(devices, some, table, integrals, *rest):
    chunks, own, other = rest[:devices], rest[devices], rest[devices + 1]
    width = chunks[0].shape[1]
    half = own.shape[2]
    flat = integrals.reshape(some * integrals.shape[1], integrals.shape[2])
    total = None
    for d in range(devices):
        chunk = lax.rem(table[0] + devices - d, devices)
        term = lax.dot_general(
            flat[:, pl.ds(pl.multiple_of(chunk * width, width), width)],
            chunks[d][...],
            (((1,), (1,)), ((), ())),
            preferred_element_type=jnp.float32,
        )
        total = term if total is None else total + term
    own[...] = total[:, :half].reshape(own.shape)
    other[...] = total[:, half:].reshape(other.shape)


def scatter_coulomb_kernel(devices, blocks, shell, cap, table, screen, own, other, *rest):
    sends = rest[:devices]
    turning, row_buf, col_buf, sems = rest[devices:]
    block = pl.program_id(0)
    pairs, half = own.shape[1], own.shape[2]
    keep = jnp.broadcast_to(screen[0], (half, pairs)).T
    value = (own[0] + other[0]) * keep
    turning[...] = value
    row_buf[block] = value.astype(jnp.bfloat16)
    for j in range(shell):
        col_buf[block, pl.ds(j * shell, shell), :] = turning[
            pl.ds(j, shell, stride=shell), :
        ].astype(jnp.bfloat16)

    def copy(group, b, step):
        buf = (row_buf, col_buf)[group]
        return pltpu.make_async_copy(
            buf.at[b],
            sends[step].at[group * cap + table[(2 * group + 1) * blocks + b]],
            sems.at[group, b],
        )

    for group in range(2):
        for step in range(devices):

            @pl.when(table[2 * group * blocks + block] == step)
            def _():
                copy(group, block, step).start()

    @pl.when(block == blocks - 1)
    def _():
        for group in range(2):
            for b in range(blocks):
                copy(group, b, 0).wait()


def local(three_index, density, screen, pair_shells, home_slot, mirror_slot):
    blocks, pairs, aux_dev = three_index.shape
    ndens = density.shape[2]
    shell = math.isqrt(pairs)
    n = lax.axis_size("pair")
    parts = lax.axis_size("aux")
    me = lax.axis_index("pair")
    core = lax.axis_index("aux")
    half = ndens // parts
    width = aux_dev // n
    cap = 2 + (blocks - 1) // n
    some = 2 if blocks % 2 == 0 else 1
    steps = blocks // some
    any_spec = pl.BlockSpec(memory_space=pl.ANY)
    params = pltpu.CompilerParams(vmem_limit_bytes=VMEM_BYTES)

    def shift(x, d):
        return lax.ppermute(x, "pair", [(s, (s + d) % n) for s in range(n)])

    def swap(x):
        return lax.ppermute(x, "aux", [(s, (s + 1) % parts) for s in range(parts)])

    home_target, home_rank, home_source, home_row_rank = tables(home_slot, n, blocks, me)
    mirror_target, mirror_rank, mirror_source, mirror_row_rank = tables(
        mirror_slot, n, blocks, me
    )
    ints = functools.partial(jnp.concatenate, axis=0)

    send_table = ints([(home_source - me) % n, home_row_rank, core[None].astype(jnp.int32)])
    slots = jax.ShapeDtypeStruct((cap, pairs, half), jnp.bfloat16)
    sends = pl.pallas_call(
        functools.partial(scatter_density_kernel, n, blocks, half),
        out_shape=[slots] * n,
        grid_spec=pltpu.PrefetchScalarGridSpec(
            num_scalar_prefetch=1,
            grid=(),
            in_specs=[any_spec],
            out_specs=[any_spec] * n,
            scratch_shapes=[pltpu.SemaphoreType.DMA((blocks,))],
        ),
        name="scatter_density",
    )(send_table, density)
    received = [sends[0]] + [shift(sends[d], d) for d in range(1, n)]
    pick_table = ints([(me - home_target) % n, home_rank])
    own = pl.pallas_call(
        functools.partial(gather_kernel, n, blocks, 1),
        out_shape=[jax.ShapeDtypeStruct((blocks, pairs, half), jnp.bfloat16)],
        grid_spec=pltpu.PrefetchScalarGridSpec(
            num_scalar_prefetch=1,
            grid=(),
            in_specs=[any_spec] * n,
            out_specs=[any_spec],
            scratch_shapes=[pltpu.SemaphoreType.DMA((1, blocks))],
        ),
        name="gather_density",
    )(pick_table, *received)[0]
    other = swap(own)

    weight = jnp.where(pair_shells[:, 0] != pair_shells[:, 1], 2.0, 1.0)
    factor = (screen.astype(jnp.float32) * weight[:, None]).astype(jnp.bfloat16)
    where = me[None].astype(jnp.int32)
    block_map = lambda i, t: (i, 0, 0)
    whole_map = lambda i, t: (0, 0)
    parts_fit = pl.pallas_call(
        functools.partial(fit_kernel, n, some, steps),
        out_shape=[jax.ShapeDtypeStruct((ndens, width), jnp.float32)]
        + [jax.ShapeDtypeStruct((ndens, width), jnp.bfloat16)] * (n - 1),
        grid_spec=pltpu.PrefetchScalarGridSpec(
            num_scalar_prefetch=1,
            grid=(steps,),
            in_specs=[
                pl.BlockSpec((some, 1, pairs), block_map),
                pl.BlockSpec((some, pairs, half), block_map),
                pl.BlockSpec((some, pairs, half), block_map),
                pl.BlockSpec((some, pairs, aux_dev), block_map),
            ],
            out_specs=[pl.BlockSpec((ndens, width), whole_map)] * n,
            scratch_shapes=[pltpu.VMEM((ndens, aux_dev), jnp.float32)],
        ),
        compiler_params=params,
        name="fit",
    )(where, factor[:, None, :], own, other, three_index)
    summed = parts_fit[0]
    for d in range(1, n):
        summed = summed + shift(parts_fit[d], d).astype(jnp.float32)
    coef = summed.astype(jnp.bfloat16)
    chunks = [coef] + [shift(coef, d) for d in range(1, n)]

    mine, theirs = pl.pallas_call(
        functools.partial(apply_kernel, n, some),
        out_shape=[jax.ShapeDtypeStruct((blocks, pairs, half), jnp.float32)] * 2,
        grid_spec=pltpu.PrefetchScalarGridSpec(
            num_scalar_prefetch=1,
            grid=(steps,),
            in_specs=[pl.BlockSpec((some, pairs, aux_dev), block_map)]
            + [pl.BlockSpec((ndens, width), whole_map)] * n,
            out_specs=[pl.BlockSpec((some, pairs, half), block_map)] * 2,
        ),
        compiler_params=params,
        name="apply",
    )(where, three_index, *chunks)
    added = swap(theirs)

    out_table = ints(
        [(home_target - me) % n, home_rank, (mirror_target - me) % n, mirror_rank]
    )
    slots = jax.ShapeDtypeStruct((2 * cap, pairs, half), jnp.bfloat16)
    sends = pl.pallas_call(
        functools.partial(scatter_coulomb_kernel, n, blocks, shell, cap),
        out_shape=[slots] * n,
        grid_spec=pltpu.PrefetchScalarGridSpec(
            num_scalar_prefetch=1,
            grid=(blocks,),
            in_specs=[
                pl.BlockSpec((1, 1, pairs), block_map),
                pl.BlockSpec((1, pairs, half), block_map),
                pl.BlockSpec((1, pairs, half), block_map),
            ],
            out_specs=[any_spec] * n,
            scratch_shapes=[
                pltpu.VMEM((pairs, half), jnp.float32),
                pltpu.VMEM((blocks, pairs, half), jnp.bfloat16),
                pltpu.VMEM((blocks, pairs, half), jnp.bfloat16),
                pltpu.SemaphoreType.DMA((2, blocks)),
            ],
        ),
        compiler_params=params,
        name="scatter_coulomb",
    )(out_table, screen.astype(jnp.float32)[:, None, :], mine, added)
    received = [sends[0]] + [shift(sends[d], d) for d in range(1, n)]
    in_table = ints(
        [
            (me - home_source) % n,
            home_row_rank,
            (me - mirror_source) % n,
            cap + mirror_row_rank,
        ]
    )
    rows, cols = pl.pallas_call(
        functools.partial(gather_kernel, n, blocks, 2),
        out_shape=[jax.ShapeDtypeStruct((blocks, pairs, half), jnp.bfloat16)] * 2,
        grid_spec=pltpu.PrefetchScalarGridSpec(
            num_scalar_prefetch=1,
            grid=(),
            in_specs=[any_spec] * n,
            out_specs=[any_spec] * 2,
            scratch_shapes=[pltpu.SemaphoreType.DMA((2, blocks))],
        ),
        name="gather_coulomb",
    )(in_table, *received)
    return rows, cols


def solution(mesh):
    in_specs = (
        P(("mol", "pair"), None, "aux"),
        P(("mol", "pair"), None, None),
        P(("mol", "pair"), None),
        P(("mol", "pair"), None),
        P("mol"),
        P("mol"),
    )
    out_specs = (P(("mol", "pair"), None, "aux"), P(("mol", "pair"), None, "aux"))
    return jax.shard_map(local, mesh=mesh, in_specs=in_specs, out_specs=out_specs, check_vma=False)
```

```python
import functools
import math

import jax
import jax.numpy as jnp
from jax import lax
from jax.experimental import pallas as pl
from jax.experimental.pallas import tpu as pltpu
from jax.sharding import PartitionSpec as P

VMEM_BYTES = 48 * 1024 * 1024


def tables(slots, devices, blocks_dev, me):
    total = slots.shape[0]
    numbers = jnp.arange(total, dtype=jnp.int32)
    source = numbers // blocks_dev
    target = slots // blocks_dev
    joined = source * devices + target
    earlier = (joined[:, None] == joined[None, :]) & (numbers[None, :] < numbers[:, None])
    rank = jnp.sum(earlier.astype(jnp.int32), axis=1)
    own_target = lax.dynamic_slice_in_dim(target, me * blocks_dev, blocks_dev, 0)
    own_rank = lax.dynamic_slice_in_dim(rank, me * blocks_dev, blocks_dev, 0)
    rows = me * blocks_dev + jnp.arange(blocks_dev, dtype=jnp.int32)
    hot = slots[None, :] == rows[:, None]
    row_source = jnp.sum(jnp.where(hot, source[None, :], 0), axis=1)
    row_rank = jnp.sum(jnp.where(hot, rank[None, :], 0), axis=1)
    return own_target, own_rank, row_source, row_rank


def scatter_density_kernel(devices, blocks, table, density, *rest):
    sends, sems = rest[:devices], rest[devices]

    def copy(row, step):
        return pltpu.make_async_copy(
            density.at[row],
            sends[step].at[table[blocks + row]],
            sems.at[row],
        )

    for row in range(blocks):
        for step in range(devices):

            @pl.when(table[row] == step)
            def _():
                copy(row, step).start()

    for row in range(blocks):
        copy(row, 0).wait()


def gather_kernel(devices, blocks, groups, table, *rest):
    received, outs, sems = rest[:devices], rest[devices : devices + groups], rest[devices + groups]

    def copy(group, row, step):
        return pltpu.make_async_copy(
            received[step].at[table[(2 * group + 1) * blocks + row]],
            outs[group].at[row],
            sems.at[group, row],
        )

    for group in range(groups):
        for row in range(blocks):
            for step in range(devices):

                @pl.when(table[2 * group * blocks + row] == step)
                def _():
                    copy(group, row, step).start()

    for group in range(groups):
        for row in range(blocks):
            copy(group, row, 0).wait()


def fit_kernel(devices, some, steps, table, factor, own, other, integrals, *rest):
    own_part, sends, total = rest[0], rest[1:devices], rest[devices]
    step = pl.program_id(0)
    width = own_part.shape[1]

    @pl.when(step == 0)
    def _():
        total[...] = jnp.zeros_like(total)

    turned = []
    for b in range(some):
        both = jnp.concatenate([own[b], other[b]], axis=1)
        turned.append(both.T * factor[b])
    fitted = jnp.concatenate(turned, axis=1)
    flat = integrals.reshape(some * integrals.shape[1], integrals.shape[2])
    for chunk in range(devices):
        at = pl.ds(chunk * width, width)
        total[:, at] += jnp.dot(fitted, flat[:, at], preferred_element_type=jnp.float32)

    @pl.when(step == steps - 1)
    def _():
        for d in range(devices):
            chunk = lax.rem(table[0] + d, devices)
            value = total[:, pl.ds(pl.multiple_of(chunk * width, width), width)]
            if d == 0:
                own_part[...] = value
            else:
                sends[d - 1][...] = value.astype(jnp.bfloat16)


def apply_kernel(devices, some, table, integrals, *rest):
    chunks, own, other = rest[:devices], rest[devices], rest[devices + 1]
    width = chunks[0].shape[1]
    half = own.shape[2]
    flat = integrals.reshape(some * integrals.shape[1], integrals.shape[2])
    total = None
    for d in range(devices):
        chunk = lax.rem(table[0] + devices - d, devices)
        term = lax.dot_general(
            flat[:, pl.ds(pl.multiple_of(chunk * width, width), width)],
            chunks[d][...],
            (((1,), (1,)), ((), ())),
            preferred_element_type=jnp.float32,
        )
        total = term if total is None else total + term
    own[...] = total[:, :half].reshape(own.shape)
    other[...] = total[:, half:].reshape(other.shape).astype(other.dtype)


def scatter_coulomb_kernel(
    devices, blocks, some, shell, cap, table, screen, own, other, *rest
):
    sends = rest[:devices]
    turning, row_buf, col_buf, sems = rest[devices:]
    first = pl.program_id(0) * some
    pairs, half = own.shape[1], own.shape[2]

    def copy(group, b, step):
        buf = (row_buf, col_buf)[group]
        return pltpu.make_async_copy(
            buf.at[b],
            sends[step].at[group * cap + table[(2 * group + 1) * blocks + b]],
            sems.at[group, b],
        )

    for b in range(some):
        block = first + b
        keep = jnp.broadcast_to(screen[b], (half, pairs)).T
        value = (own[b] + other[b].astype(jnp.float32)) * keep
        turning[b] = value
        row_buf[block] = value.astype(jnp.bfloat16)
        for j in range(shell):
            col_buf[block, pl.ds(j * shell, shell), :] = turning[
                b, pl.ds(j, shell, stride=shell), :
            ].astype(jnp.bfloat16)
        for group in range(2):
            for step in range(devices):

                @pl.when(table[2 * group * blocks + block] == step)
                def _():
                    copy(group, block, step).start()

    @pl.when(first == blocks - some)
    def _():
        for group in range(2):
            for b in range(blocks):
                copy(group, b, 0).wait()


def local(three_index, density, screen, pair_shells, home_slot, mirror_slot):
    blocks, pairs, aux_dev = three_index.shape
    ndens = density.shape[2]
    shell = math.isqrt(pairs)
    n = lax.axis_size("pair")
    parts = lax.axis_size("aux")
    me = lax.axis_index("pair")
    core = lax.axis_index("aux")
    half = ndens // parts
    width = aux_dev // n
    cap = 2 + (blocks - 1) // n
    some = 2 if blocks % 2 == 0 else 1
    steps = blocks // some
    any_spec = pl.BlockSpec(memory_space=pl.ANY)
    params = pltpu.CompilerParams(vmem_limit_bytes=VMEM_BYTES)

    def shift(x, d):
        return lax.ppermute(x, "pair", [(s, (s + d) % n) for s in range(n)])

    def swap(x):
        return lax.ppermute(x, "aux", [(s, (s + 1) % parts) for s in range(parts)])

    home_target, home_rank, home_source, home_row_rank = tables(home_slot, n, blocks, me)
    mirror_target, mirror_rank, mirror_source, mirror_row_rank = tables(
        mirror_slot, n, blocks, me
    )
    ints = functools.partial(jnp.concatenate, axis=0)

    send_table = ints([(home_source - me) % n, home_row_rank, core[None].astype(jnp.int32)])
    slots = jax.ShapeDtypeStruct((cap, pairs, half), jnp.bfloat16)
    sends = pl.pallas_call(
        functools.partial(scatter_density_kernel, n, blocks),
        out_shape=[slots] * n,
        grid_spec=pltpu.PrefetchScalarGridSpec(
            num_scalar_prefetch=1,
            grid=(1,),
            in_specs=[
                pl.BlockSpec((blocks, pairs, half), lambda i, t: (0, 0, t[2 * blocks]))
            ],
            out_specs=[any_spec] * n,
            scratch_shapes=[pltpu.SemaphoreType.DMA((blocks,))],
        ),
        compiler_params=params,
        name="scatter_density",
    )(send_table, density)
    received = [sends[0]] + [shift(sends[d], d) for d in range(1, n)]
    pick_table = ints([(me - home_target) % n, home_rank])
    own = pl.pallas_call(
        functools.partial(gather_kernel, n, blocks, 1),
        out_shape=[jax.ShapeDtypeStruct((blocks, pairs, half), jnp.bfloat16)],
        grid_spec=pltpu.PrefetchScalarGridSpec(
            num_scalar_prefetch=1,
            grid=(1,),
            in_specs=[any_spec] * n,
            out_specs=[pl.BlockSpec((blocks, pairs, half), lambda i, t: (0, 0, 0))],
            scratch_shapes=[pltpu.SemaphoreType.DMA((1, blocks))],
        ),
        compiler_params=params,
        name="gather_density",
    )(pick_table, *received)[0]
    other = swap(own)

    weight = jnp.where(pair_shells[:, 0] != pair_shells[:, 1], 2.0, 1.0)
    factor = (screen.astype(jnp.float32) * weight[:, None]).astype(jnp.bfloat16)
    where = me[None].astype(jnp.int32)
    block_map = lambda i, t: (i, 0, 0)
    whole_map = lambda i, t: (0, 0)
    parts_fit = pl.pallas_call(
        functools.partial(fit_kernel, n, some, steps),
        out_shape=[jax.ShapeDtypeStruct((ndens, width), jnp.float32)]
        + [jax.ShapeDtypeStruct((ndens, width), jnp.bfloat16)] * (n - 1),
        grid_spec=pltpu.PrefetchScalarGridSpec(
            num_scalar_prefetch=1,
            grid=(steps,),
            in_specs=[
                pl.BlockSpec((some, 1, pairs), block_map),
                pl.BlockSpec((some, pairs, half), block_map),
                pl.BlockSpec((some, pairs, half), block_map),
                pl.BlockSpec((some, pairs, aux_dev), block_map),
            ],
            out_specs=[pl.BlockSpec((ndens, width), whole_map)] * n,
            scratch_shapes=[pltpu.VMEM((ndens, aux_dev), jnp.float32)],
        ),
        compiler_params=params,
        name="fit",
    )(where, factor[:, None, :], own, other, three_index)
    summed = parts_fit[0]
    for d in range(1, n):
        summed = summed + shift(parts_fit[d], d).astype(jnp.float32)
    coef = summed.astype(jnp.bfloat16)
    chunks = [coef] + [shift(coef, d) for d in range(1, n)]

    mine, theirs = pl.pallas_call(
        functools.partial(apply_kernel, n, some),
        out_shape=[
            jax.ShapeDtypeStruct((blocks, pairs, half), jnp.float32),
            jax.ShapeDtypeStruct((blocks, pairs, half), jnp.bfloat16),
        ],
        grid_spec=pltpu.PrefetchScalarGridSpec(
            num_scalar_prefetch=1,
            grid=(steps,),
            in_specs=[pl.BlockSpec((some, pairs, aux_dev), block_map)]
            + [pl.BlockSpec((ndens, width), whole_map)] * n,
            out_specs=[pl.BlockSpec((some, pairs, half), block_map)] * 2,
        ),
        compiler_params=params,
        name="apply",
    )(where, three_index, *chunks)
    added = swap(theirs)

    out_table = ints(
        [(home_target - me) % n, home_rank, (mirror_target - me) % n, mirror_rank]
    )
    slots = jax.ShapeDtypeStruct((2 * cap, pairs, half), jnp.bfloat16)
    sends = pl.pallas_call(
        functools.partial(scatter_coulomb_kernel, n, blocks, some, shell, cap),
        out_shape=[slots] * n,
        grid_spec=pltpu.PrefetchScalarGridSpec(
            num_scalar_prefetch=1,
            grid=(steps,),
            in_specs=[
                pl.BlockSpec((some, 1, pairs), block_map),
                pl.BlockSpec((some, pairs, half), block_map),
                pl.BlockSpec((some, pairs, half), block_map),
            ],
            out_specs=[any_spec] * n,
            scratch_shapes=[
                pltpu.VMEM((some, pairs, half), jnp.float32),
                pltpu.VMEM((blocks, pairs, half), jnp.bfloat16),
                pltpu.VMEM((blocks, pairs, half), jnp.bfloat16),
                pltpu.SemaphoreType.DMA((2, blocks)),
            ],
        ),
        compiler_params=params,
        name="scatter_coulomb",
    )(out_table, screen.astype(jnp.float32)[:, None, :], mine, added)
    received = [sends[0]] + [shift(sends[d], d) for d in range(1, n)]
    in_table = ints(
        [
            (me - home_source) % n,
            home_row_rank,
            (me - mirror_source) % n,
            cap + mirror_row_rank,
        ]
    )
    rows, cols = pl.pallas_call(
        functools.partial(gather_kernel, n, blocks, 2),
        out_shape=[jax.ShapeDtypeStruct((blocks, pairs, half), jnp.bfloat16)] * 2,
        grid_spec=pltpu.PrefetchScalarGridSpec(
            num_scalar_prefetch=1,
            grid=(1,),
            in_specs=[any_spec] * n,
            out_specs=[pl.BlockSpec((blocks, pairs, half), lambda i, t: (0, 0, 0))] * 2,
            scratch_shapes=[pltpu.SemaphoreType.DMA((2, blocks))],
        ),
        compiler_params=params,
        name="gather_coulomb",
    )(in_table, *received)
    return rows, cols


def solution(mesh):
    in_specs = (
        P(("mol", "pair"), None, "aux"),
        P(("mol", "pair"), None, None),
        P(("mol", "pair"), None),
        P(("mol", "pair"), None),
        P("mol"),
        P("mol"),
    )
    out_specs = (P(("mol", "pair"), None, "aux"), P(("mol", "pair"), None, "aux"))
    return jax.shard_map(local, mesh=mesh, in_specs=in_specs, out_specs=out_specs, check_vma=False)
```

```python
import functools
import math

import jax
import jax.numpy as jnp
from jax import lax
from jax.experimental import pallas as pl
from jax.experimental.pallas import tpu as pltpu
from jax.sharding import PartitionSpec as P

VMEM_BYTES = 48 * 1024 * 1024
CHAINS = 2


def tables(slots, devices, blocks_dev, me):
    total = slots.shape[0]
    numbers = jnp.arange(total, dtype=jnp.int32)
    source = numbers // blocks_dev
    target = slots // blocks_dev
    joined = source * devices + target
    earlier = (joined[:, None] == joined[None, :]) & (numbers[None, :] < numbers[:, None])
    rank = jnp.sum(earlier.astype(jnp.int32), axis=1)
    own_target = lax.dynamic_slice_in_dim(target, me * blocks_dev, blocks_dev, 0)
    own_rank = lax.dynamic_slice_in_dim(rank, me * blocks_dev, blocks_dev, 0)
    rows = me * blocks_dev + jnp.arange(blocks_dev, dtype=jnp.int32)
    hot = slots[None, :] == rows[:, None]
    row_source = jnp.sum(jnp.where(hot, source[None, :], 0), axis=1)
    row_rank = jnp.sum(jnp.where(hot, rank[None, :], 0), axis=1)
    return own_target, own_rank, row_source, row_rank


def scatter_density_kernel(devices, blocks, table, density, *rest):
    sends, turned, sems = rest[: CHAINS * devices], rest[-2], rest[-1]
    part = turned.shape[2]

    def copy(chain, row, step):
        return pltpu.make_async_copy(
            turned.at[chain, row],
            sends[chain * devices + step].at[table[blocks + row]],
            sems.at[chain, row],
        )

    for row in range(blocks):
        value = density[row].T
        for chain in range(CHAINS):
            turned[chain, row] = value[chain * part : (chain + 1) * part]
        for chain in range(CHAINS):
            for step in range(devices):

                @pl.when(table[row] == step)
                def _():
                    copy(chain, row, step).start()

    for chain in range(CHAINS):
        for row in range(blocks):
            copy(chain, row, 0).wait()


def gather_density_kernel(devices, blocks, table, *rest):
    received, out, sems = rest[:devices], rest[devices], rest[devices + 1]

    def copy(row, step):
        return pltpu.make_async_copy(
            received[step].at[table[blocks + row]], out.at[row], sems.at[row]
        )

    for row in range(blocks):
        for step in range(devices):

            @pl.when(table[row] == step)
            def _():
                copy(row, step).start()

    for row in range(blocks):
        copy(row, 0).wait()


def fit_kernel(devices, some, steps, table, factor, own, other, integrals, keep, send, total):
    step = pl.program_id(0)
    width = keep.shape[2]

    @pl.when(step == 0)
    def _():
        total[...] = jnp.zeros_like(total)

    fitted = jnp.concatenate(
        [jnp.concatenate([own[b], other[b]], axis=0) * factor[b] for b in range(some)], axis=1
    )
    flat = integrals.reshape(some * integrals.shape[1], integrals.shape[2])
    for chunk in range(devices):
        at = pl.ds(chunk * width, width)
        total[:, at] += jnp.dot(fitted, flat[:, at], preferred_element_type=jnp.float32)

    @pl.when(step == steps - 1)
    def _():
        for e in range(devices):
            value = total[:, pl.ds(pl.multiple_of(table[e] * width, width), width)]
            if e % 2:
                send[e // 2] = value.astype(send.dtype)
            else:
                keep[e // 2] = value


def apply_kernel(devices, some, order, table, integrals, near, far, own, other):
    width = near.shape[2]
    part = own.shape[1]
    pairs = integrals.shape[1]
    flat = integrals.reshape(some * pairs, integrals.shape[2])
    total = None
    for i, e in enumerate(order):
        chunk = near[i] if i < devices // 2 else far[i - devices // 2]
        term = lax.dot_general(
            flat[:, pl.ds(pl.multiple_of(table[e] * width, width), width)],
            chunk,
            (((1,), (1,)), ((), ())),
            preferred_element_type=jnp.float32,
        )
        total = term if total is None else total + term
    for b in range(some):
        value = total[b * pairs : (b + 1) * pairs].T
        own[b] = value[:part]
        other[b] = value[part:].astype(other.dtype)


def scatter_coulomb_kernel(devices, blocks, some, cap, table, screen, own, other, *rest):
    sends, ready, sems = rest[:devices], rest[devices], rest[devices + 1]
    first = pl.program_id(0) * some

    def copy(group, b, step):
        return pltpu.make_async_copy(
            ready.at[b],
            sends[step].at[group * cap + table[(2 * group + 1) * blocks + b]],
            sems.at[group, b],
        )

    for b in range(some):
        block = first + b
        value = (own[b] + other[b].astype(jnp.float32)) * screen[b]
        ready[block] = value.astype(jnp.bfloat16)
        for group in range(2):
            for step in range(devices):

                @pl.when(table[2 * group * blocks + block] == step)
                def _():
                    copy(group, block, step).start()

    @pl.when(first == blocks - some)
    def _():
        for group in range(2):
            for b in range(blocks):
                copy(group, b, 0).wait()


def gather_coulomb_kernel(devices, blocks, shell, table, *rest):
    received = rest[: CHAINS * devices]
    rows, cols, landed, turning, sems = rest[CHAINS * devices :]
    block = pl.program_id(0)
    part = landed.shape[2] // CHAINS

    def copy(chain, group, row, step):
        return pltpu.make_async_copy(
            received[chain * devices + step].at[table[(2 * group + 1) * blocks + row]],
            landed.at[group, row, pl.ds(chain * part, part)],
            sems.at[chain, group, row],
        )

    @pl.when(block == 0)
    def _():
        for row in range(blocks):
            for group in range(2):
                for chain in range(CHAINS):
                    for step in range(devices):

                        @pl.when(table[2 * group * blocks + row] == step)
                        def _():
                            copy(chain, group, row, step).start()

    for group in range(2):
        for chain in range(CHAINS):
            copy(chain, group, block, 0).wait()
    rows[0] = landed[0, block].T
    turning[...] = landed[1, block].astype(jnp.float32).T
    for j in range(shell):
        cols[0, pl.ds(j * shell, shell), :] = turning[
            pl.ds(j, shell, stride=shell), :
        ].astype(jnp.bfloat16)


def local(three_index, density, screen, pair_shells, home_slot, mirror_slot):
    blocks, pairs, aux_dev = three_index.shape
    ndens = density.shape[2]
    shell = math.isqrt(pairs)
    n = lax.axis_size("pair")
    cores = lax.axis_size("aux")
    me = lax.axis_index("pair")
    core = lax.axis_index("aux")
    half = ndens // cores
    part = half // CHAINS
    both = cores * part
    width = aux_dev // n
    cap = 2 + (blocks - 1) // n
    some = 2 if blocks % 2 == 0 else 1
    steps = blocks // some
    any_spec = pl.BlockSpec(memory_space=pl.ANY)
    params = pltpu.CompilerParams(vmem_limit_bytes=VMEM_BYTES)
    bf16, f32 = jnp.bfloat16, jnp.float32
    block_map = lambda i, t: (i, 0, 0)
    whole_map = lambda i, t: (0, 0, 0)
    ints = functools.partial(jnp.concatenate, axis=0)

    def shift(x, d):
        return lax.ppermute(x, "pair", [(s, (s + d) % n) for s in range(n)])

    def flip(x, bit):
        return lax.ppermute(x, "pair", [(s, s ^ bit) for s in range(n)])

    def swap(x):
        return lax.ppermute(x, "aux", [(s, (s + 1) % cores) for s in range(cores)])

    home_target, home_rank, home_source, home_row_rank = tables(home_slot, n, blocks, me)
    mirror_target, mirror_rank, mirror_source, mirror_row_rank = tables(
        mirror_slot, n, blocks, me
    )
    send_table = ints([(home_source - me) % n, home_row_rank, core[None].astype(jnp.int32)])
    pick_table = ints([(me - home_target) % n, home_rank])
    chunk_table = me ^ jnp.arange(n, dtype=jnp.int32)
    out_table = ints([(home_target - me) % n, home_rank, (mirror_target - me) % n, mirror_rank])
    in_table = ints(
        [(me - home_source) % n, home_row_rank, (me - mirror_source) % n, cap + mirror_row_rank]
    )
    weight = jnp.where(pair_shells[:, 0] != pair_shells[:, 1], 2.0, 1.0)
    factor = (screen.astype(f32) * weight[:, None]).astype(bf16)[:, None, :]
    keeping = screen.astype(f32)[:, None, :]

    sends = pl.pallas_call(
        functools.partial(scatter_density_kernel, n, blocks),
        out_shape=[jax.ShapeDtypeStruct((cap, part, pairs), bf16)] * (CHAINS * n),
        grid_spec=pltpu.PrefetchScalarGridSpec(
            num_scalar_prefetch=1,
            grid=(1,),
            in_specs=[pl.BlockSpec((blocks, pairs, half), lambda i, t: (0, 0, t[2 * blocks]))],
            out_specs=[any_spec] * (CHAINS * n),
            scratch_shapes=[
                pltpu.VMEM((CHAINS, blocks, part, pairs), bf16),
                pltpu.SemaphoreType.DMA((CHAINS, blocks)),
            ],
        ),
        compiler_params=params,
        name="scatter_density",
    )(send_table, density)

    def fetch(chain):
        mine = sends[chain * n : (chain + 1) * n]
        received = [mine[0]] + [shift(mine[d], d) for d in range(1, n)]
        own = pl.pallas_call(
            functools.partial(gather_density_kernel, n, blocks),
            out_shape=jax.ShapeDtypeStruct((blocks, part, pairs), bf16),
            grid_spec=pltpu.PrefetchScalarGridSpec(
                num_scalar_prefetch=1,
                grid=(1,),
                in_specs=[any_spec] * n,
                out_specs=pl.BlockSpec((blocks, part, pairs), whole_map),
                scratch_shapes=[pltpu.SemaphoreType.DMA((blocks,))],
            ),
            compiler_params=params,
            name="gather_density",
        )(pick_table, *received)
        return own, swap(own)

    def fit(own, other):
        keep, send = pl.pallas_call(
            functools.partial(fit_kernel, n, some, steps),
            out_shape=[
                jax.ShapeDtypeStruct((n // 2, both, width), f32),
                jax.ShapeDtypeStruct((n // 2, both, width), bf16),
            ],
            grid_spec=pltpu.PrefetchScalarGridSpec(
                num_scalar_prefetch=1,
                grid=(steps,),
                in_specs=[
                    pl.BlockSpec((some, 1, pairs), block_map),
                    pl.BlockSpec((some, part, pairs), block_map),
                    pl.BlockSpec((some, part, pairs), block_map),
                    pl.BlockSpec((some, pairs, aux_dev), block_map),
                ],
                out_specs=[pl.BlockSpec((n // 2, both, width), whole_map)] * 2,
                scratch_shapes=[pltpu.VMEM((both, aux_dev), f32)],
            ),
            compiler_params=params,
            cost_estimate=pl.CostEstimate(
                flops=2 * blocks * pairs * aux_dev * both,
                bytes_accessed=2 * blocks * pairs * aux_dev,
                transcendentals=0,
            ),
            name="fit",
        )(chunk_table, factor, own, other, three_index)
        bit = 1
        while True:
            value = keep + flip(send, bit).astype(f32)
            bit *= 2
            if bit == n:
                break
            keep, send = value[0::2], value[1::2].astype(bf16)
        near, order = value.astype(bf16), [0]
        while True:
            bit //= 2
            far = flip(near, bit)
            order = order + [e ^ bit for e in order]
            if bit == 1:
                return near, far, order
            near = jnp.concatenate([near, far], axis=0)

    def apply(near, far, order):
        mine, theirs = pl.pallas_call(
            functools.partial(apply_kernel, n, some, order),
            out_shape=[
                jax.ShapeDtypeStruct((blocks, part, pairs), f32),
                jax.ShapeDtypeStruct((blocks, part, pairs), bf16),
            ],
            grid_spec=pltpu.PrefetchScalarGridSpec(
                num_scalar_prefetch=1,
                grid=(steps,),
                in_specs=[
                    pl.BlockSpec((some, pairs, aux_dev), block_map),
                    pl.BlockSpec((n // 2, both, width), whole_map),
                    pl.BlockSpec((n // 2, both, width), whole_map),
                ],
                out_specs=[pl.BlockSpec((some, part, pairs), block_map)] * 2,
            ),
            compiler_params=params,
            cost_estimate=pl.CostEstimate(
                flops=2 * blocks * pairs * aux_dev * both,
                bytes_accessed=2 * blocks * pairs * aux_dev,
                transcendentals=0,
            ),
            name="apply",
        )(chunk_table, three_index, near, far)
        return mine, swap(theirs)

    def deliver(mine, added):
        out = pl.pallas_call(
            functools.partial(scatter_coulomb_kernel, n, blocks, some, cap),
            out_shape=[jax.ShapeDtypeStruct((2 * cap, part, pairs), bf16)] * n,
            grid_spec=pltpu.PrefetchScalarGridSpec(
                num_scalar_prefetch=1,
                grid=(steps,),
                in_specs=[
                    pl.BlockSpec((some, 1, pairs), block_map),
                    pl.BlockSpec((some, part, pairs), block_map),
                    pl.BlockSpec((some, part, pairs), block_map),
                ],
                out_specs=[any_spec] * n,
                scratch_shapes=[
                    pltpu.VMEM((blocks, part, pairs), bf16),
                    pltpu.SemaphoreType.DMA((2, blocks)),
                ],
            ),
            compiler_params=params,
            name="scatter_coulomb",
        )(out_table, keeping, mine, added)
        return [out[0]] + [shift(out[d], d) for d in range(1, n)]

    fetched = [fetch(chain) for chain in range(CHAINS)]
    fits = [fit(*pair) for pair in fetched]
    sums = [apply(*found) for found in fits]
    received = [piece for pair in sums for piece in deliver(*pair)]
    rows, cols = pl.pallas_call(
        functools.partial(gather_coulomb_kernel, n, blocks, shell),
        out_shape=[jax.ShapeDtypeStruct((blocks, pairs, half), bf16)] * 2,
        grid_spec=pltpu.PrefetchScalarGridSpec(
            num_scalar_prefetch=1,
            grid=(blocks,),
            in_specs=[any_spec] * (CHAINS * n),
            out_specs=[pl.BlockSpec((1, pairs, half), block_map)] * 2,
            scratch_shapes=[
                pltpu.VMEM((2, blocks, half, pairs), bf16),
                pltpu.VMEM((pairs, half), f32),
                pltpu.SemaphoreType.DMA((CHAINS, 2, blocks)),
            ],
        ),
        compiler_params=params,
        name="gather_coulomb",
    )(in_table, *received)
    return rows, cols


def solution(mesh):
    in_specs = (
        P(("mol", "pair"), None, "aux"),
        P(("mol", "pair"), None, None),
        P(("mol", "pair"), None),
        P(("mol", "pair"), None),
        P("mol"),
        P("mol"),
    )
    out_specs = (P(("mol", "pair"), None, "aux"), P(("mol", "pair"), None, "aux"))
    return jax.shard_map(local, mesh=mesh, in_specs=in_specs, out_specs=out_specs, check_vma=False)
```

```python
import functools
import math

import jax
import jax.numpy as jnp
from jax import lax
from jax.experimental import pallas as pl
from jax.experimental.pallas import tpu as pltpu
from jax.sharding import PartitionSpec as P

VMEM_BYTES = 24 * 1024 * 1024
CHAINS = 2


def tables(slots, devices, blocks_dev, me):
    total = slots.shape[0]
    numbers = jnp.arange(total, dtype=jnp.int32)
    source = numbers // blocks_dev
    target = slots // blocks_dev
    joined = source * devices + target
    earlier = (joined[:, None] == joined[None, :]) & (numbers[None, :] < numbers[:, None])
    rank = jnp.sum(earlier.astype(jnp.int32), axis=1)
    own_target = lax.dynamic_slice_in_dim(target, me * blocks_dev, blocks_dev, 0)
    own_rank = lax.dynamic_slice_in_dim(rank, me * blocks_dev, blocks_dev, 0)
    rows = me * blocks_dev + jnp.arange(blocks_dev, dtype=jnp.int32)
    hot = slots[None, :] == rows[:, None]
    row_source = jnp.sum(jnp.where(hot, source[None, :], 0), axis=1)
    row_rank = jnp.sum(jnp.where(hot, rank[None, :], 0), axis=1)
    return own_target, own_rank, row_source, row_rank


def slots_of(steps, ranks, devices, cap):
    held = (steps * cap + ranks)[None, :] == jnp.arange(devices * cap, dtype=jnp.int32)[:, None]
    numbers = jnp.arange(steps.shape[0], dtype=jnp.int32)
    return jnp.max(jnp.where(held, numbers[None, :], -1), axis=1)


def load_kernel(source, target, sem):
    copy = pltpu.make_async_copy(source, target, sem)
    copy.start()
    copy.wait()


def scatter_density_kernel(devices, blocks, cap, table, density, *rest):
    sends, turned = rest[: CHAINS * devices], rest[-1]
    part = sends[0].shape[1]
    for row in range(blocks):
        turned[row] = density[row].T
    for step in range(devices):
        for rank in range(cap):
            row = jnp.maximum(table[step * cap + rank], 0)
            for chain in range(CHAINS):
                sends[chain * devices + step][rank] = turned[row, pl.ds(chain * part, part)]


def gather_density_kernel(devices, cap, table, *rest):
    received, out = rest[:devices], rest[-1]
    for step in range(devices):
        for rank in range(cap):
            row = table[step * cap + rank]

            @pl.when(row >= 0)
            def _():
                out[row] = received[step][rank]


def fit_kernel(devices, blocks, table, factor, own, other, integrals, keep, send):
    width = keep.shape[2]
    pairs = integrals.shape[1]
    fitted = jnp.concatenate(
        [jnp.concatenate([own[b], other[b]], axis=0) * factor[b] for b in range(blocks)], axis=1
    )
    for e in range(devices):
        at = pl.ds(pl.multiple_of(table[e] * width, width), width)
        value = jnp.dot(
            fitted,
            integrals[:, :, at].reshape(blocks * pairs, width),
            preferred_element_type=jnp.float32,
        )
        if e % 2:
            send[e // 2] = value.astype(send.dtype)
        else:
            keep[e // 2] = value


def apply_kernel(devices, blocks, order, table, integrals, near, far, *rest):
    own, other = rest[-2:]
    width = near.shape[2]
    part = own.shape[1]
    pairs = integrals.shape[1]
    total = None
    for i, e in enumerate(order):
        chunk = near[i] if i < devices // 2 else far[i - devices // 2]
        at = pl.ds(pl.multiple_of(table[e] * width, width), width)
        term = lax.dot_general(
            integrals[:, :, at].reshape(blocks * pairs, width),
            chunk,
            (((1,), (1,)), ((), ())),
            preferred_element_type=jnp.float32,
        )
        total = term if total is None else total + term
    for b in range(blocks):
        value = total[b * pairs : (b + 1) * pairs].T
        own[b] = value[:part]
        other[b] = value[part:].astype(other.dtype)


def scatter_coulomb_kernel(devices, blocks, cap, table, screen, own, other, *rest):
    sends, ready = rest[:devices], rest[devices]
    for b in range(blocks):
        value = (own[b] + other[b].astype(jnp.float32)) * screen[b]
        ready[b] = value.astype(jnp.bfloat16)
    for group in range(2):
        for step in range(devices):
            for rank in range(cap):
                b = jnp.maximum(table[(group * devices + step) * cap + rank], 0)
                sends[step][group * cap + rank] = ready[b]


def gather_coulomb_kernel(devices, blocks, shell, cap, table, *rest):
    received = rest[: CHAINS * devices]
    rows, cols, landed, done, sems = rest[CHAINS * devices :]
    part = received[0].shape[1]
    pairs = landed.shape[3]
    for group in range(2):
        for step in range(devices):
            for rank in range(cap):
                row = table[(group * devices + step) * cap + rank]

                @pl.when(row >= 0)
                def _():
                    for chain in range(CHAINS):
                        landed[group, row, pl.ds(chain * part, part)] = received[
                            chain * devices + step
                        ][group * cap + rank]

    to = lax.broadcasted_iota(jnp.int32, (pairs, pairs), 0)
    source = lax.broadcasted_iota(jnp.int32, (pairs, pairs), 1)
    turns = (to, (to % shell) * shell + to // shell)
    copies = []
    for group in range(2):
        turn = (source == turns[group]).astype(jnp.bfloat16)
        for row in range(blocks):
            done[group, row] = lax.dot_general(
                turn,
                landed[group, row],
                (((1,), (1,)), ((), ())),
                preferred_element_type=jnp.float32,
            ).astype(jnp.bfloat16)
            copy = pltpu.make_async_copy(
                done.at[group, row], (rows, cols)[group].at[row], sems.at[group, row]
            )
            copy.start()
            copies.append(copy)
    for copy in copies:
        copy.wait()


def local(three_index, density, screen, pair_shells, home_slot, mirror_slot):
    blocks, pairs, aux_dev = three_index.shape
    ndens = density.shape[2]
    shell = math.isqrt(pairs)
    n = lax.axis_size("pair")
    cores = lax.axis_size("aux")
    me = lax.axis_index("pair")
    core = lax.axis_index("aux")
    half = ndens // cores
    part = half // CHAINS
    both = cores * part
    width = aux_dev // n
    cap = 2 + (blocks - 1) // n
    bf16, f32 = jnp.bfloat16, jnp.float32
    in_vmem = pl.BlockSpec(memory_space=pltpu.VMEM)
    anywhere = pl.BlockSpec(memory_space=pl.ANY)
    ints = functools.partial(jnp.concatenate, axis=0)

    def call(kernel, name, table, args, out_shape, out_specs, after=(), scratch=(), flops=0):
        return pl.pallas_call(
            kernel,
            out_shape=out_shape,
            grid_spec=pltpu.PrefetchScalarGridSpec(
                num_scalar_prefetch=1,
                grid=(),
                in_specs=[in_vmem] * len(args) + [anywhere] * len(after),
                out_specs=out_specs,
                scratch_shapes=list(scratch),
            ),
            compiler_params=pltpu.CompilerParams(vmem_limit_bytes=VMEM_BYTES),
            cost_estimate=pl.CostEstimate(flops=flops, bytes_accessed=0, transcendentals=0),
            name=name,
        )(table, *args, *after)

    def shift(x, d):
        return lax.ppermute(x, "pair", [(s, (s + d) % n) for s in range(n)])

    def flip(x, bit):
        return lax.ppermute(x, "pair", [(s, s ^ bit) for s in range(n)])

    def swap(x):
        return lax.ppermute(x, "aux", [(s, (s + 1) % cores) for s in range(cores)])

    home_target, home_rank, home_source, home_row_rank = tables(home_slot, n, blocks, me)
    mirror_target, mirror_rank, mirror_source, mirror_row_rank = tables(
        mirror_slot, n, blocks, me
    )
    send_table = ints(
        [slots_of((home_source - me) % n, home_row_rank, n, cap), core[None].astype(jnp.int32)]
    )
    pick_table = slots_of((me - home_target) % n, home_rank, n, cap)
    chunk_table = me ^ jnp.arange(n, dtype=jnp.int32)
    out_table = ints(
        [
            slots_of((home_target - me) % n, home_rank, n, cap),
            slots_of((mirror_target - me) % n, mirror_rank, n, cap),
        ]
    )
    in_table = ints(
        [
            slots_of((me - home_source) % n, home_row_rank, n, cap),
            slots_of((me - mirror_source) % n, mirror_row_rank, n, cap),
        ]
    )
    weight = jnp.where(pair_shells[:, 0] != pair_shells[:, 1], 2.0, 1.0)
    factor = (screen.astype(f32) * weight[:, None]).astype(bf16)[:, None, :]
    keeping = screen.astype(f32)[:, None, :]

    integrals = pl.pallas_call(
        load_kernel,
        out_shape=pltpu.VMEM((blocks, pairs, aux_dev), bf16),
        in_specs=[anywhere],
        out_specs=in_vmem,
        scratch_shapes=[pltpu.SemaphoreType.DMA],
        compiler_params=pltpu.CompilerParams(vmem_limit_bytes=2 * 1024 * 1024),
        name="load_integrals",
    )(three_index)

    sends = pl.pallas_call(
        functools.partial(scatter_density_kernel, n, blocks, cap),
        out_shape=[jax.ShapeDtypeStruct((cap, part, pairs), bf16)] * (CHAINS * n),
        grid_spec=pltpu.PrefetchScalarGridSpec(
            num_scalar_prefetch=1,
            grid=(1,),
            in_specs=[pl.BlockSpec((blocks, pairs, half), lambda i, t: (0, 0, t[n * cap]))],
            out_specs=[pl.BlockSpec((cap, part, pairs), lambda i, t: (0, 0, 0))] * (CHAINS * n),
            scratch_shapes=[pltpu.VMEM((blocks, half, pairs), bf16)],
        ),
        compiler_params=pltpu.CompilerParams(vmem_limit_bytes=VMEM_BYTES),
        name="scatter_density",
    )(send_table, density)

    def fetch(chain, after):
        mine = sends[chain * n : (chain + 1) * n]
        received = [mine[0]] + [shift(mine[d], d) for d in range(1, n)]
        own = call(
            functools.partial(gather_density_kernel, n, cap),
            "gather_density",
            pick_table,
            received,
            jax.ShapeDtypeStruct((blocks, part, pairs), bf16),
            in_vmem,
            after,
        )
        return own, swap(own)

    def fit(own, other):
        return call(
            functools.partial(fit_kernel, n, blocks),
            "fit",
            chunk_table,
            [factor, own, other, integrals],
            [
                jax.ShapeDtypeStruct((n // 2, both, width), f32),
                jax.ShapeDtypeStruct((n // 2, both, width), bf16),
            ],
            [in_vmem] * 2,
            flops=2 * blocks * pairs * aux_dev * both,
        )

    def total(keep, send):
        bit = 1
        while True:
            value = keep + flip(send, bit).astype(f32)
            bit *= 2
            if bit == n:
                break
            keep, send = value[0::2], value[1::2].astype(bf16)
        near, order = value.astype(bf16), [0]
        while True:
            bit //= 2
            far = flip(near, bit)
            order = order + [e ^ bit for e in order]
            if bit == 1:
                return near, far, order
            near = jnp.concatenate([near, far], axis=0)

    def apply(near, far, order, after):
        mine, theirs = call(
            functools.partial(apply_kernel, n, blocks, order),
            "apply",
            chunk_table,
            [integrals, near, far],
            [
                jax.ShapeDtypeStruct((blocks, part, pairs), f32),
                jax.ShapeDtypeStruct((blocks, part, pairs), bf16),
            ],
            [in_vmem] * 2,
            after,
            flops=2 * blocks * pairs * aux_dev * both,
        )
        return mine, swap(theirs)

    def pack(mine, added):
        return call(
            functools.partial(scatter_coulomb_kernel, n, blocks, cap),
            "scatter_coulomb",
            out_table,
            [keeping, mine, added],
            [jax.ShapeDtypeStruct((2 * cap, part, pairs), bf16)] * n,
            [in_vmem] * n,
            scratch=[pltpu.VMEM((blocks, part, pairs), bf16)],
        )

    fits = []
    for chain in range(CHAINS):
        fits.append(fit(*fetch(chain, fits[-1][:1] if fits else ())))
    packed = []
    for pieces in fits:
        packed.append(pack(*apply(*total(*pieces), packed[-1][:1] if packed else ())))
    received = [
        out[d] if d == 0 else shift(out[d], d) for out in packed for d in range(n)
    ]
    return call(
        functools.partial(gather_coulomb_kernel, n, blocks, shell, cap),
        "gather_coulomb",
        in_table,
        received,
        [jax.ShapeDtypeStruct((blocks, pairs, half), bf16)] * 2,
        [anywhere] * 2,
        scratch=[
            pltpu.VMEM((2, blocks, half, pairs), bf16),
            pltpu.VMEM((2, blocks, pairs, half), bf16),
            pltpu.SemaphoreType.DMA((2, blocks)),
        ],
    )


def solution(mesh):
    in_specs = (
        P(("mol", "pair"), None, "aux"),
        P(("mol", "pair"), None, None),
        P(("mol", "pair"), None),
        P(("mol", "pair"), None),
        P("mol"),
        P("mol"),
    )
    out_specs = (P(("mol", "pair"), None, "aux"), P(("mol", "pair"), None, "aux"))
    return jax.shard_map(local, mesh=mesh, in_specs=in_specs, out_specs=out_specs, check_vma=False)
```

```python
import functools
import math

import jax
import jax.numpy as jnp
from jax import lax
from jax.experimental import pallas as pl
from jax.experimental.pallas import tpu as pltpu
from jax.sharding import PartitionSpec as P

VMEM_BYTES = 24 * 1024 * 1024
CHAINS = 2


def tables(slots, devices, blocks_dev, me):
    total = slots.shape[0]
    numbers = jnp.arange(total, dtype=jnp.int32)
    source = numbers // blocks_dev
    target = slots // blocks_dev
    joined = source * devices + target
    earlier = (joined[:, None] == joined[None, :]) & (numbers[None, :] < numbers[:, None])
    rank = jnp.sum(earlier.astype(jnp.int32), axis=1)
    own_target = lax.dynamic_slice_in_dim(target, me * blocks_dev, blocks_dev, 0)
    own_rank = lax.dynamic_slice_in_dim(rank, me * blocks_dev, blocks_dev, 0)
    rows = me * blocks_dev + jnp.arange(blocks_dev, dtype=jnp.int32)
    hot = slots[None, :] == rows[:, None]
    row_source = jnp.sum(jnp.where(hot, source[None, :], 0), axis=1)
    row_rank = jnp.sum(jnp.where(hot, rank[None, :], 0), axis=1)
    return own_target, own_rank, row_source, row_rank


def slots_of(steps, ranks, devices, cap):
    held = (steps * cap + ranks)[None, :] == jnp.arange(devices * cap, dtype=jnp.int32)[:, None]
    numbers = jnp.arange(steps.shape[0], dtype=jnp.int32)
    return jnp.max(jnp.where(held, numbers[None, :], -1), axis=1)


def load_kernel(source, target, sem):
    copy = pltpu.make_async_copy(source, target, sem)
    copy.start()
    copy.wait()


def scatter_density_kernel(devices, blocks, cap, table, density, *rest):
    sends, whole, turned = rest[:devices], rest[devices], rest[-1]
    part = whole.shape[2]
    for row in range(blocks):
        turned[row] = density[row].T
    for step in range(devices):
        for rank in range(cap):
            row = jnp.maximum(table[step * cap + rank], 0)
            sends[step][rank] = turned[row, pl.ds(0, part)]
            row = jnp.maximum(table[(devices + step) * cap + rank], 0)
            whole[step, rank] = turned[row, pl.ds(part, part)]


def slot(received, devices, step, rank):
    return received[0][step, rank] if len(received) == 1 else received[step][rank]


def gather_density_kernel(devices, cap, count, table, *rest):
    received, out = rest[:count], rest[-1]
    for step in range(devices):
        for rank in range(cap):
            row = table[step * cap + rank]

            @pl.when(row >= 0)
            def _():
                out[row] = slot(received, devices, step, rank)


def fit_kernel(devices, blocks, table, factor, own, other, integrals, keep, send):
    width = keep.shape[2]
    pairs = integrals.shape[1]
    fitted = jnp.concatenate(
        [jnp.concatenate([own[b], other[b]], axis=0) * factor[b] for b in range(blocks)], axis=1
    )
    for e in range(devices):
        at = pl.ds(pl.multiple_of(table[e] * width, width), width)
        value = jnp.dot(
            fitted,
            integrals[:, :, at].reshape(blocks * pairs, width),
            preferred_element_type=jnp.float32,
        )
        if e % 2:
            send[e // 2] = value.astype(send.dtype)
        else:
            keep[e // 2] = value


def apply_kernel(devices, blocks, order, table, integrals, near, far, *rest):
    own, other = rest[-2:]
    width = near.shape[2]
    part = own.shape[1]
    pairs = integrals.shape[1]
    total = None
    for i, e in enumerate(order):
        chunk = near[i] if i < devices // 2 else far[i - devices // 2]
        at = pl.ds(pl.multiple_of(table[e] * width, width), width)
        term = lax.dot_general(
            integrals[:, :, at].reshape(blocks * pairs, width),
            chunk,
            (((1,), (1,)), ((), ())),
            preferred_element_type=jnp.float32,
        )
        total = term if total is None else total + term
    for b in range(blocks):
        value = total[b * pairs : (b + 1) * pairs].T
        own[b] = value[:part]
        other[b] = value[part:].astype(other.dtype)


def scatter_coulomb_kernel(devices, blocks, cap, table, screen, own, other, *rest):
    sends, ready = rest[:-1], rest[-1]
    for b in range(blocks):
        value = (own[b] + other[b].astype(jnp.float32)) * screen[b]
        ready[b] = value.astype(jnp.bfloat16)
    for group in range(2):
        for step in range(devices):
            for rank in range(cap):
                b = jnp.maximum(table[(group * devices + step) * cap + rank], 0)
                if len(sends) == 1:
                    sends[0][step, group * cap + rank] = ready[b]
                else:
                    sends[step][group * cap + rank] = ready[b]


def gather_coulomb_kernel(devices, blocks, shell, cap, counts, table, *rest):
    received, start = [], 0
    for count in counts:
        received.append(rest[start : start + count])
        start += count
    rows, cols, landed, done, sems = rest[start:]
    part = landed.shape[2] // len(counts)
    pairs = landed.shape[3]
    for chain, pieces in enumerate(received):
        for group in range(2):
            for step in range(devices):
                for rank in range(cap):
                    row = table[((chain * 2 + group) * devices + step) * cap + rank]

                    @pl.when(row >= 0)
                    def _():
                        landed[group, row, pl.ds(chain * part, part)] = slot(
                            pieces, devices, step, group * cap + rank
                        )

    to = lax.broadcasted_iota(jnp.int32, (pairs, pairs), 0)
    source = lax.broadcasted_iota(jnp.int32, (pairs, pairs), 1)
    turns = (to, (to % shell) * shell + to // shell)
    copies = []
    for group in range(2):
        turn = (source == turns[group]).astype(jnp.bfloat16)
        for row in range(blocks):
            done[group, row] = lax.dot_general(
                turn,
                landed[group, row],
                (((1,), (1,)), ((), ())),
                preferred_element_type=jnp.float32,
            ).astype(jnp.bfloat16)
            copy = pltpu.make_async_copy(
                done.at[group, row], (rows, cols)[group].at[row], sems.at[group, row]
            )
            copy.start()
            copies.append(copy)
    for copy in copies:
        copy.wait()


def local(three_index, density, screen, pair_shells, home_slot, mirror_slot):
    blocks, pairs, aux_dev = three_index.shape
    ndens = density.shape[2]
    shell = math.isqrt(pairs)
    n = lax.axis_size("pair")
    cores = lax.axis_size("aux")
    me = lax.axis_index("pair")
    core = lax.axis_index("aux")
    half = ndens // cores
    part = half // CHAINS
    both = cores * part
    width = aux_dev // n
    cap = 2 + (blocks - 1) // n
    bf16, f32 = jnp.bfloat16, jnp.float32
    in_vmem = pl.BlockSpec(memory_space=pltpu.VMEM)
    anywhere = pl.BlockSpec(memory_space=pl.ANY)
    ints = functools.partial(jnp.concatenate, axis=0)

    def call(kernel, name, table, args, out_shape, out_specs, ready=(), scratch=(), flops=0):
        return pl.pallas_call(
            kernel,
            out_shape=out_shape,
            grid_spec=pltpu.PrefetchScalarGridSpec(
                num_scalar_prefetch=1,
                grid=(),
                in_specs=[in_vmem] * len(args) + [anywhere] * len(ready),
                out_specs=out_specs,
                scratch_shapes=list(scratch),
            ),
            compiler_params=pltpu.CompilerParams(vmem_limit_bytes=VMEM_BYTES),
            cost_estimate=pl.CostEstimate(flops=flops, bytes_accessed=0, transcendentals=0),
            name=name,
        )(table, *args, *ready)

    def shift(x, d):
        return lax.ppermute(x, "pair", [(s, (s + d) % n) for s in range(n)])

    def flip(x, bit):
        return lax.ppermute(x, "pair", [(s, s ^ bit) for s in range(n)])

    def after(x, *others):
        return lax.optimization_barrier((x, *others))[0]

    def swap(x):
        return lax.ppermute(x, "aux", [(s, (s + 1) % cores) for s in range(cores)])

    home_target, home_rank, home_source, home_row_rank = tables(home_slot, n, blocks, me)
    mirror_target, mirror_rank, mirror_source, mirror_row_rank = tables(
        mirror_slot, n, blocks, me
    )
    held = functools.partial(slots_of, devices=n, cap=cap)
    send_table = ints(
        [
            held((home_source - me) % n, home_row_rank),
            held(home_source, home_row_rank),
            core[None].astype(jnp.int32),
        ]
    )
    pick_tables = (held((me - home_target) % n, home_rank), held(home_target, home_rank))
    chunk_table = me ^ jnp.arange(n, dtype=jnp.int32)
    out_tables = (
        ints([held(home_target, home_rank), held(mirror_target, mirror_rank)]),
        ints(
            [
                held((home_target - me) % n, home_rank),
                held((mirror_target - me) % n, mirror_rank),
            ]
        ),
    )
    in_table = ints(
        [
            held(home_source, home_row_rank),
            held(mirror_source, mirror_row_rank),
            held((me - home_source) % n, home_row_rank),
            held((me - mirror_source) % n, mirror_row_rank),
        ]
    )
    weight = jnp.where(pair_shells[:, 0] != pair_shells[:, 1], 2.0, 1.0)
    factor = (screen.astype(f32) * weight[:, None]).astype(bf16)[:, None, :]
    keeping = screen.astype(f32)[:, None, :]

    integrals = pl.pallas_call(
        load_kernel,
        out_shape=pltpu.VMEM((blocks, pairs, aux_dev), bf16),
        in_specs=[anywhere],
        out_specs=in_vmem,
        scratch_shapes=[pltpu.SemaphoreType.DMA],
        compiler_params=pltpu.CompilerParams(vmem_limit_bytes=2 * 1024 * 1024),
        name="load_integrals",
    )(three_index)

    sends = pl.pallas_call(
        functools.partial(scatter_density_kernel, n, blocks, cap),
        out_shape=[jax.ShapeDtypeStruct((cap, part, pairs), bf16)] * n
        + [jax.ShapeDtypeStruct((n, cap, part, pairs), bf16)],
        grid_spec=pltpu.PrefetchScalarGridSpec(
            num_scalar_prefetch=1,
            grid=(1,),
            in_specs=[pl.BlockSpec((blocks, pairs, half), lambda i, t: (0, 0, t[2 * n * cap]))],
            out_specs=[pl.BlockSpec((cap, part, pairs), lambda i, t: (0, 0, 0))] * n
            + [pl.BlockSpec((n, cap, part, pairs), lambda i, t: (0, 0, 0, 0))],
            scratch_shapes=[pltpu.VMEM((blocks, half, pairs), bf16)],
        ),
        compiler_params=pltpu.CompilerParams(vmem_limit_bytes=VMEM_BYTES),
        name="scatter_density",
    )(send_table, density)

    def fetch(received, pick_table, ready):
        own = call(
            functools.partial(gather_density_kernel, n, cap, len(received)),
            "gather_density",
            pick_table,
            received,
            jax.ShapeDtypeStruct((blocks, part, pairs), bf16),
            in_vmem,
            ready,
        )
        return own, swap(own)

    def fit(own, other):
        return call(
            functools.partial(fit_kernel, n, blocks),
            "fit",
            chunk_table,
            [factor, own, other, integrals],
            [
                jax.ShapeDtypeStruct((n // 2, both, width), f32),
                jax.ShapeDtypeStruct((n // 2, both, width), bf16),
            ],
            [in_vmem] * 2,
            flops=2 * blocks * pairs * aux_dev * both,
        )

    def total(keep, send, marks):
        bit = 1
        while True:
            value = keep + flip(send, bit).astype(f32)
            bit *= 2
            if bit == n:
                break
            keep, send = value[0::2], value[1::2].astype(bf16)
            marks.append(send)
        near, order = value.astype(bf16), [0]
        while True:
            bit //= 2
            far = flip(near, bit)
            order = order + [e ^ bit for e in order]
            if bit == 1:
                return near, far, order
            near = jnp.concatenate([near, far], axis=0)

    def apply(near, far, order, ready):
        mine, theirs = call(
            functools.partial(apply_kernel, n, blocks, order),
            "apply",
            chunk_table,
            [integrals, near, far],
            [
                jax.ShapeDtypeStruct((blocks, part, pairs), f32),
                jax.ShapeDtypeStruct((blocks, part, pairs), bf16),
            ],
            [in_vmem] * 2,
            ready,
            flops=2 * blocks * pairs * aux_dev * both,
        )
        return mine, swap(theirs)

    def pack(mine, added, out_table, shapes):
        return call(
            functools.partial(scatter_coulomb_kernel, n, blocks, cap),
            "scatter_coulomb",
            out_table,
            [keeping, mine, added],
            shapes,
            [in_vmem] * len(shapes),
            scratch=[pltpu.VMEM((blocks, part, pairs), bf16)],
        )

    def spread(x):
        return lax.all_to_all(x, "pair", 0, 0, tiled=True)

    first = [sends[0]]
    for d in range(1, n):
        first.append(shift(after(sends[d], integrals) if d > n - 3 else sends[d], d))
    second = [spread(sends[n])]
    marks = []
    begun = fit(*fetch(first, pick_tables[0], ()))
    found = total(*begun, marks)
    begun = fit(*fetch(second, pick_tables[1], marks[:1]))
    whole = [jax.ShapeDtypeStruct((n, 2 * cap, part, pairs), bf16)]
    pieces = [jax.ShapeDtypeStruct((2 * cap, part, pairs), bf16)] * n
    out = pack(*apply(*found, ()), out_tables[0], whole)
    received = [spread(out[0])]
    out = pack(*apply(*total(*begun, marks), out), out_tables[1], pieces)
    received += [out[0]] + [shift(out[d], d) for d in range(1, n)]
    return call(
        functools.partial(gather_coulomb_kernel, n, blocks, shell, cap, (1, n)),
        "gather_coulomb",
        in_table,
        received,
        [jax.ShapeDtypeStruct((blocks, pairs, half), bf16)] * 2,
        [anywhere] * 2,
        scratch=[
            pltpu.VMEM((2, blocks, half, pairs), bf16),
            pltpu.VMEM((2, blocks, pairs, half), bf16),
            pltpu.SemaphoreType.DMA((2, blocks)),
        ],
    )


def solution(mesh):
    in_specs = (
        P(("mol", "pair"), None, "aux"),
        P(("mol", "pair"), None, None),
        P(("mol", "pair"), None),
        P(("mol", "pair"), None),
        P("mol"),
        P("mol"),
    )
    out_specs = (P(("mol", "pair"), None, "aux"), P(("mol", "pair"), None, "aux"))
    return jax.shard_map(local, mesh=mesh, in_specs=in_specs, out_specs=out_specs, check_vma=False)
```

```python
import functools
import math

import jax
import jax.numpy as jnp
from jax import lax
from jax.experimental import pallas as pl
from jax.experimental.pallas import tpu as pltpu
from jax.sharding import PartitionSpec as P

VMEM_BYTES = 20 * 1024 * 1024


def tables(slots, devices, blocks_dev, me):
    total = slots.shape[0]
    numbers = jnp.arange(total, dtype=jnp.int32)
    source = numbers // blocks_dev
    target = slots // blocks_dev
    joined = source * devices + target
    earlier = (joined[:, None] == joined[None, :]) & (numbers[None, :] < numbers[:, None])
    rank = jnp.sum(earlier.astype(jnp.int32), axis=1)
    own_target = lax.dynamic_slice_in_dim(target, me * blocks_dev, blocks_dev, 0)
    own_rank = lax.dynamic_slice_in_dim(rank, me * blocks_dev, blocks_dev, 0)
    rows = me * blocks_dev + jnp.arange(blocks_dev, dtype=jnp.int32)
    hot = slots[None, :] == rows[:, None]
    row_source = jnp.sum(jnp.where(hot, source[None, :], 0), axis=1)
    row_rank = jnp.sum(jnp.where(hot, rank[None, :], 0), axis=1)
    return own_target, own_rank, row_source, row_rank


def slots_of(steps, ranks, devices, cap):
    held = (steps * cap + ranks)[None, :] == jnp.arange(devices * cap, dtype=jnp.int32)[:, None]
    numbers = jnp.arange(steps.shape[0], dtype=jnp.int32)
    return jnp.max(jnp.where(held, numbers[None, :], -1), axis=1)


def load_kernel(source, target, sem):
    copy = pltpu.make_async_copy(source, target, sem)
    copy.start()
    copy.wait()


def scatter_density_kernel(devices, blocks, cap, table, density, *rest):
    sends, turned = rest[:devices], rest[-1]
    for row in range(blocks):
        turned[row] = density[row].T
    for step in range(devices):
        for rank in range(cap):
            row = jnp.maximum(table[step * cap + rank], 0)
            sends[step][rank] = turned[row]


def gather_density_kernel(devices, cap, table, *rest):
    received, out = rest[:devices], rest[-1]
    for step in range(devices):
        for rank in range(cap):
            row = table[step * cap + rank]

            @pl.when(row >= 0)
            def _():
                out[row] = received[step][rank]


def fit_kernel(bits, blocks, table, factor, density, integrals, *rest):
    keep, send = rest[-2:]
    width = keep.shape[2]
    pairs = integrals.shape[1]
    fitted = jnp.concatenate([density[b] * factor[b] for b in range(blocks)], axis=1)
    for i in range(keep.shape[0]):
        e = sum(bit for j, bit in enumerate(bits[1:]) if i >> j & 1)
        for relative, out in ((e ^ bits[0], send), (e, keep)):
            at = pl.ds(pl.multiple_of(table[relative] * width, width), width)
            out[i] = jnp.dot(
                fitted,
                integrals[:, :, at].reshape(blocks * pairs, width),
                preferred_element_type=jnp.float32,
            ).astype(out.dtype)


def apply_kernel(orders, some, table, integrals, near, far, near_other, far_other, own, other):
    blocks, pairs, half = integrals.shape[0], integrals.shape[1], own.shape[1]
    count, _, width = near.shape
    chunks = []
    for order, low, high in ((orders[0], near, far), (orders[1], near_other, far_other)):
        chunks.append({e: (low, i) if i < count else (high, i - count) for i, e in enumerate(order)})
    for first in range(0, blocks, some):
        total = None
        for e in range(2 * count):
            at = pl.ds(pl.multiple_of(table[e] * width, width), width)
            term = lax.dot_general(
                integrals[first : first + some, :, at].reshape(some * pairs, width),
                jnp.concatenate([piece[e][0][piece[e][1]] for piece in chunks], axis=0),
                (((1,), (1,)), ((), ())),
                preferred_element_type=jnp.float32,
            )
            total = term if total is None else total + term
        for b in range(some):
            value = total[b * pairs : (b + 1) * pairs].T
            own[first + b] = value[:half]
            other[first + b] = value[half:].astype(other.dtype)


def scatter_coulomb_kernel(devices, blocks, cap, table, screen, own, other, *rest):
    sends, ready = rest[:devices], rest[devices]
    for b in range(blocks):
        value = (own[b] + other[b].astype(jnp.float32)) * screen[b]
        ready[b] = value.astype(jnp.bfloat16)
    for group in range(2):
        for step in range(devices):
            for rank in range(cap):
                b = jnp.maximum(table[(group * devices + step) * cap + rank], 0)
                sends[step][group * cap + rank] = ready[b]


def gather_coulomb_kernel(devices, blocks, shell, cap, table, *rest):
    received = rest[:devices]
    rows, cols, landed, done, sems = rest[devices:]
    pairs = landed.shape[3]
    for group in range(2):
        for step in range(devices):
            for rank in range(cap):
                row = table[(group * devices + step) * cap + rank]

                @pl.when(row >= 0)
                def _():
                    landed[group, row] = received[step][group * cap + rank]

    to = lax.broadcasted_iota(jnp.int32, (pairs, pairs), 0)
    source = lax.broadcasted_iota(jnp.int32, (pairs, pairs), 1)
    turns = (to, (to % shell) * shell + to // shell)
    copies = []
    for group in range(2):
        turn = (source == turns[group]).astype(jnp.bfloat16)
        for row in range(blocks):
            done[group, row] = lax.dot_general(
                turn,
                landed[group, row],
                (((1,), (1,)), ((), ())),
                preferred_element_type=jnp.float32,
            ).astype(jnp.bfloat16)
            copy = pltpu.make_async_copy(
                done.at[group, row], (rows, cols)[group].at[row], sems.at[group, row]
            )
            copy.start()
            copies.append(copy)
    for copy in copies:
        copy.wait()


def local(three_index, density, screen, pair_shells, home_slot, mirror_slot):
    blocks, pairs, aux_dev = three_index.shape
    ndens = density.shape[2]
    shell = math.isqrt(pairs)
    n = lax.axis_size("pair")
    cores = lax.axis_size("aux")
    me = lax.axis_index("pair")
    core = lax.axis_index("aux")
    half = ndens // cores
    width = aux_dev // n
    cap = 2 + (blocks - 1) // n
    bf16, f32 = jnp.bfloat16, jnp.float32
    in_vmem = pl.BlockSpec(memory_space=pltpu.VMEM)
    anywhere = pl.BlockSpec(memory_space=pl.ANY)
    ints = functools.partial(jnp.concatenate, axis=0)

    def call(kernel, name, table, args, out_shape, out_specs, ready=(), scratch=()):
        return pl.pallas_call(
            kernel,
            out_shape=out_shape,
            grid_spec=pltpu.PrefetchScalarGridSpec(
                num_scalar_prefetch=1,
                grid=(),
                in_specs=[in_vmem] * len(args) + [anywhere] * len(ready),
                out_specs=out_specs,
                scratch_shapes=list(scratch),
            ),
            compiler_params=pltpu.CompilerParams(vmem_limit_bytes=VMEM_BYTES),
            name=name,
        )(table, *args, *ready)

    def shift(x, d):
        return lax.ppermute(x, "pair", [(s, (s + d) % n) for s in range(n)])

    def flip(x, bit):
        return lax.ppermute(x, "pair", [(s, s ^ bit) for s in range(n)])

    def swap(x):
        return lax.ppermute(x, "aux", [(s, (s + 1) % cores) for s in range(cores)])

    def after(x, *others):
        return lax.optimization_barrier((x, *others))[0]

    home_target, home_rank, home_source, home_row_rank = tables(home_slot, n, blocks, me)
    mirror_target, mirror_rank, mirror_source, mirror_row_rank = tables(
        mirror_slot, n, blocks, me
    )
    held = functools.partial(slots_of, devices=n, cap=cap)
    send_table = ints([held((home_source - me) % n, home_row_rank), core[None].astype(jnp.int32)])
    pick_table = held((me - home_target) % n, home_rank)
    chunk_table = me ^ jnp.arange(n, dtype=jnp.int32)
    out_table = ints(
        [
            held((home_target - me) % n, home_rank),
            held((mirror_target - me) % n, mirror_rank),
        ]
    )
    in_table = ints(
        [held((me - home_source) % n, home_row_rank), held((me - mirror_source) % n, mirror_row_rank)]
    )
    weight = jnp.where(pair_shells[:, 0] != pair_shells[:, 1], 2.0, 1.0)
    factor = (screen.astype(f32) * weight[:, None]).astype(bf16)[:, None, :]
    keeping = screen.astype(f32)[:, None, :]

    integrals = pl.pallas_call(
        load_kernel,
        out_shape=pltpu.VMEM((blocks, pairs, aux_dev), bf16),
        in_specs=[anywhere],
        out_specs=in_vmem,
        scratch_shapes=[pltpu.SemaphoreType.DMA],
        compiler_params=pltpu.CompilerParams(vmem_limit_bytes=2 * 1024 * 1024),
        name="load_integrals",
    )(three_index)

    sends = pl.pallas_call(
        functools.partial(scatter_density_kernel, n, blocks, cap),
        out_shape=[jax.ShapeDtypeStruct((cap, half, pairs), bf16)] * n,
        grid_spec=pltpu.PrefetchScalarGridSpec(
            num_scalar_prefetch=1,
            grid=(1,),
            in_specs=[pl.BlockSpec((blocks, pairs, half), lambda i, t: (0, 0, t[n * cap]))],
            out_specs=[pl.BlockSpec((cap, half, pairs), lambda i, t: (0, 0, 0))] * n,
            scratch_shapes=[pltpu.VMEM((blocks, half, pairs), bf16)],
        ),
        compiler_params=pltpu.CompilerParams(vmem_limit_bytes=VMEM_BYTES),
        name="scatter_density",
    )(send_table, density)
    received = [sends[0]] + [
        shift(after(sends[d], integrals) if d > n - 3 else sends[d], d) for d in range(1, n)
    ]
    own = call(
        functools.partial(gather_density_kernel, n, cap),
        "gather_density",
        pick_table,
        received,
        jax.ShapeDtypeStruct((blocks, half, pairs), bf16),
        in_vmem,
    )
    other = swap(own)

    bits = [1 << j for j in range(n.bit_length() - 1)]
    orders = (bits, bits[1::-1] + bits[2:])

    def fit(value, bits, ready=()):
        return call(
            functools.partial(fit_kernel, bits, blocks),
            "fit",
            chunk_table,
            [factor, value, integrals],
            [
                jax.ShapeDtypeStruct((n // 2, half, width), f32),
                jax.ShapeDtypeStruct((n // 2, half, width), bf16),
            ],
            [in_vmem] * 2,
            ready,
        )

    def step_together(states):
        flat, tree = jax.tree.flatten(states)
        return jax.tree.unflatten(tree, lax.optimization_barrier(flat))

    def totals(states):
        for j in range(len(bits)):
            states = step_together(states)
            found = []
            for (keep, send), order in zip(states, orders):
                value = keep + flip(send, order[j]).astype(f32)
                if j < len(bits) - 1:
                    found.append((value[0::2], value[1::2].astype(bf16)))
                else:
                    found.append(value.astype(bf16))
            states = found
        relative = [[0] for _ in orders]
        for j in reversed(range(len(bits))):
            states = step_together(states)
            fars = [flip(near, order[j]) for near, order in zip(states, orders)]
            relative = [r + [e ^ order[j] for e in r] for r, order in zip(relative, orders)]
            if j == 0:
                return [(*pair, r) for pair, r in zip(zip(states, fars), relative)]
            states = [jnp.concatenate(pair, axis=0) for pair in zip(states, fars)]

    fit_own = fit(own, orders[0])
    fit_other = fit(other, orders[1], fit_own[:1])
    (near_own, far_own, order_own), (near_other, far_other, order_other) = totals(
        [tuple(fit_own), tuple(fit_other)]
    )

    mine, theirs = call(
        functools.partial(apply_kernel, (order_own, order_other), blocks // 2),
        "apply",
        chunk_table,
        [integrals, near_own, far_own, near_other, far_other],
        [
            jax.ShapeDtypeStruct((blocks, half, pairs), f32),
            jax.ShapeDtypeStruct((blocks, half, pairs), bf16),
        ],
        [in_vmem] * 2,
    )
    sends = call(
        functools.partial(scatter_coulomb_kernel, n, blocks, cap),
        "scatter_coulomb",
        out_table,
        [keeping, mine, swap(theirs)],
        [jax.ShapeDtypeStruct((2 * cap, half, pairs), bf16)] * n,
        [in_vmem] * n,
        scratch=[pltpu.VMEM((blocks, half, pairs), bf16)],
    )
    received = [sends[0]] + [shift(sends[d], d) for d in range(1, n)]
    return call(
        functools.partial(gather_coulomb_kernel, n, blocks, shell, cap),
        "gather_coulomb",
        in_table,
        received,
        [jax.ShapeDtypeStruct((blocks, pairs, half), bf16)] * 2,
        [anywhere] * 2,
        scratch=[
            pltpu.VMEM((2, blocks, half, pairs), bf16),
            pltpu.VMEM((2, blocks, pairs, half), bf16),
            pltpu.SemaphoreType.DMA((2, blocks)),
        ],
    )


def solution(mesh):
    in_specs = (
        P(("mol", "pair"), None, "aux"),
        P(("mol", "pair"), None, None),
        P(("mol", "pair"), None),
        P(("mol", "pair"), None),
        P("mol"),
        P("mol"),
    )
    out_specs = (P(("mol", "pair"), None, "aux"), P(("mol", "pair"), None, "aux"))
    return jax.shard_map(local, mesh=mesh, in_specs=in_specs, out_specs=out_specs, check_vma=False)
```

```python
import functools
import math

import jax
import jax.numpy as jnp
from jax import lax
from jax.experimental import pallas as pl
from jax.experimental.pallas import tpu as pltpu
from jax.sharding import PartitionSpec as P

VMEM_BYTES = 20 * 1024 * 1024


def tables(slots, devices, blocks_dev, me):
    total = slots.shape[0]
    numbers = jnp.arange(total, dtype=jnp.int32)
    source = numbers // blocks_dev
    target = slots // blocks_dev
    joined = source * devices + target
    earlier = (joined[:, None] == joined[None, :]) & (numbers[None, :] < numbers[:, None])
    rank = jnp.sum(earlier.astype(jnp.int32), axis=1)
    own_target = lax.dynamic_slice_in_dim(target, me * blocks_dev, blocks_dev, 0)
    own_rank = lax.dynamic_slice_in_dim(rank, me * blocks_dev, blocks_dev, 0)
    rows = me * blocks_dev + jnp.arange(blocks_dev, dtype=jnp.int32)
    hot = slots[None, :] == rows[:, None]
    row_source = jnp.sum(jnp.where(hot, source[None, :], 0), axis=1)
    row_rank = jnp.sum(jnp.where(hot, rank[None, :], 0), axis=1)
    return own_target, own_rank, row_source, row_rank


def slots_of(steps, ranks, devices, cap):
    held = (steps * cap + ranks)[None, :] == jnp.arange(devices * cap, dtype=jnp.int32)[:, None]
    numbers = jnp.arange(steps.shape[0], dtype=jnp.int32)
    return jnp.max(jnp.where(held, numbers[None, :], -1), axis=1)


def load_kernel(source, ready, target, sem):
    copy = pltpu.make_async_copy(source, target, sem)
    copy.start()
    copy.wait()


def scatter_density_kernel(devices, blocks, cap, table, density, *rest):
    sends, turned = rest[:devices], rest[-1]
    for row in range(blocks):
        turned[row] = density[row].T
    for step in range(devices):
        for rank in range(cap):
            row = jnp.maximum(table[step * cap + rank], 0)
            sends[step][rank] = turned[row]


def gather_density_kernel(devices, cap, table, *rest):
    received, out = rest[:devices], rest[-1]
    for step in range(devices):
        for rank in range(cap):
            row = table[step * cap + rank]

            @pl.when(row >= 0)
            def _():
                out[row] = received[step][rank]


def fit_kernel(bits, blocks, table, factor, density, integrals, *rest):
    keep, send = rest[-2:]
    width = keep.shape[2]
    pairs = integrals.shape[1]
    fitted = jnp.concatenate([density[b] * factor[b] for b in range(blocks)], axis=1)
    for i in range(keep.shape[0]):
        e = sum(bit for j, bit in enumerate(bits[1:]) if i >> j & 1)
        for relative, out in ((e ^ bits[0], send), (e, keep)):
            at = pl.ds(pl.multiple_of(table[relative] * width, width), width)
            out[i] = jnp.dot(
                fitted,
                integrals[:, :, at].reshape(blocks * pairs, width),
                preferred_element_type=jnp.float32,
            ).astype(out.dtype)


def apply_kernel(orders, some, table, integrals, near, far, near_other, far_other, own, other):
    blocks, pairs, half = integrals.shape[0], integrals.shape[1], own.shape[1]
    count, _, width = near.shape
    chunks = []
    for order, low, high in ((orders[0], near, far), (orders[1], near_other, far_other)):
        chunks.append({e: (low, i) if i < count else (high, i - count) for i, e in enumerate(order)})
    for first in range(0, blocks, some):
        total = None
        for e in range(2 * count):
            at = pl.ds(pl.multiple_of(table[e] * width, width), width)
            term = lax.dot_general(
                integrals[first : first + some, :, at].reshape(some * pairs, width),
                jnp.concatenate([piece[e][0][piece[e][1]] for piece in chunks], axis=0),
                (((1,), (1,)), ((), ())),
                preferred_element_type=jnp.float32,
            )
            total = term if total is None else total + term
        for b in range(some):
            value = total[b * pairs : (b + 1) * pairs].T
            own[first + b] = value[:half]
            other[first + b] = value[half:].astype(other.dtype)


def scatter_coulomb_kernel(devices, blocks, cap, table, screen, own, other, *rest):
    sends, ready = rest[:devices], rest[devices]
    for b in range(blocks):
        value = (own[b] + other[b].astype(jnp.float32)) * screen[b]
        ready[b] = value.astype(jnp.bfloat16)
    for group in range(2):
        for step in range(devices):
            for rank in range(cap):
                b = jnp.maximum(table[(group * devices + step) * cap + rank], 0)
                sends[step][group * cap + rank] = ready[b]


def gather_coulomb_kernel(devices, blocks, shell, cap, table, *rest):
    received = rest[:devices]
    rows, cols, landed, done, sems = rest[devices:]
    pairs = landed.shape[3]
    for group in range(2):
        for step in range(devices):
            for rank in range(cap):
                row = table[(group * devices + step) * cap + rank]

                @pl.when(row >= 0)
                def _():
                    landed[group, row] = received[step][group * cap + rank]

    to = lax.broadcasted_iota(jnp.int32, (pairs, pairs), 0)
    source = lax.broadcasted_iota(jnp.int32, (pairs, pairs), 1)
    turns = (to, (to % shell) * shell + to // shell)
    copies = []
    for group in range(2):
        turn = (source == turns[group]).astype(jnp.bfloat16)
        for row in range(blocks):
            done[group, row] = lax.dot_general(
                turn,
                landed[group, row],
                (((1,), (1,)), ((), ())),
                preferred_element_type=jnp.float32,
            ).astype(jnp.bfloat16)
            copy = pltpu.make_async_copy(
                done.at[group, row], (rows, cols)[group].at[row], sems.at[group, row]
            )
            copy.start()
            copies.append(copy)
    for copy in copies:
        copy.wait()


def local(three_index, density, screen, pair_shells, home_slot, mirror_slot):
    blocks, pairs, aux_dev = three_index.shape
    ndens = density.shape[2]
    shell = math.isqrt(pairs)
    n = lax.axis_size("pair")
    cores = lax.axis_size("aux")
    me = lax.axis_index("pair")
    core = lax.axis_index("aux")
    half = ndens // cores
    width = aux_dev // n
    cap = 2 + (blocks - 1) // n
    bf16, f32 = jnp.bfloat16, jnp.float32
    in_vmem = pl.BlockSpec(memory_space=pltpu.VMEM)
    anywhere = pl.BlockSpec(memory_space=pl.ANY)
    ints = functools.partial(jnp.concatenate, axis=0)

    def call(kernel, name, table, args, out_shape, out_specs, ready=(), scratch=()):
        return pl.pallas_call(
            kernel,
            out_shape=out_shape,
            grid_spec=pltpu.PrefetchScalarGridSpec(
                num_scalar_prefetch=1,
                grid=(),
                in_specs=[in_vmem] * len(args) + [anywhere] * len(ready),
                out_specs=out_specs,
                scratch_shapes=list(scratch),
            ),
            compiler_params=pltpu.CompilerParams(vmem_limit_bytes=VMEM_BYTES),
            name=name,
        )(table, *args, *ready)

    def shift(x, d):
        return lax.ppermute(x, "pair", [(s, (s + d) % n) for s in range(n)])

    def flip(x, bit):
        return lax.ppermute(x, "pair", [(s, s ^ bit) for s in range(n)])

    def swap(x):
        return lax.ppermute(x, "aux", [(s, (s + 1) % cores) for s in range(cores)])

    def after(x, *others):
        return lax.optimization_barrier((x, *others))[0]

    home_target, home_rank, home_source, home_row_rank = tables(home_slot, n, blocks, me)
    mirror_target, mirror_rank, mirror_source, mirror_row_rank = tables(
        mirror_slot, n, blocks, me
    )
    held = functools.partial(slots_of, devices=n, cap=cap)
    send_table = ints([held((home_source - me) % n, home_row_rank), core[None].astype(jnp.int32)])
    pick_table = held((me - home_target) % n, home_rank)
    chunk_table = me ^ jnp.arange(n, dtype=jnp.int32)
    out_table = ints(
        [
            held((home_target - me) % n, home_rank),
            held((mirror_target - me) % n, mirror_rank),
        ]
    )
    in_table = ints(
        [held((me - home_source) % n, home_row_rank), held((me - mirror_source) % n, mirror_row_rank)]
    )
    weight = jnp.where(pair_shells[:, 0] != pair_shells[:, 1], 2.0, 1.0)
    factor = (screen.astype(f32) * weight[:, None]).astype(bf16)[:, None, :]
    keeping = screen.astype(f32)[:, None, :]

    sends = pl.pallas_call(
        functools.partial(scatter_density_kernel, n, blocks, cap),
        out_shape=[jax.ShapeDtypeStruct((cap, half, pairs), bf16)] * n,
        grid_spec=pltpu.PrefetchScalarGridSpec(
            num_scalar_prefetch=1,
            grid=(1,),
            in_specs=[pl.BlockSpec((blocks, pairs, half), lambda i, t: (0, 0, t[n * cap]))],
            out_specs=[pl.BlockSpec((cap, half, pairs), lambda i, t: (0, 0, 0))] * n,
            scratch_shapes=[pltpu.VMEM((blocks, half, pairs), bf16)],
        ),
        compiler_params=pltpu.CompilerParams(vmem_limit_bytes=VMEM_BYTES),
        name="scatter_density",
    )(send_table, density)
    steps = sorted(range(1, n), key=lambda d: abs(2 * d - n))
    received = [sends[0]] + [None] * (n - 1)
    for d in steps[:-1]:
        received[d] = shift(sends[d], d)
    integrals = pl.pallas_call(
        load_kernel,
        out_shape=pltpu.VMEM((blocks, pairs, aux_dev), bf16),
        in_specs=[anywhere, anywhere],
        out_specs=in_vmem,
        scratch_shapes=[pltpu.SemaphoreType.DMA],
        compiler_params=pltpu.CompilerParams(vmem_limit_bytes=2 * 1024 * 1024),
        name="load_integrals",
    )(three_index, received[steps[0]])
    received[steps[-1]] = shift(after(sends[steps[-1]], integrals), steps[-1])
    own = call(
        functools.partial(gather_density_kernel, n, cap),
        "gather_density",
        pick_table,
        received,
        jax.ShapeDtypeStruct((blocks, half, pairs), bf16),
        in_vmem,
    )
    other = swap(own)

    bits = [1 << j for j in range(n.bit_length() - 1)]
    orders = (bits, bits[1::-1] + bits[2:])

    def fit(value, bits, ready=()):
        return call(
            functools.partial(fit_kernel, bits, blocks),
            "fit",
            chunk_table,
            [factor, value, integrals],
            [
                jax.ShapeDtypeStruct((n // 2, half, width), f32),
                jax.ShapeDtypeStruct((n // 2, half, width), bf16),
            ],
            [in_vmem] * 2,
            ready,
        )

    def step_together(states):
        flat, tree = jax.tree.flatten(states)
        return jax.tree.unflatten(tree, lax.optimization_barrier(flat))

    def totals(states):
        for j in range(len(bits)):
            states = step_together(states)
            found = []
            for (keep, send), order in zip(states, orders):
                value = keep + flip(send, order[j]).astype(f32)
                if j < len(bits) - 1:
                    found.append((value[0::2], value[1::2].astype(bf16)))
                else:
                    found.append(value.astype(bf16))
            states = found
        relative = [[0] for _ in orders]
        for j in reversed(range(len(bits))):
            states = step_together(states)
            fars = [flip(near, order[j]) for near, order in zip(states, orders)]
            relative = [r + [e ^ order[j] for e in r] for r, order in zip(relative, orders)]
            if j == 0:
                return [(*pair, r) for pair, r in zip(zip(states, fars), relative)]
            states = [jnp.concatenate(pair, axis=0) for pair in zip(states, fars)]

    fit_own = fit(own, orders[0])
    fit_other = fit(other, orders[1], fit_own[:1])
    (near_own, far_own, order_own), (near_other, far_other, order_other) = totals(
        [tuple(fit_own), tuple(fit_other)]
    )

    mine, theirs = call(
        functools.partial(apply_kernel, (order_own, order_other), blocks // 2),
        "apply",
        chunk_table,
        [integrals, near_own, far_own, near_other, far_other],
        [
            jax.ShapeDtypeStruct((blocks, half, pairs), f32),
            jax.ShapeDtypeStruct((blocks, half, pairs), bf16),
        ],
        [in_vmem] * 2,
    )
    sends = call(
        functools.partial(scatter_coulomb_kernel, n, blocks, cap),
        "scatter_coulomb",
        out_table,
        [keeping, mine, swap(theirs)],
        [jax.ShapeDtypeStruct((2 * cap, half, pairs), bf16)] * n,
        [in_vmem] * n,
        scratch=[pltpu.VMEM((blocks, half, pairs), bf16)],
    )
    for d in steps:
        received[d] = shift(sends[d], d)
    received[0] = sends[0]
    return call(
        functools.partial(gather_coulomb_kernel, n, blocks, shell, cap),
        "gather_coulomb",
        in_table,
        received,
        [jax.ShapeDtypeStruct((blocks, pairs, half), bf16)] * 2,
        [anywhere] * 2,
        scratch=[
            pltpu.VMEM((2, blocks, half, pairs), bf16),
            pltpu.VMEM((2, blocks, pairs, half), bf16),
            pltpu.SemaphoreType.DMA((2, blocks)),
        ],
    )


def solution(mesh):
    in_specs = (
        P(("mol", "pair"), None, "aux"),
        P(("mol", "pair"), None, None),
        P(("mol", "pair"), None),
        P(("mol", "pair"), None),
        P("mol"),
        P("mol"),
    )
    out_specs = (P(("mol", "pair"), None, "aux"), P(("mol", "pair"), None, "aux"))
    return jax.shard_map(local, mesh=mesh, in_specs=in_specs, out_specs=out_specs, check_vma=False)
```

```python
import functools
import math

import jax
import jax.numpy as jnp
from jax import lax
from jax.experimental import pallas as pl
from jax.experimental.pallas import tpu as pltpu
from jax.sharding import PartitionSpec as P

VMEM_BYTES = 20 * 1024 * 1024


def tables(slots, devices, blocks_dev, me):
    total = slots.shape[0]
    numbers = jnp.arange(total, dtype=jnp.int32)
    source = numbers // blocks_dev
    target = slots // blocks_dev
    joined = source * devices + target
    earlier = (joined[:, None] == joined[None, :]) & (numbers[None, :] < numbers[:, None])
    rank = jnp.sum(earlier.astype(jnp.int32), axis=1)
    own_target = lax.dynamic_slice_in_dim(target, me * blocks_dev, blocks_dev, 0)
    own_rank = lax.dynamic_slice_in_dim(rank, me * blocks_dev, blocks_dev, 0)
    rows = me * blocks_dev + jnp.arange(blocks_dev, dtype=jnp.int32)
    hot = slots[None, :] == rows[:, None]
    row_source = jnp.sum(jnp.where(hot, source[None, :], 0), axis=1)
    row_rank = jnp.sum(jnp.where(hot, rank[None, :], 0), axis=1)
    return own_target, own_rank, row_source, row_rank


def slots_of(steps, ranks, devices, cap):
    held = (steps * cap + ranks)[None, :] == jnp.arange(devices * cap, dtype=jnp.int32)[:, None]
    numbers = jnp.arange(steps.shape[0], dtype=jnp.int32)
    return jnp.max(jnp.where(held, numbers[None, :], -1), axis=1)


def load_kernel(source, ready, target, sem):
    copy = pltpu.make_async_copy(source, target, sem)
    copy.start()
    copy.wait()


def scatter_density_kernel(devices, blocks, cap, table, density, *rest):
    sends, turned = rest[:devices], rest[-1]
    for row in range(blocks):
        turned[row] = density[row].T
    for step in range(devices):
        for rank in range(cap):
            row = jnp.maximum(table[step * cap + rank], 0)
            sends[step][rank] = turned[row]


def gather_density_kernel(steps, cap, table, *rest):
    out = rest[-1]
    for step, piece in zip(steps, rest):
        for rank in range(cap):
            row = table[step * cap + rank]

            @pl.when(row >= 0)
            def _():
                out[row] = piece[rank]


def fit_kernel(bits, blocks, table, factor, density, integrals, *rest):
    keep, send = rest[-2:]
    width = keep.shape[2]
    pairs = integrals.shape[1]
    fitted = jnp.concatenate([density[b] * factor[b] for b in range(blocks)], axis=1)
    for i in range(keep.shape[0]):
        e = sum(bit for j, bit in enumerate(bits[1:]) if i >> j & 1)
        for relative, out in ((e ^ bits[0], send), (e, keep)):
            at = pl.ds(pl.multiple_of(table[relative] * width, width), width)
            out[i] = jnp.dot(
                fitted,
                integrals[:, :, at].reshape(blocks * pairs, width),
                preferred_element_type=jnp.float32,
            ).astype(out.dtype)


def apply_kernel(orders, some, table, integrals, near, far, near_other, far_other, own, other):
    blocks, pairs, half = integrals.shape[0], integrals.shape[1], own.shape[1]
    count, _, width = near.shape
    chunks = []
    for order, low, high in ((orders[0], near, far), (orders[1], near_other, far_other)):
        chunks.append({e: (low, i) if i < count else (high, i - count) for i, e in enumerate(order)})
    for first in range(0, blocks, some):
        total = None
        for e in range(2 * count):
            at = pl.ds(pl.multiple_of(table[e] * width, width), width)
            term = lax.dot_general(
                integrals[first : first + some, :, at].reshape(some * pairs, width),
                jnp.concatenate([piece[e][0][piece[e][1]] for piece in chunks], axis=0),
                (((1,), (1,)), ((), ())),
                preferred_element_type=jnp.float32,
            )
            total = term if total is None else total + term
        for b in range(some):
            value = total[b * pairs : (b + 1) * pairs].T
            own[first + b] = value[:half]
            other[first + b] = value[half:].astype(other.dtype)


def scatter_coulomb_kernel(devices, blocks, cap, table, screen, own, other, *rest):
    sends, ready = rest[:devices], rest[devices]
    for b in range(blocks):
        value = (own[b] + other[b].astype(jnp.float32)) * screen[b]
        ready[b] = value.astype(jnp.bfloat16)
    for group in range(2):
        for step in range(devices):
            for rank in range(cap):
                b = jnp.maximum(table[(group * devices + step) * cap + rank], 0)
                sends[step][group * cap + rank] = ready[b]


def gather_coulomb_kernel(steps, blocks, shell, cap, table, *rest):
    devices = len(steps)
    rows, cols, landed, done, sems = rest[devices:]
    pairs = landed.shape[3]
    for step, piece in zip(steps, rest):
        for group in range(2):
            for rank in range(cap):
                row = table[(group * devices + step) * cap + rank]

                @pl.when(row >= 0)
                def _():
                    landed[group, row] = piece[group * cap + rank]

    to = lax.broadcasted_iota(jnp.int32, (pairs, pairs), 0)
    source = lax.broadcasted_iota(jnp.int32, (pairs, pairs), 1)
    turns = (to, (to % shell) * shell + to // shell)
    copies = []
    for group in range(2):
        turn = (source == turns[group]).astype(jnp.bfloat16)
        for row in range(blocks):
            done[group, row] = lax.dot_general(
                turn,
                landed[group, row],
                (((1,), (1,)), ((), ())),
                preferred_element_type=jnp.float32,
            ).astype(jnp.bfloat16)
            copy = pltpu.make_async_copy(
                done.at[group, row], (rows, cols)[group].at[row], sems.at[group, row]
            )
            copy.start()
            copies.append(copy)
    for copy in copies:
        copy.wait()


def local(three_index, density, screen, pair_shells, home_slot, mirror_slot):
    blocks, pairs, aux_dev = three_index.shape
    ndens = density.shape[2]
    shell = math.isqrt(pairs)
    n = lax.axis_size("pair")
    cores = lax.axis_size("aux")
    me = lax.axis_index("pair")
    core = lax.axis_index("aux")
    half = ndens // cores
    width = aux_dev // n
    cap = 2 + (blocks - 1) // n
    bf16, f32 = jnp.bfloat16, jnp.float32
    in_vmem = pl.BlockSpec(memory_space=pltpu.VMEM)
    anywhere = pl.BlockSpec(memory_space=pl.ANY)
    ints = functools.partial(jnp.concatenate, axis=0)

    def call(kernel, name, table, args, out_shape, out_specs, ready=(), scratch=()):
        return pl.pallas_call(
            kernel,
            out_shape=out_shape,
            grid_spec=pltpu.PrefetchScalarGridSpec(
                num_scalar_prefetch=1,
                grid=(),
                in_specs=[in_vmem] * len(args) + [anywhere] * len(ready),
                out_specs=out_specs,
                scratch_shapes=list(scratch),
            ),
            compiler_params=pltpu.CompilerParams(vmem_limit_bytes=VMEM_BYTES),
            name=name,
        )(table, *args, *ready)

    def shift(x, d):
        return lax.ppermute(x, "pair", [(s, (s + d) % n) for s in range(n)])

    def flip(x, bit):
        return lax.ppermute(x, "pair", [(s, s ^ bit) for s in range(n)])

    def swap(x):
        return lax.ppermute(x, "aux", [(s, (s + 1) % cores) for s in range(cores)])

    def after(x, *others):
        return lax.optimization_barrier((x, *others))[0]

    home_target, home_rank, home_source, home_row_rank = tables(home_slot, n, blocks, me)
    held = functools.partial(slots_of, devices=n, cap=cap)
    send_table = ints([held((home_source - me) % n, home_row_rank), core[None].astype(jnp.int32)])
    pick_table = held((me - home_target) % n, home_rank)
    chunk_table = me ^ jnp.arange(n, dtype=jnp.int32)
    weight = jnp.where(pair_shells[:, 0] != pair_shells[:, 1], 2.0, 1.0)
    factor = (screen.astype(f32) * weight[:, None]).astype(bf16)[:, None, :]
    keeping = screen.astype(f32)[:, None, :]

    sends = pl.pallas_call(
        functools.partial(scatter_density_kernel, n, blocks, cap),
        out_shape=[jax.ShapeDtypeStruct((cap, half, pairs), bf16)] * n,
        grid_spec=pltpu.PrefetchScalarGridSpec(
            num_scalar_prefetch=1,
            grid=(1,),
            in_specs=[pl.BlockSpec((blocks, pairs, half), lambda i, t: (0, 0, t[n * cap]))],
            out_specs=[pl.BlockSpec((cap, half, pairs), lambda i, t: (0, 0, 0))] * n,
            scratch_shapes=[pltpu.VMEM((blocks, half, pairs), bf16)],
        ),
        compiler_params=pltpu.CompilerParams(vmem_limit_bytes=VMEM_BYTES),
        name="scatter_density",
    )(send_table, density)
    steps = sorted(range(1, n), key=lambda d: abs(2 * d - n))
    received = [shift(sends[d], d) for d in steps[:-1]]
    integrals = pl.pallas_call(
        load_kernel,
        out_shape=pltpu.VMEM((blocks, pairs, aux_dev), bf16),
        in_specs=[anywhere, anywhere],
        out_specs=in_vmem,
        scratch_shapes=[pltpu.SemaphoreType.DMA],
        compiler_params=pltpu.CompilerParams(vmem_limit_bytes=2 * 1024 * 1024),
        name="load_integrals",
    )(three_index, received[0])
    received += [shift(after(sends[steps[-1]], integrals), steps[-1]), sends[0]]
    steps = (*steps, 0)
    own = call(
        functools.partial(gather_density_kernel, steps, cap),
        "gather_density",
        pick_table,
        received,
        jax.ShapeDtypeStruct((blocks, half, pairs), bf16),
        in_vmem,
    )
    other = swap(own)

    mirror_target, mirror_rank, mirror_source, mirror_row_rank = tables(
        after(mirror_slot, own), n, blocks, me
    )
    out_table = ints(
        [
            held((home_target - me) % n, home_rank),
            held((mirror_target - me) % n, mirror_rank),
        ]
    )
    in_table = ints(
        [held((me - home_source) % n, home_row_rank), held((me - mirror_source) % n, mirror_row_rank)]
    )

    bits = [1 << j for j in range(n.bit_length() - 1)]
    orders = (bits[1::-1] + bits[2:], bits)

    def fit(value, bits, ready=()):
        return call(
            functools.partial(fit_kernel, bits, blocks),
            "fit",
            chunk_table,
            [factor, value, integrals],
            [
                jax.ShapeDtypeStruct((n // 2, half, width), f32),
                jax.ShapeDtypeStruct((n // 2, half, width), bf16),
            ],
            [in_vmem] * 2,
            ready,
        )

    def step_together(states):
        flat, tree = jax.tree.flatten(states)
        return jax.tree.unflatten(tree, lax.optimization_barrier(flat))

    def totals(states):
        for j in range(len(bits)):
            states = step_together(states)
            found = []
            for (keep, send), order in zip(states, orders):
                value = keep + flip(send, order[j]).astype(f32)
                if j < len(bits) - 1:
                    found.append((value[0::2], value[1::2].astype(bf16)))
                else:
                    found.append(value.astype(bf16))
            states = found
        relative = [[0] for _ in orders]
        for j in reversed(range(len(bits))):
            states = step_together(states)
            fars = [flip(near, order[j]) for near, order in zip(states, orders)]
            relative = [r + [e ^ order[j] for e in r] for r, order in zip(relative, orders)]
            if j == 0:
                return [(*pair, r) for pair, r in zip(zip(states, fars), relative)]
            states = [jnp.concatenate(pair, axis=0) for pair in zip(states, fars)]

    fit_own = fit(own, orders[1])
    fit_other = fit(other, orders[0], fit_own[:1])
    (near_other, far_other, order_other), (near_own, far_own, order_own) = totals(
        [tuple(fit_other), tuple(fit_own)]
    )

    mine, theirs = call(
        functools.partial(apply_kernel, (order_own, order_other), blocks // 2),
        "apply",
        chunk_table,
        [integrals, near_own, far_own, near_other, far_other],
        [
            jax.ShapeDtypeStruct((blocks, half, pairs), f32),
            jax.ShapeDtypeStruct((blocks, half, pairs), bf16),
        ],
        [in_vmem] * 2,
    )
    sends = call(
        functools.partial(scatter_coulomb_kernel, n, blocks, cap),
        "scatter_coulomb",
        out_table,
        [keeping, mine, swap(theirs)],
        [jax.ShapeDtypeStruct((2 * cap, half, pairs), bf16)] * n,
        [in_vmem] * n,
        scratch=[pltpu.VMEM((blocks, half, pairs), bf16)],
    )
    received = [shift(sends[d], d) if d else sends[d] for d in steps]
    return call(
        functools.partial(gather_coulomb_kernel, steps, blocks, shell, cap),
        "gather_coulomb",
        in_table,
        received,
        [jax.ShapeDtypeStruct((blocks, pairs, half), bf16)] * 2,
        [anywhere] * 2,
        scratch=[
            pltpu.VMEM((2, blocks, half, pairs), bf16),
            pltpu.VMEM((2, blocks, pairs, half), bf16),
            pltpu.SemaphoreType.DMA((2, blocks)),
        ],
    )


def solution(mesh):
    in_specs = (
        P(("mol", "pair"), None, "aux"),
        P(("mol", "pair"), None, None),
        P(("mol", "pair"), None),
        P(("mol", "pair"), None),
        P("mol"),
        P("mol"),
    )
    out_specs = (P(("mol", "pair"), None, "aux"), P(("mol", "pair"), None, "aux"))
    return jax.shard_map(local, mesh=mesh, in_specs=in_specs, out_specs=out_specs, check_vma=False)
```

```python
import functools
import math

import jax
import jax.numpy as jnp
from jax import lax
from jax.experimental import pallas as pl
from jax.experimental.pallas import tpu as pltpu
from jax.sharding import PartitionSpec as P

VMEM_BYTES = 20 * 1024 * 1024


def tables(slots, devices, blocks_dev, me):
    total = slots.shape[0]
    numbers = jnp.arange(total, dtype=jnp.int32)
    source = numbers // blocks_dev
    target = slots // blocks_dev
    joined = source * devices + target
    earlier = (joined[:, None] == joined[None, :]) & (numbers[None, :] < numbers[:, None])
    rank = jnp.sum(earlier.astype(jnp.int32), axis=1)
    held = []
    for device in (me, me ^ (devices // 2)):
        for values in (target, rank):
            held.append(lax.dynamic_slice_in_dim(values, device * blocks_dev, blocks_dev, 0))
    rows = me * blocks_dev + jnp.arange(blocks_dev, dtype=jnp.int32)
    hot = slots[None, :] == rows[:, None]
    row_source = jnp.sum(jnp.where(hot, source[None, :], 0), axis=1)
    row_rank = jnp.sum(jnp.where(hot, rank[None, :], 0), axis=1)
    return held[:2], held[2:], (row_source, row_rank)


def slots_of(steps, ranks, devices, cap):
    held = (steps * cap + ranks)[None, :] == jnp.arange(devices * cap, dtype=jnp.int32)[:, None]
    numbers = jnp.arange(steps.shape[0], dtype=jnp.int32)
    return jnp.max(jnp.where(held, numbers[None, :], -1), axis=1)


def load_kernel(source, ready, target, sem):
    copy = pltpu.make_async_copy(source, target, sem)
    copy.start()
    copy.wait()


def scatter_density_kernel(devices, blocks, cap, table, density, *rest):
    sends, turned = rest[:devices], rest[-1]
    for row in range(blocks):
        turned[row] = density[row].T
    for step in range(devices):
        for rank in range(cap):
            row = jnp.maximum(table[step * cap + rank], 0)
            sends[step][rank] = turned[row]


def gather_density_kernel(steps, cap, table, *rest):
    out = rest[-1]
    for step, piece in zip(steps, rest):
        for rank in range(cap):
            row = table[step * cap + rank]

            @pl.when(row >= 0)
            def _():
                out[row] = piece[rank]


def fit_kernel(bits, blocks, table, factor, density, integrals, *rest):
    keep, send = rest[-2:]
    width = keep.shape[2]
    pairs = integrals.shape[1]
    fitted = jnp.concatenate([density[b] * factor[b] for b in range(blocks)], axis=1)
    for i in range(keep.shape[0]):
        e = sum(bit for j, bit in enumerate(bits[1:]) if i >> j & 1)
        for relative, out in ((e ^ bits[0], send), (e, keep)):
            at = pl.ds(pl.multiple_of(table[relative] * width, width), width)
            out[i] = jnp.dot(
                fitted,
                integrals[:, :, at].reshape(blocks * pairs, width),
                preferred_element_type=jnp.float32,
            ).astype(out.dtype)


def apply_kernel(orders, some, table, integrals, near, far, near_other, far_other, own, other):
    blocks, pairs, half = integrals.shape[0], integrals.shape[1], own.shape[1]
    count, _, width = near.shape
    chunks = []
    for order, low, high in ((orders[0], near, far), (orders[1], near_other, far_other)):
        chunks.append({e: (low, i) if i < count else (high, i - count) for i, e in enumerate(order)})
    for first in range(0, blocks, some):
        total = None
        for e in range(2 * count):
            at = pl.ds(pl.multiple_of(table[e] * width, width), width)
            term = lax.dot_general(
                integrals[first : first + some, :, at].reshape(some * pairs, width),
                jnp.concatenate([piece[e][0][piece[e][1]] for piece in chunks], axis=0),
                (((1,), (1,)), ((), ())),
                preferred_element_type=jnp.float32,
            )
            total = term if total is None else total + term
        for b in range(some):
            value = total[b * pairs : (b + 1) * pairs].T
            own[first + b] = value[:half]
            other[first + b] = value[half:].astype(other.dtype)


def scatter_coulomb_kernel(devices, blocks, cap, table, screen, own, other, *rest):
    near, far, whole, ready = rest[: devices // 2], rest[devices // 2 : devices], rest[-2], rest[-1]
    part = whole.shape[2]
    for b in range(blocks):
        value = (own[b] + other[b].astype(jnp.float32)) * screen[b]
        ready[b] = value.astype(jnp.bfloat16)
        whole[b] = ready[b, :, pl.ds(0, part)]
    for group in range(2):
        for step in range(devices):
            for rank in range(cap):
                b = jnp.maximum(table[(group * devices + step) * cap + rank], 0)
                if step < devices // 2:
                    near[step][group * cap + rank] = ready[b]
                else:
                    far[step - devices // 2][group * cap + rank] = ready[b, :, pl.ds(part, part)]


def pass_on_kernel(devices, cap, table, whole, *outs):
    for group in range(2):
        for step in range(devices // 2):
            for rank in range(cap):
                b = jnp.maximum(table[(group * devices + devices // 2 + step) * cap + rank], 0)
                outs[step][group * cap + rank] = whole[b]


def gather_coulomb_kernel(devices, blocks, shell, cap, table, *rest):
    half = devices // 2
    near, far, passed = rest[:half], rest[half:devices], rest[devices : devices + half]
    rows, cols, landed, done, sems = rest[devices + half :]
    pairs = landed.shape[3]
    part = far[0].shape[2]
    for step in range(devices):
        for group in range(2):
            for rank in range(cap):
                row = table[(group * devices + step) * cap + rank]
                at = group * cap + rank

                @pl.when(row >= 0)
                def _():
                    if step < half:
                        landed[group, row] = near[step][at]
                    else:
                        landed[group, row, :, pl.ds(0, part)] = passed[step - half][at]
                        landed[group, row, :, pl.ds(part, part)] = far[step - half][at]

    to = lax.broadcasted_iota(jnp.int32, (pairs, pairs), 0)
    source = lax.broadcasted_iota(jnp.int32, (pairs, pairs), 1)
    turns = (to, (to % shell) * shell + to // shell)
    copies = []
    for group in range(2):
        turn = (source == turns[group]).astype(jnp.bfloat16)
        for row in range(blocks):
            done[group, row] = lax.dot_general(
                turn,
                landed[group, row],
                (((1,), (1,)), ((), ())),
                preferred_element_type=jnp.float32,
            ).astype(jnp.bfloat16)
            copy = pltpu.make_async_copy(
                done.at[group, row], (rows, cols)[group].at[row], sems.at[group, row]
            )
            copy.start()
            copies.append(copy)
    for copy in copies:
        copy.wait()


def local(three_index, density, screen, pair_shells, home_slot, mirror_slot):
    blocks, pairs, aux_dev = three_index.shape
    ndens = density.shape[2]
    shell = math.isqrt(pairs)
    n = lax.axis_size("pair")
    cores = lax.axis_size("aux")
    me = lax.axis_index("pair")
    core = lax.axis_index("aux")
    half = ndens // cores
    part = pairs // 2
    width = aux_dev // n
    cap = 2 + (blocks - 1) // n
    bf16, f32 = jnp.bfloat16, jnp.float32
    in_vmem = pl.BlockSpec(memory_space=pltpu.VMEM)
    anywhere = pl.BlockSpec(memory_space=pl.ANY)
    ints = functools.partial(jnp.concatenate, axis=0)

    def call(kernel, name, table, args, out_shape, out_specs, ready=(), scratch=()):
        return pl.pallas_call(
            kernel,
            out_shape=out_shape,
            grid_spec=pltpu.PrefetchScalarGridSpec(
                num_scalar_prefetch=1,
                grid=(),
                in_specs=[in_vmem] * len(args) + [anywhere] * len(ready),
                out_specs=out_specs,
                scratch_shapes=list(scratch),
            ),
            compiler_params=pltpu.CompilerParams(vmem_limit_bytes=VMEM_BYTES),
            name=name,
        )(table, *args, *ready)

    def flip(x, bit):
        return lax.ppermute(x, "pair", [(s, s ^ bit) for s in range(n)])

    def swap(x):
        return lax.ppermute(x, "aux", [(s, (s + 1) % cores) for s in range(cores)])

    def after(x, *others):
        return lax.optimization_barrier((x, *others))[0]

    def slots(peers, ranks, device):
        return slots_of(peers ^ device, ranks, n, cap)

    home_held, home_passed, home_rows = tables(home_slot, n, blocks, me)
    send_table = ints([slots(*home_rows, me), core[None].astype(jnp.int32)])
    pick_table = slots(*home_held, me)
    chunk_table = me ^ jnp.arange(n, dtype=jnp.int32)
    weight = jnp.where(pair_shells[:, 0] != pair_shells[:, 1], 2.0, 1.0)
    factor = (screen.astype(f32) * weight[:, None]).astype(bf16)[:, None, :]
    keeping = screen.astype(f32)[:, None, :]

    sends = pl.pallas_call(
        functools.partial(scatter_density_kernel, n, blocks, cap),
        out_shape=[jax.ShapeDtypeStruct((cap, half, pairs), bf16)] * n,
        grid_spec=pltpu.PrefetchScalarGridSpec(
            num_scalar_prefetch=1,
            grid=(1,),
            in_specs=[pl.BlockSpec((blocks, pairs, half), lambda i, t: (0, 0, t[n * cap]))],
            out_specs=[pl.BlockSpec((cap, half, pairs), lambda i, t: (0, 0, 0))] * n,
            scratch_shapes=[pltpu.VMEM((blocks, half, pairs), bf16)],
        ),
        compiler_params=pltpu.CompilerParams(vmem_limit_bytes=VMEM_BYTES),
        name="scatter_density",
    )(send_table, density)
    steps = [*range(n // 2, n), *range(1, n // 2)]
    received = [flip(sends[d], d) for d in steps[:-1]]
    integrals = pl.pallas_call(
        load_kernel,
        out_shape=pltpu.VMEM((blocks, pairs, aux_dev), bf16),
        in_specs=[anywhere, anywhere],
        out_specs=in_vmem,
        scratch_shapes=[pltpu.SemaphoreType.DMA],
        compiler_params=pltpu.CompilerParams(vmem_limit_bytes=2 * 1024 * 1024),
        name="load_integrals",
    )(three_index, received[0])
    received += [flip(after(sends[steps[-1]], integrals), steps[-1]), sends[0]]
    steps = (*steps, 0)
    own = call(
        functools.partial(gather_density_kernel, steps, cap),
        "gather_density",
        pick_table,
        received,
        jax.ShapeDtypeStruct((blocks, half, pairs), bf16),
        in_vmem,
    )
    other = swap(own)

    mirror_held, mirror_passed, mirror_rows = tables(after(mirror_slot, own), n, blocks, me)
    out_table = ints([slots(*home_held, me), slots(*mirror_held, me)])
    pass_table = ints([slots(*held, me ^ (n // 2)) for held in (home_passed, mirror_passed)])
    in_table = ints([slots(*home_rows, me), slots(*mirror_rows, me)])

    bits = [1 << j for j in range(n.bit_length() - 1)]
    orders = (bits[1::-1] + bits[2:], bits)

    def fit(value, bits, ready=()):
        return call(
            functools.partial(fit_kernel, bits, blocks),
            "fit",
            chunk_table,
            [factor, value, integrals],
            [
                jax.ShapeDtypeStruct((n // 2, half, width), f32),
                jax.ShapeDtypeStruct((n // 2, half, width), bf16),
            ],
            [in_vmem] * 2,
            ready,
        )

    def step_together(states):
        flat, tree = jax.tree.flatten(states)
        return jax.tree.unflatten(tree, lax.optimization_barrier(flat))

    def totals(states):
        for j in range(len(bits)):
            states = step_together(states)
            found = []
            for (keep, send), order in zip(states, orders):
                value = keep + flip(send, order[j]).astype(f32)
                if j < len(bits) - 1:
                    found.append((value[0::2], value[1::2].astype(bf16)))
                else:
                    found.append(value.astype(bf16))
            states = found
        relative = [[0] for _ in orders]
        for j in reversed(range(len(bits))):
            states = step_together(states)
            fars = [flip(near, order[j]) for near, order in zip(states, orders)]
            relative = [r + [e ^ order[j] for e in r] for r, order in zip(relative, orders)]
            if j == 0:
                return [(*pair, r) for pair, r in zip(zip(states, fars), relative)]
            states = [jnp.concatenate(pair, axis=0) for pair in zip(states, fars)]

    fit_own = fit(own, orders[1])
    fit_other = fit(other, orders[0], fit_own[:1])
    (near_other, far_other, order_other), (near_own, far_own, order_own) = totals(
        [tuple(fit_other), tuple(fit_own)]
    )

    mine, theirs = call(
        functools.partial(apply_kernel, (order_own, order_other), blocks // 2),
        "apply",
        chunk_table,
        [integrals, near_own, far_own, near_other, far_other],
        [
            jax.ShapeDtypeStruct((blocks, half, pairs), f32),
            jax.ShapeDtypeStruct((blocks, half, pairs), bf16),
        ],
        [in_vmem] * 2,
    )
    sends = call(
        functools.partial(scatter_coulomb_kernel, n, blocks, cap),
        "scatter_coulomb",
        out_table,
        [keeping, mine, swap(theirs)],
        [jax.ShapeDtypeStruct((2 * cap, half, pairs), bf16)] * (n // 2)
        + [jax.ShapeDtypeStruct((2 * cap, half, part), bf16)] * (n // 2)
        + [jax.ShapeDtypeStruct((blocks, half, part), bf16)],
        [in_vmem] * (n + 1),
        scratch=[pltpu.VMEM((blocks, half, pairs), bf16)],
    )
    whole = flip(sends[n], n // 2)
    far = [flip(sends[d], d) for d in range(n // 2, n)]
    near = [sends[0]] + [flip(sends[d], d) for d in range(1, n // 2)]
    passed = call(
        functools.partial(pass_on_kernel, n, cap),
        "pass_on",
        pass_table,
        [whole],
        [jax.ShapeDtypeStruct((2 * cap, half, part), bf16)] * (n // 2),
        [in_vmem] * (n // 2),
    )
    passed = [passed[0]] + [flip(passed[d], d) for d in range(1, n // 2)]
    return call(
        functools.partial(gather_coulomb_kernel, n, blocks, shell, cap),
        "gather_coulomb",
        in_table,
        [*near, *far, *passed],
        [jax.ShapeDtypeStruct((blocks, pairs, half), bf16)] * 2,
        [anywhere] * 2,
        scratch=[
            pltpu.VMEM((2, blocks, half, pairs), bf16),
            pltpu.VMEM((2, blocks, pairs, half), bf16),
            pltpu.SemaphoreType.DMA((2, blocks)),
        ],
    )


def solution(mesh):
    in_specs = (
        P(("mol", "pair"), None, "aux"),
        P(("mol", "pair"), None, None),
        P(("mol", "pair"), None),
        P(("mol", "pair"), None),
        P("mol"),
        P("mol"),
    )
    out_specs = (P(("mol", "pair"), None, "aux"), P(("mol", "pair"), None, "aux"))
    return jax.shard_map(local, mesh=mesh, in_specs=in_specs, out_specs=out_specs, check_vma=False)
```

```python
import functools
import math

import jax
import jax.numpy as jnp
from jax import lax
from jax.experimental import pallas as pl
from jax.experimental.pallas import tpu as pltpu
from jax.sharding import PartitionSpec as P

VMEM_BYTES = 20 * 1024 * 1024


def tables(slots, devices, blocks_dev, me):
    total = slots.shape[0]
    numbers = jnp.arange(total, dtype=jnp.int32)
    source = numbers // blocks_dev
    target = slots // blocks_dev
    joined = source * devices + target
    earlier = (joined[:, None] == joined[None, :]) & (numbers[None, :] < numbers[:, None])
    rank = jnp.sum(earlier.astype(jnp.int32), axis=1)
    held = []
    for device in (me, me ^ (devices // 2)):
        for values in (target, rank):
            held.append(lax.dynamic_slice_in_dim(values, device * blocks_dev, blocks_dev, 0))
    rows = me * blocks_dev + jnp.arange(blocks_dev, dtype=jnp.int32)
    hot = slots[None, :] == rows[:, None]
    row_source = jnp.sum(jnp.where(hot, source[None, :], 0), axis=1)
    row_rank = jnp.sum(jnp.where(hot, rank[None, :], 0), axis=1)
    return held[:2], held[2:], (row_source, row_rank)


def slots_of(steps, ranks, devices, cap):
    held = (steps * cap + ranks)[None, :] == jnp.arange(devices * cap, dtype=jnp.int32)[:, None]
    numbers = jnp.arange(steps.shape[0], dtype=jnp.int32)
    return jnp.max(jnp.where(held, numbers[None, :], -1), axis=1)


def load_kernel(source, ready, target, sem):
    copy = pltpu.make_async_copy(source, target, sem)
    copy.start()
    copy.wait()


def scatter_density_kernel(devices, blocks, cap, table, density, *rest):
    sends, turned = rest[:devices], rest[-1]
    for row in range(blocks):
        turned[row] = density[row].T
    for step in range(devices):
        for rank in range(cap):
            row = jnp.maximum(table[step * cap + rank], 0)
            sends[step][rank] = turned[row]


def gather_density_kernel(steps, cap, table, *rest):
    out = rest[-1]
    for step, piece in zip(steps, rest):
        for rank in range(cap):
            row = table[step * cap + rank]

            @pl.when(row >= 0)
            def _():
                out[row] = piece[rank]


def fit_kernel(bits, blocks, table, factor, density, integrals, *rest):
    keep, send = rest[-2:]
    width = keep.shape[2]
    pairs = integrals.shape[1]
    fitted = jnp.concatenate([density[b] * factor[b] for b in range(blocks)], axis=1)
    for i in range(keep.shape[0]):
        e = sum(bit for j, bit in enumerate(bits[1:]) if i >> j & 1)
        for relative, out in ((e ^ bits[0], send), (e, keep)):
            at = pl.ds(pl.multiple_of(table[relative] * width, width), width)
            out[i] = jnp.dot(
                fitted,
                integrals[:, :, at].reshape(blocks * pairs, width),
                preferred_element_type=jnp.float32,
            ).astype(out.dtype)


def apply_kernel(orders, some, table, integrals, near, far, near_other, far_other, own, other):
    blocks, pairs, half = integrals.shape[0], integrals.shape[1], own.shape[1]
    count, _, width = near.shape
    chunks = []
    for order, low, high in ((orders[0], near, far), (orders[1], near_other, far_other)):
        chunks.append({e: (low, i) if i < count else (high, i - count) for i, e in enumerate(order)})
    for first in range(0, blocks, some):
        total = None
        for e in range(2 * count):
            at = pl.ds(pl.multiple_of(table[e] * width, width), width)
            term = lax.dot_general(
                integrals[first : first + some, :, at].reshape(some * pairs, width),
                jnp.concatenate([piece[e][0][piece[e][1]] for piece in chunks], axis=0),
                (((1,), (1,)), ((), ())),
                preferred_element_type=jnp.float32,
            )
            total = term if total is None else total + term
        for b in range(some):
            value = total[b * pairs : (b + 1) * pairs].T
            own[first + b] = value[:half]
            other[first + b] = value[half:].astype(other.dtype)


def scatter_coulomb_kernel(devices, blocks, cap, table, screen, own, other, *rest):
    near, far, whole, ready = rest[: devices // 2], rest[devices // 2 : devices], rest[-2], rest[-1]
    part = whole.shape[2]
    for b in range(blocks):
        value = (own[b] + other[b].astype(jnp.float32)) * screen[b]
        ready[b] = value.astype(jnp.bfloat16)
        whole[b] = ready[b, :, pl.ds(0, part)]
    for group in range(2):
        for step in range(devices):
            for rank in range(cap):
                b = jnp.maximum(table[(group * devices + step) * cap + rank], 0)
                if step < devices // 2:
                    near[step][group * cap + rank] = ready[b]
                else:
                    far[step - devices // 2][group * cap + rank] = ready[b, :, pl.ds(part, part)]


def pass_on_kernel(devices, cap, table, whole, *outs):
    for group in range(2):
        for step in range(devices // 2):
            for rank in range(cap):
                b = jnp.maximum(table[(group * devices + devices // 2 + step) * cap + rank], 0)
                outs[step][group * cap + rank] = whole[b]


def gather_coulomb_kernel(devices, blocks, shell, cap, table, *rest):
    half = devices // 2
    near, passed, far = rest[:half], rest[half:devices], rest[devices : devices + half]
    rows, cols, landed, done, sems = rest[devices + half :]
    pairs = landed.shape[3]
    part = far[0].shape[2]
    for step in range(devices):
        for group in range(2):
            for rank in range(cap):
                row = table[(group * devices + step) * cap + rank]
                at = group * cap + rank

                @pl.when(row >= 0)
                def _():
                    if step < half:
                        landed[group, row] = near[step][at]
                    else:
                        landed[group, row, :, pl.ds(0, part)] = passed[step - half][at]
                        landed[group, row, :, pl.ds(part, part)] = far[step - half][at]

    to = lax.broadcasted_iota(jnp.int32, (pairs, pairs), 0)
    source = lax.broadcasted_iota(jnp.int32, (pairs, pairs), 1)
    turns = (to, (to % shell) * shell + to // shell)
    copies = []
    for group in range(2):
        turn = (source == turns[group]).astype(jnp.bfloat16)
        for row in range(blocks):
            done[group, row] = lax.dot_general(
                turn,
                landed[group, row],
                (((1,), (1,)), ((), ())),
                preferred_element_type=jnp.float32,
            ).astype(jnp.bfloat16)
            copy = pltpu.make_async_copy(
                done.at[group, row], (rows, cols)[group].at[row], sems.at[group, row]
            )
            copy.start()
            copies.append(copy)
    for copy in copies:
        copy.wait()


def local(three_index, density, screen, pair_shells, home_slot, mirror_slot):
    blocks, pairs, aux_dev = three_index.shape
    ndens = density.shape[2]
    shell = math.isqrt(pairs)
    n = lax.axis_size("pair")
    cores = lax.axis_size("aux")
    me = lax.axis_index("pair")
    core = lax.axis_index("aux")
    half = ndens // cores
    part = pairs // 2
    width = aux_dev // n
    cap = 2 + (blocks - 1) // n
    bf16, f32 = jnp.bfloat16, jnp.float32
    in_vmem = pl.BlockSpec(memory_space=pltpu.VMEM)
    anywhere = pl.BlockSpec(memory_space=pl.ANY)
    ints = functools.partial(jnp.concatenate, axis=0)

    def call(kernel, name, table, args, out_shape, out_specs, ready=(), scratch=()):
        return pl.pallas_call(
            kernel,
            out_shape=out_shape,
            grid_spec=pltpu.PrefetchScalarGridSpec(
                num_scalar_prefetch=1,
                grid=(),
                in_specs=[in_vmem] * len(args) + [anywhere] * len(ready),
                out_specs=out_specs,
                scratch_shapes=list(scratch),
            ),
            compiler_params=pltpu.CompilerParams(vmem_limit_bytes=VMEM_BYTES),
            name=name,
        )(table, *args, *ready)

    def flip(x, bit):
        return lax.ppermute(x, "pair", [(s, s ^ bit) for s in range(n)])

    def swap(x):
        return lax.ppermute(x, "aux", [(s, (s + 1) % cores) for s in range(cores)])

    def after(x, *others):
        return lax.optimization_barrier((x, *others))[0]

    def slots(peers, ranks, device):
        return slots_of(peers ^ device, ranks, n, cap)

    home_held, home_passed, home_rows = tables(home_slot, n, blocks, me)
    send_table = ints([slots(*home_rows, me), core[None].astype(jnp.int32)])
    pick_table = slots(*home_held, me)
    chunk_table = me ^ jnp.arange(n, dtype=jnp.int32)
    weight = jnp.where(pair_shells[:, 0] != pair_shells[:, 1], 2.0, 1.0)
    factor = (screen.astype(f32) * weight[:, None]).astype(bf16)[:, None, :]
    keeping = screen.astype(f32)[:, None, :]

    sends = pl.pallas_call(
        functools.partial(scatter_density_kernel, n, blocks, cap),
        out_shape=[jax.ShapeDtypeStruct((cap, half, pairs), bf16)] * n,
        grid_spec=pltpu.PrefetchScalarGridSpec(
            num_scalar_prefetch=1,
            grid=(1,),
            in_specs=[pl.BlockSpec((blocks, pairs, half), lambda i, t: (0, 0, t[n * cap]))],
            out_specs=[pl.BlockSpec((cap, half, pairs), lambda i, t: (0, 0, 0))] * n,
            scratch_shapes=[pltpu.VMEM((blocks, half, pairs), bf16)],
        ),
        compiler_params=pltpu.CompilerParams(vmem_limit_bytes=VMEM_BYTES),
        name="scatter_density",
    )(send_table, density)
    steps = range(1, n)
    received = [flip(sends[d], d) for d in steps[:-1]]
    integrals = pl.pallas_call(
        load_kernel,
        out_shape=pltpu.VMEM((blocks, pairs, aux_dev), bf16),
        in_specs=[anywhere, anywhere],
        out_specs=in_vmem,
        scratch_shapes=[pltpu.SemaphoreType.DMA],
        compiler_params=pltpu.CompilerParams(vmem_limit_bytes=2 * 1024 * 1024),
        name="load_integrals",
    )(three_index, received[1])
    received += [flip(after(sends[steps[-1]], integrals), steps[-1]), sends[0]]
    steps = (*steps, 0)
    own = call(
        functools.partial(gather_density_kernel, steps, cap),
        "gather_density",
        pick_table,
        received,
        jax.ShapeDtypeStruct((blocks, half, pairs), bf16),
        in_vmem,
    )
    other = swap(own)

    mirror_held, mirror_passed, mirror_rows = tables(after(mirror_slot, own), n, blocks, me)
    out_table = ints([slots(*home_held, me), slots(*mirror_held, me)])
    pass_table = ints([slots(*held, me ^ (n // 2)) for held in (home_passed, mirror_passed)])
    in_table = ints([slots(*home_rows, me), slots(*mirror_rows, me)])

    bits = [1 << j for j in range(n.bit_length() - 1)]
    orders = (bits[1::-1] + bits[2:], bits)

    def fit(value, bits, ready=()):
        return call(
            functools.partial(fit_kernel, bits, blocks),
            "fit",
            chunk_table,
            [factor, value, integrals],
            [
                jax.ShapeDtypeStruct((n // 2, half, width), f32),
                jax.ShapeDtypeStruct((n // 2, half, width), bf16),
            ],
            [in_vmem] * 2,
            ready,
        )

    def step_together(states):
        flat, tree = jax.tree.flatten(states)
        return jax.tree.unflatten(tree, lax.optimization_barrier(flat))

    def totals(states):
        for j in range(len(bits)):
            states = step_together(states)
            found = []
            for (keep, send), order in zip(states, orders):
                value = keep + flip(send, order[j]).astype(f32)
                if j < len(bits) - 1:
                    found.append((value[0::2], value[1::2].astype(bf16)))
                else:
                    found.append(value.astype(bf16))
            states = found
        relative = [[0] for _ in orders]
        for j in reversed(range(len(bits))):
            states = step_together(states)
            fars = [flip(near, order[j]) for near, order in zip(states, orders)]
            relative = [r + [e ^ order[j] for e in r] for r, order in zip(relative, orders)]
            if j == 0:
                return [(*pair, r) for pair, r in zip(zip(states, fars), relative)]
            states = [jnp.concatenate(pair, axis=0) for pair in zip(states, fars)]

    fit_own = fit(own, orders[1])
    fit_other = fit(other, orders[0], fit_own[:1])
    (near_other, far_other, order_other), (near_own, far_own, order_own) = totals(
        [tuple(fit_other), tuple(fit_own)]
    )

    mine, theirs = call(
        functools.partial(apply_kernel, (order_own, order_other), blocks // 2),
        "apply",
        chunk_table,
        [integrals, near_own, far_own, near_other, far_other],
        [
            jax.ShapeDtypeStruct((blocks, half, pairs), f32),
            jax.ShapeDtypeStruct((blocks, half, pairs), bf16),
        ],
        [in_vmem] * 2,
    )
    sends = call(
        functools.partial(scatter_coulomb_kernel, n, blocks, cap),
        "scatter_coulomb",
        out_table,
        [keeping, mine, swap(theirs)],
        [jax.ShapeDtypeStruct((2 * cap, half, pairs), bf16)] * (n // 2)
        + [jax.ShapeDtypeStruct((2 * cap, half, part), bf16)] * (n // 2)
        + [jax.ShapeDtypeStruct((blocks, half, part), bf16)],
        [in_vmem] * (n + 1),
        scratch=[pltpu.VMEM((blocks, half, pairs), bf16)],
    )
    whole = flip(sends[n], n // 2)
    near = [sends[0]] + [flip(sends[d], d) for d in range(1, n // 2)]
    passed = call(
        functools.partial(pass_on_kernel, n, cap),
        "pass_on",
        pass_table,
        [whole],
        [jax.ShapeDtypeStruct((2 * cap, half, part), bf16)] * (n // 2),
        [in_vmem] * (n // 2),
    )
    passed = [passed[0]] + [flip(passed[d], d) for d in range(1, n // 2)]
    far = [flip(sends[n // 2], n // 2)]
    for i in range(1, n // 2):
        far.append(flip(after(sends[n // 2 + i], near[1] if i == 1 else passed[i - 1]), n // 2 + i))
    return call(
        functools.partial(gather_coulomb_kernel, n, blocks, shell, cap),
        "gather_coulomb",
        in_table,
        [*near, *passed, *far],
        [jax.ShapeDtypeStruct((blocks, pairs, half), bf16)] * 2,
        [anywhere] * 2,
        scratch=[
            pltpu.VMEM((2, blocks, half, pairs), bf16),
            pltpu.VMEM((2, blocks, pairs, half), bf16),
            pltpu.SemaphoreType.DMA((2, blocks)),
        ],
    )


def solution(mesh):
    in_specs = (
        P(("mol", "pair"), None, "aux"),
        P(("mol", "pair"), None, None),
        P(("mol", "pair"), None),
        P(("mol", "pair"), None),
        P("mol"),
        P("mol"),
    )
    out_specs = (P(("mol", "pair"), None, "aux"), P(("mol", "pair"), None, "aux"))
    return jax.shard_map(local, mesh=mesh, in_specs=in_specs, out_specs=out_specs, check_vma=False)
```

```python
import functools
import math

import jax
import jax.numpy as jnp
from jax import lax
from jax.experimental import pallas as pl
from jax.experimental.pallas import tpu as pltpu
from jax.sharding import PartitionSpec as P

VMEM_BYTES = 20 * 1024 * 1024


def tables(slots, devices, blocks_dev, me):
    total = slots.shape[0]
    numbers = jnp.arange(total, dtype=jnp.int32)
    source = numbers // blocks_dev
    target = slots // blocks_dev
    joined = source * devices + target
    earlier = (joined[:, None] == joined[None, :]) & (numbers[None, :] < numbers[:, None])
    rank = jnp.sum(earlier.astype(jnp.int32), axis=1)
    held = []
    for device in (me, me ^ (devices // 2)):
        for values in (target, rank):
            held.append(lax.dynamic_slice_in_dim(values, device * blocks_dev, blocks_dev, 0))
    rows = me * blocks_dev + jnp.arange(blocks_dev, dtype=jnp.int32)
    hot = slots[None, :] == rows[:, None]
    row_source = jnp.sum(jnp.where(hot, source[None, :], 0), axis=1)
    row_rank = jnp.sum(jnp.where(hot, rank[None, :], 0), axis=1)
    return held[:2], held[2:], (row_source, row_rank)


def slots_of(steps, ranks, devices, cap):
    held = (steps * cap + ranks)[None, :] == jnp.arange(devices * cap, dtype=jnp.int32)[:, None]
    numbers = jnp.arange(steps.shape[0], dtype=jnp.int32)
    return jnp.max(jnp.where(held, numbers[None, :], -1), axis=1)


def load_kernel(source, ready, target, sem):
    copy = pltpu.make_async_copy(source, target, sem)
    copy.start()
    copy.wait()


def scatter_density_kernel(devices, blocks, cap, table, density, *rest):
    sends, turned = rest[:devices], rest[-1]
    for row in range(blocks):
        turned[row] = density[row].T
    for step in range(devices):
        for rank in range(cap):
            row = jnp.maximum(table[step * cap + rank], 0)
            sends[step][rank] = turned[row]


def gather_density_kernel(steps, cap, table, *rest):
    out = rest[-1]
    for step, piece in zip(steps, rest):
        for rank in range(cap):
            row = table[step * cap + rank]

            @pl.when(row >= 0)
            def _():
                out[row] = piece[rank]


def fit_kernel(bits, blocks, table, factor, density, integrals, *rest):
    keep, send = rest[-2:]
    width = keep.shape[2]
    pairs = integrals.shape[1]
    fitted = jnp.concatenate([density[b] * factor[b] for b in range(blocks)], axis=1)
    for i in range(keep.shape[0]):
        e = sum(bit for j, bit in enumerate(bits[1:]) if i >> j & 1)
        for relative, out in ((e ^ bits[0], send), (e, keep)):
            at = pl.ds(pl.multiple_of(table[relative] * width, width), width)
            out[i] = jnp.dot(
                fitted,
                integrals[:, :, at].reshape(blocks * pairs, width),
                preferred_element_type=jnp.float32,
            ).astype(out.dtype)


def apply_kernel(orders, some, table, integrals, near, far, near_other, far_other, own, other):
    blocks, pairs, half = integrals.shape[0], integrals.shape[1], own.shape[1]
    count, _, width = near.shape
    chunks = []
    for order, low, high in ((orders[0], near, far), (orders[1], near_other, far_other)):
        chunks.append({e: (low, i) if i < count else (high, i - count) for i, e in enumerate(order)})
    for first in range(0, blocks, some):
        total = None
        for e in range(2 * count):
            at = pl.ds(pl.multiple_of(table[e] * width, width), width)
            term = lax.dot_general(
                integrals[first : first + some, :, at].reshape(some * pairs, width),
                jnp.concatenate([piece[e][0][piece[e][1]] for piece in chunks], axis=0),
                (((1,), (1,)), ((), ())),
                preferred_element_type=jnp.float32,
            )
            total = term if total is None else total + term
        for b in range(some):
            value = total[b * pairs : (b + 1) * pairs].T
            own[first + b] = value[:half]
            other[first + b] = value[half:].astype(other.dtype)


def scatter_coulomb_kernel(devices, blocks, cap, table, screen, own, other, *rest):
    near, far, whole, ready = rest[: devices // 2], rest[devices // 2 : devices], rest[-2], rest[-1]
    part = whole.shape[2]
    for b in range(blocks):
        value = (own[b] + other[b].astype(jnp.float32)) * screen[b]
        ready[b] = value.astype(jnp.bfloat16)
        whole[b] = ready[b, :, pl.ds(0, part)]
    for group in range(2):
        for step in range(devices):
            for rank in range(cap):
                b = jnp.maximum(table[(group * devices + step) * cap + rank], 0)
                if step < devices // 2:
                    near[step][group * cap + rank] = ready[b]
                else:
                    far[step - devices // 2][group * cap + rank] = ready[b, :, pl.ds(part, part)]


def pass_on_kernel(devices, cap, table, whole, *rest):
    outs = rest[-(devices // 2) :]
    for group in range(2):
        for step in range(devices // 2):
            for rank in range(cap):
                b = jnp.maximum(table[(group * devices + devices // 2 + step) * cap + rank], 0)
                outs[step][group * cap + rank] = whole[b]


def gather_coulomb_kernel(devices, blocks, shell, cap, table, *rest):
    half = devices // 2
    near, passed, far = rest[:half], rest[half:devices], rest[devices : devices + half]
    rows, cols, landed, done, sems = rest[devices + half :]
    pairs = landed.shape[3]
    part = far[0].shape[2]
    for step in range(devices):
        for group in range(2):
            for rank in range(cap):
                row = table[(group * devices + step) * cap + rank]
                at = group * cap + rank

                @pl.when(row >= 0)
                def _():
                    if step < half:
                        landed[group, row] = near[step][at]
                    else:
                        landed[group, row, :, pl.ds(0, part)] = passed[step - half][at]
                        landed[group, row, :, pl.ds(part, part)] = far[step - half][at]

    to = lax.broadcasted_iota(jnp.int32, (pairs, pairs), 0)
    source = lax.broadcasted_iota(jnp.int32, (pairs, pairs), 1)
    turns = (to, (to % shell) * shell + to // shell)
    copies = []
    for group in range(2):
        turn = (source == turns[group]).astype(jnp.bfloat16)
        for row in range(blocks):
            done[group, row] = lax.dot_general(
                turn,
                landed[group, row],
                (((1,), (1,)), ((), ())),
                preferred_element_type=jnp.float32,
            ).astype(jnp.bfloat16)
            copy = pltpu.make_async_copy(
                done.at[group, row], (rows, cols)[group].at[row], sems.at[group, row]
            )
            copy.start()
            copies.append(copy)
    for copy in copies:
        copy.wait()


def local(three_index, density, screen, pair_shells, home_slot, mirror_slot):
    blocks, pairs, aux_dev = three_index.shape
    ndens = density.shape[2]
    shell = math.isqrt(pairs)
    n = lax.axis_size("pair")
    cores = lax.axis_size("aux")
    me = lax.axis_index("pair")
    core = lax.axis_index("aux")
    half = ndens // cores
    part = pairs // 2
    width = aux_dev // n
    cap = 2 + (blocks - 1) // n
    bf16, f32 = jnp.bfloat16, jnp.float32
    in_vmem = pl.BlockSpec(memory_space=pltpu.VMEM)
    anywhere = pl.BlockSpec(memory_space=pl.ANY)
    ints = functools.partial(jnp.concatenate, axis=0)

    def call(kernel, name, table, args, out_shape, out_specs, ready=(), scratch=()):
        return pl.pallas_call(
            kernel,
            out_shape=out_shape,
            grid_spec=pltpu.PrefetchScalarGridSpec(
                num_scalar_prefetch=1,
                grid=(),
                in_specs=[in_vmem] * len(args) + [anywhere] * len(ready),
                out_specs=out_specs,
                scratch_shapes=list(scratch),
            ),
            compiler_params=pltpu.CompilerParams(vmem_limit_bytes=VMEM_BYTES),
            name=name,
        )(table, *args, *ready)

    def flip(x, bit):
        return lax.ppermute(x, "pair", [(s, s ^ bit) for s in range(n)])

    def swap(x):
        return lax.ppermute(x, "aux", [(s, (s + 1) % cores) for s in range(cores)])

    def after(x, *others):
        return lax.optimization_barrier((x, *others))[0]

    def slots(peers, ranks, device):
        return slots_of(peers ^ device, ranks, n, cap)

    home_held, home_passed, home_rows = tables(home_slot, n, blocks, me)
    send_table = ints([slots(*home_rows, me), core[None].astype(jnp.int32)])
    pick_table = slots(*home_held, me)
    chunk_table = me ^ jnp.arange(n, dtype=jnp.int32)
    weight = jnp.where(pair_shells[:, 0] != pair_shells[:, 1], 2.0, 1.0)
    factor = (screen.astype(f32) * weight[:, None]).astype(bf16)[:, None, :]
    keeping = screen.astype(f32)[:, None, :]

    sends = pl.pallas_call(
        functools.partial(scatter_density_kernel, n, blocks, cap),
        out_shape=[jax.ShapeDtypeStruct((cap, half, pairs), bf16)] * n,
        grid_spec=pltpu.PrefetchScalarGridSpec(
            num_scalar_prefetch=1,
            grid=(1,),
            in_specs=[pl.BlockSpec((blocks, pairs, half), lambda i, t: (0, 0, t[n * cap]))],
            out_specs=[pl.BlockSpec((cap, half, pairs), lambda i, t: (0, 0, 0))] * n,
            scratch_shapes=[pltpu.VMEM((blocks, half, pairs), bf16)],
        ),
        compiler_params=pltpu.CompilerParams(vmem_limit_bytes=VMEM_BYTES),
        name="scatter_density",
    )(send_table, density)
    steps = [n // 2, n // 2 + 1, *range(1, n // 2), *range(n // 2 + 2, n)]
    received = []
    for i, d in enumerate(steps[:-1]):
        send = sends[d]
        if d > n // 2 + 1:
            send = after(send, received[i - n // 2 + 1])
        received.append(flip(send, d))
    integrals = pl.pallas_call(
        load_kernel,
        out_shape=pltpu.VMEM((blocks, pairs, aux_dev), bf16),
        in_specs=[anywhere, anywhere],
        out_specs=in_vmem,
        scratch_shapes=[pltpu.SemaphoreType.DMA],
        compiler_params=pltpu.CompilerParams(vmem_limit_bytes=2 * 1024 * 1024),
        name="load_integrals",
    )(three_index, received[2])
    received += [flip(after(sends[steps[-1]], received[3], integrals), steps[-1]), sends[0]]
    steps = (*steps, 0)
    own = call(
        functools.partial(gather_density_kernel, steps, cap),
        "gather_density",
        pick_table,
        received,
        jax.ShapeDtypeStruct((blocks, half, pairs), bf16),
        in_vmem,
    )
    other = swap(own)

    mirror_held, mirror_passed, mirror_rows = tables(after(mirror_slot, own), n, blocks, me)
    out_table = ints([slots(*home_held, me), slots(*mirror_held, me)])
    pass_table = ints([slots(*held, me ^ (n // 2)) for held in (home_passed, mirror_passed)])
    in_table = ints([slots(*home_rows, me), slots(*mirror_rows, me)])

    bits = [1 << j for j in range(n.bit_length() - 1)]
    orders = (bits[1::-1] + bits[2:], bits)

    def fit(value, bits, ready=()):
        return call(
            functools.partial(fit_kernel, bits, blocks),
            "fit",
            chunk_table,
            [factor, value, integrals],
            [
                jax.ShapeDtypeStruct((n // 2, half, width), f32),
                jax.ShapeDtypeStruct((n // 2, half, width), bf16),
            ],
            [in_vmem] * 2,
            ready,
        )

    def step_together(states):
        flat, tree = jax.tree.flatten(states)
        return jax.tree.unflatten(tree, lax.optimization_barrier(flat))

    def totals(states):
        for j in range(len(bits)):
            states = step_together(states)
            found = []
            for (keep, send), order in zip(states, orders):
                value = keep + flip(send, order[j]).astype(f32)
                if j < len(bits) - 1:
                    found.append((value[0::2], value[1::2].astype(bf16)))
                else:
                    found.append(value.astype(bf16))
            states = found
        relative = [[0] for _ in orders]
        for j in reversed(range(len(bits))):
            states = step_together(states)
            fars = [flip(near, order[j]) for near, order in zip(states, orders)]
            relative = [r + [e ^ order[j] for e in r] for r, order in zip(relative, orders)]
            if j == 0:
                return [(*pair, r) for pair, r in zip(zip(states, fars), relative)]
            states = [jnp.concatenate(pair, axis=0) for pair in zip(states, fars)]

    fit_own = fit(own, orders[1])
    fit_other = fit(other, orders[0], fit_own[:1])
    (near_other, far_other, order_other), (near_own, far_own, order_own) = totals(
        [tuple(fit_other), tuple(fit_own)]
    )

    mine, theirs = call(
        functools.partial(apply_kernel, (order_own, order_other), blocks // 2),
        "apply",
        chunk_table,
        [integrals, near_own, far_own, near_other, far_other],
        [
            jax.ShapeDtypeStruct((blocks, half, pairs), f32),
            jax.ShapeDtypeStruct((blocks, half, pairs), bf16),
        ],
        [in_vmem] * 2,
    )
    sends = call(
        functools.partial(scatter_coulomb_kernel, n, blocks, cap),
        "scatter_coulomb",
        out_table,
        [keeping, mine, swap(theirs)],
        [jax.ShapeDtypeStruct((2 * cap, half, pairs), bf16)] * (n // 2)
        + [jax.ShapeDtypeStruct((2 * cap, half, part), bf16)] * (n // 2)
        + [jax.ShapeDtypeStruct((blocks, half, part), bf16)],
        [in_vmem] * (n + 1),
        scratch=[pltpu.VMEM((blocks, half, pairs), bf16)],
    )
    def direct(i, ready):
        return flip(after(sends[n // 2 + i], ready), n // 2 + i)

    whole = flip(sends[n], n // 2)
    near = [sends[0]] + [flip(sends[d], d) for d in range(1, n // 2)]
    far = [direct(0, sends[0])]
    for i in range(1, 3):
        far.append(direct(i, far[i - 1]))
    passed = call(
        functools.partial(pass_on_kernel, n, cap),
        "pass_on",
        pass_table,
        [whole],
        [jax.ShapeDtypeStruct((2 * cap, half, part), bf16)] * (n // 2),
        [in_vmem] * (n // 2),
        far[1:2],
    )
    passed = [passed[0]] + [flip(passed[d], d) for d in range(1, n // 2)]
    for i in range(3, n // 2):
        far.append(direct(i, passed[i - 2]))
    return call(
        functools.partial(gather_coulomb_kernel, n, blocks, shell, cap),
        "gather_coulomb",
        in_table,
        [*near, *passed, *far],
        [jax.ShapeDtypeStruct((blocks, pairs, half), bf16)] * 2,
        [anywhere] * 2,
        scratch=[
            pltpu.VMEM((2, blocks, half, pairs), bf16),
            pltpu.VMEM((2, blocks, pairs, half), bf16),
            pltpu.SemaphoreType.DMA((2, blocks)),
        ],
    )


def solution(mesh):
    in_specs = (
        P(("mol", "pair"), None, "aux"),
        P(("mol", "pair"), None, None),
        P(("mol", "pair"), None),
        P(("mol", "pair"), None),
        P("mol"),
        P("mol"),
    )
    out_specs = (P(("mol", "pair"), None, "aux"), P(("mol", "pair"), None, "aux"))
    return jax.shard_map(local, mesh=mesh, in_specs=in_specs, out_specs=out_specs, check_vma=False)
```

```python
import functools
import math

import jax
import jax.numpy as jnp
from jax import lax
from jax.experimental import pallas as pl
from jax.experimental.pallas import tpu as pltpu
from jax.sharding import PartitionSpec as P

VMEM_BYTES = 20 * 1024 * 1024


def tables(slots, devices, blocks_dev, me):
    total = slots.shape[0]
    numbers = jnp.arange(total, dtype=jnp.int32)
    source = numbers // blocks_dev
    target = slots // blocks_dev
    joined = source * devices + target
    earlier = (joined[:, None] == joined[None, :]) & (numbers[None, :] < numbers[:, None])
    rank = jnp.sum(earlier.astype(jnp.int32), axis=1)
    held = []
    for device in (me, me ^ (devices // 2)):
        for values in (target, rank):
            held.append(lax.dynamic_slice_in_dim(values, device * blocks_dev, blocks_dev, 0))
    rows = me * blocks_dev + jnp.arange(blocks_dev, dtype=jnp.int32)
    hot = slots[None, :] == rows[:, None]
    row_source = jnp.sum(jnp.where(hot, source[None, :], 0), axis=1)
    row_rank = jnp.sum(jnp.where(hot, rank[None, :], 0), axis=1)
    return held[:2], held[2:], (row_source, row_rank)


def slots_of(steps, ranks, devices, cap):
    held = (steps * cap + ranks)[None, :] == jnp.arange(devices * cap, dtype=jnp.int32)[:, None]
    numbers = jnp.arange(steps.shape[0], dtype=jnp.int32)
    return jnp.max(jnp.where(held, numbers[None, :], -1), axis=1)


def load_kernel(source, ready, target, sem):
    copy = pltpu.make_async_copy(source, target, sem)
    copy.start()
    copy.wait()


def scatter_density_kernel(devices, blocks, cap, table, density, *rest):
    sends, turned = rest[:devices], rest[-1]
    for row in range(blocks):
        turned[row] = density[row].T
    for step in range(devices):
        for rank in range(cap):
            row = jnp.maximum(table[step * cap + rank], 0)
            sends[step][rank] = turned[row]


def gather_density_kernel(steps, cap, table, *rest):
    out = rest[-1]
    for step, piece in zip(steps, rest):
        for rank in range(cap):
            row = table[step * cap + rank]

            @pl.when(row >= 0)
            def _():
                out[row] = piece[rank]


def fit_kernel(bits, blocks, table, factor, density, integrals, *rest):
    keep, send = rest[-2:]
    width = keep.shape[2]
    pairs = integrals.shape[1]
    fitted = jnp.concatenate([density[b] * factor[b] for b in range(blocks)], axis=1)
    for i in range(keep.shape[0]):
        e = sum(bit for j, bit in enumerate(bits[1:]) if i >> j & 1)
        for relative, out in ((e ^ bits[0], send), (e, keep)):
            at = pl.ds(pl.multiple_of(table[relative] * width, width), width)
            out[i] = jnp.dot(
                fitted,
                integrals[:, :, at].reshape(blocks * pairs, width),
                preferred_element_type=jnp.float32,
            ).astype(out.dtype)


def apply_kernel(orders, some, table, integrals, near, far, near_other, far_other, own, other):
    blocks, pairs, half = integrals.shape[0], integrals.shape[1], own.shape[1]
    count, _, width = near.shape
    chunks = []
    for order, low, high in ((orders[0], near, far), (orders[1], near_other, far_other)):
        chunks.append({e: (low, i) if i < count else (high, i - count) for i, e in enumerate(order)})
    for first in range(0, blocks, some):
        total = None
        for e in range(2 * count):
            at = pl.ds(pl.multiple_of(table[e] * width, width), width)
            term = lax.dot_general(
                integrals[first : first + some, :, at].reshape(some * pairs, width),
                jnp.concatenate([piece[e][0][piece[e][1]] for piece in chunks], axis=0),
                (((1,), (1,)), ((), ())),
                preferred_element_type=jnp.float32,
            )
            total = term if total is None else total + term
        for b in range(some):
            value = total[b * pairs : (b + 1) * pairs].T
            own[first + b] = value[:half]
            other[first + b] = value[half:].astype(other.dtype)


def scatter_coulomb_kernel(devices, blocks, cap, table, screen, own, other, *rest):
    near, far, whole, ready = rest[: devices // 2], rest[devices // 2 : devices], rest[-2], rest[-1]
    part = whole.shape[2]
    for b in range(blocks):
        value = (own[b] + other[b].astype(jnp.float32)) * screen[b]
        ready[b] = value.astype(jnp.bfloat16)
        whole[b] = ready[b, :, pl.ds(0, part)]
    for group in range(2):
        for step in range(devices):
            for rank in range(cap):
                b = jnp.maximum(table[(group * devices + step) * cap + rank], 0)
                if step < devices // 2:
                    near[step][group * cap + rank] = ready[b]
                else:
                    far[step - devices // 2][group * cap + rank] = ready[b, :, pl.ds(part, part)]


def pass_on_kernel(devices, cap, table, whole, *rest):
    outs = rest[-(devices // 2) :]
    for group in range(2):
        for step in range(devices // 2):
            for rank in range(cap):
                b = jnp.maximum(table[(group * devices + devices // 2 + step) * cap + rank], 0)
                outs[step][group * cap + rank] = whole[b]


def gather_coulomb_kernel(devices, blocks, shell, cap, table, *rest):
    half = devices // 2
    near, passed, far = rest[:half], rest[half:devices], rest[devices : devices + half]
    rows, cols, landed, done, sems = rest[devices + half :]
    pairs = landed.shape[3]
    part = far[0].shape[2]
    for step in range(devices):
        for group in range(2):
            for rank in range(cap):
                row = table[(group * devices + step) * cap + rank]
                at = group * cap + rank

                @pl.when(row >= 0)
                def _():
                    if step < half:
                        landed[group, row] = near[step][at]
                    else:
                        landed[group, row, :, pl.ds(0, part)] = passed[step - half][at]
                        landed[group, row, :, pl.ds(part, part)] = far[step - half][at]

    to = lax.broadcasted_iota(jnp.int32, (pairs, pairs), 0)
    source = lax.broadcasted_iota(jnp.int32, (pairs, pairs), 1)
    turns = (to, (to % shell) * shell + to // shell)
    copies = []
    for group in range(2):
        turn = (source == turns[group]).astype(jnp.bfloat16)
        for row in range(blocks):
            done[group, row] = lax.dot_general(
                turn,
                landed[group, row],
                (((1,), (1,)), ((), ())),
                preferred_element_type=jnp.float32,
            ).astype(jnp.bfloat16)
            copy = pltpu.make_async_copy(
                done.at[group, row], (rows, cols)[group].at[row], sems.at[group, row]
            )
            copy.start()
            copies.append(copy)
    for copy in copies:
        copy.wait()


def local(three_index, density, screen, pair_shells, home_slot, mirror_slot):
    blocks, pairs, aux_dev = three_index.shape
    ndens = density.shape[2]
    shell = math.isqrt(pairs)
    n = lax.axis_size("pair")
    cores = lax.axis_size("aux")
    me = lax.axis_index("pair")
    core = lax.axis_index("aux")
    half = ndens // cores
    part = pairs // 2
    width = aux_dev // n
    cap = 2 + (blocks - 1) // n
    bf16, f32 = jnp.bfloat16, jnp.float32
    in_vmem = pl.BlockSpec(memory_space=pltpu.VMEM)
    anywhere = pl.BlockSpec(memory_space=pl.ANY)
    ints = functools.partial(jnp.concatenate, axis=0)

    def call(kernel, name, table, args, out_shape, out_specs, ready=(), scratch=()):
        return pl.pallas_call(
            kernel,
            out_shape=out_shape,
            grid_spec=pltpu.PrefetchScalarGridSpec(
                num_scalar_prefetch=1,
                grid=(),
                in_specs=[in_vmem] * len(args) + [anywhere] * len(ready),
                out_specs=out_specs,
                scratch_shapes=list(scratch),
            ),
            compiler_params=pltpu.CompilerParams(vmem_limit_bytes=VMEM_BYTES),
            name=name,
        )(table, *args, *ready)

    def shift(x, d):
        return lax.ppermute(x, "pair", [(s, (s + d) % n) for s in range(n)])

    def flip(x, bit):
        return lax.ppermute(x, "pair", [(s, s ^ bit) for s in range(n)])

    def swap(x):
        return lax.ppermute(x, "aux", [(s, (s + 1) % cores) for s in range(cores)])

    def after(x, *others):
        return lax.optimization_barrier((x, *others))[0]

    def slots(peers, ranks, device):
        return slots_of(peers ^ device, ranks, n, cap)

    home_held, home_passed, home_rows = tables(home_slot, n, blocks, me)
    send_table = ints(
        [slots_of((home_rows[0] - me) % n, home_rows[1], n, cap), core[None].astype(jnp.int32)]
    )
    pick_table = slots_of((me - home_held[0]) % n, home_held[1], n, cap)
    chunk_table = me ^ jnp.arange(n, dtype=jnp.int32)
    weight = jnp.where(pair_shells[:, 0] != pair_shells[:, 1], 2.0, 1.0)
    factor = (screen.astype(f32) * weight[:, None]).astype(bf16)[:, None, :]
    keeping = screen.astype(f32)[:, None, :]

    sends = pl.pallas_call(
        functools.partial(scatter_density_kernel, n, blocks, cap),
        out_shape=[jax.ShapeDtypeStruct((cap, half, pairs), bf16)] * n,
        grid_spec=pltpu.PrefetchScalarGridSpec(
            num_scalar_prefetch=1,
            grid=(1,),
            in_specs=[pl.BlockSpec((blocks, pairs, half), lambda i, t: (0, 0, t[n * cap]))],
            out_specs=[pl.BlockSpec((cap, half, pairs), lambda i, t: (0, 0, 0))] * n,
            scratch_shapes=[pltpu.VMEM((blocks, half, pairs), bf16)],
        ),
        compiler_params=pltpu.CompilerParams(vmem_limit_bytes=VMEM_BYTES),
        name="scatter_density",
    )(send_table, density)
    steps = sorted(range(1, n), key=lambda d: abs(2 * d - n))
    received = [shift(sends[d], d) for d in steps[:-1]]
    integrals = pl.pallas_call(
        load_kernel,
        out_shape=pltpu.VMEM((blocks, pairs, aux_dev), bf16),
        in_specs=[anywhere, anywhere],
        out_specs=in_vmem,
        scratch_shapes=[pltpu.SemaphoreType.DMA],
        compiler_params=pltpu.CompilerParams(vmem_limit_bytes=2 * 1024 * 1024),
        name="load_integrals",
    )(three_index, received[0])
    received += [shift(after(sends[steps[-1]], integrals), steps[-1]), sends[0]]
    steps = (*steps, 0)
    own = call(
        functools.partial(gather_density_kernel, steps, cap),
        "gather_density",
        pick_table,
        received,
        jax.ShapeDtypeStruct((blocks, half, pairs), bf16),
        in_vmem,
    )
    other = swap(own)

    mirror_held, mirror_passed, mirror_rows = tables(after(mirror_slot, own), n, blocks, me)
    out_table = ints([slots(*home_held, me), slots(*mirror_held, me)])
    pass_table = ints([slots(*held, me ^ (n // 2)) for held in (home_passed, mirror_passed)])
    in_table = ints([slots(*home_rows, me), slots(*mirror_rows, me)])

    bits = [1 << j for j in range(n.bit_length() - 1)]
    orders = (bits[1::-1] + bits[2:], bits)

    def fit(value, bits, ready=()):
        return call(
            functools.partial(fit_kernel, bits, blocks),
            "fit",
            chunk_table,
            [factor, value, integrals],
            [
                jax.ShapeDtypeStruct((n // 2, half, width), f32),
                jax.ShapeDtypeStruct((n // 2, half, width), bf16),
            ],
            [in_vmem] * 2,
            ready,
        )

    def step_together(states):
        flat, tree = jax.tree.flatten(states)
        return jax.tree.unflatten(tree, lax.optimization_barrier(flat))

    def totals(states):
        for j in range(len(bits)):
            states = step_together(states)
            found = []
            for (keep, send), order in zip(states, orders):
                value = keep + flip(send, order[j]).astype(f32)
                if j < len(bits) - 1:
                    found.append((value[0::2], value[1::2].astype(bf16)))
                else:
                    found.append(value.astype(bf16))
            states = found
        relative = [[0] for _ in orders]
        for j in reversed(range(len(bits))):
            states = step_together(states)
            fars = [flip(near, order[j]) for near, order in zip(states, orders)]
            relative = [r + [e ^ order[j] for e in r] for r, order in zip(relative, orders)]
            if j == 0:
                return [(*pair, r) for pair, r in zip(zip(states, fars), relative)]
            states = [jnp.concatenate(pair, axis=0) for pair in zip(states, fars)]

    fit_own = fit(own, orders[1])
    fit_other = fit(other, orders[0], fit_own[:1])
    (near_other, far_other, order_other), (near_own, far_own, order_own) = totals(
        [tuple(fit_other), tuple(fit_own)]
    )

    mine, theirs = call(
        functools.partial(apply_kernel, (order_own, order_other), blocks // 2),
        "apply",
        chunk_table,
        [integrals, near_own, far_own, near_other, far_other],
        [
            jax.ShapeDtypeStruct((blocks, half, pairs), f32),
            jax.ShapeDtypeStruct((blocks, half, pairs), bf16),
        ],
        [in_vmem] * 2,
    )
    sends = call(
        functools.partial(scatter_coulomb_kernel, n, blocks, cap),
        "scatter_coulomb",
        out_table,
        [keeping, mine, swap(theirs)],
        [jax.ShapeDtypeStruct((2 * cap, half, pairs), bf16)] * (n // 2)
        + [jax.ShapeDtypeStruct((2 * cap, half, part), bf16)] * (n // 2)
        + [jax.ShapeDtypeStruct((blocks, half, part), bf16)],
        [in_vmem] * (n + 1),
        scratch=[pltpu.VMEM((blocks, half, pairs), bf16)],
    )
    def direct(i, *ready):
        return flip(after(sends[n // 2 + i], *ready), n // 2 + i)

    whole = flip(sends[n], n // 2)
    near = [sends[0]] + [flip(sends[d], d) for d in range(1, n // 2)]
    far = [direct(0), direct(1, near[1]), direct(2, near[2])]
    passed = call(
        functools.partial(pass_on_kernel, n, cap),
        "pass_on",
        pass_table,
        [whole],
        [jax.ShapeDtypeStruct((2 * cap, half, part), bf16)] * (n // 2),
        [in_vmem] * (n // 2),
        near[1:],
    )
    passed = [passed[0]] + [flip(passed[d], d) for d in range(1, n // 2)]
    for i in range(3, n // 2):
        far.append(direct(i, passed[i - 2]))
    return call(
        functools.partial(gather_coulomb_kernel, n, blocks, shell, cap),
        "gather_coulomb",
        in_table,
        [*near, *passed, *far],
        [jax.ShapeDtypeStruct((blocks, pairs, half), bf16)] * 2,
        [anywhere] * 2,
        scratch=[
            pltpu.VMEM((2, blocks, half, pairs), bf16),
            pltpu.VMEM((2, blocks, pairs, half), bf16),
            pltpu.SemaphoreType.DMA((2, blocks)),
        ],
    )


def solution(mesh):
    in_specs = (
        P(("mol", "pair"), None, "aux"),
        P(("mol", "pair"), None, None),
        P(("mol", "pair"), None),
        P(("mol", "pair"), None),
        P("mol"),
        P("mol"),
    )
    out_specs = (P(("mol", "pair"), None, "aux"), P(("mol", "pair"), None, "aux"))
    return jax.shard_map(local, mesh=mesh, in_specs=in_specs, out_specs=out_specs, check_vma=False)
```

```python
import functools
import math

import jax
import jax.numpy as jnp
from jax import lax
from jax.experimental import pallas as pl
from jax.experimental.pallas import tpu as pltpu
from jax.sharding import PartitionSpec as P

VMEM_BYTES = 20 * 1024 * 1024


def tables(slots, devices, blocks_dev, me):
    total = slots.shape[0]
    numbers = jnp.arange(total, dtype=jnp.int32)
    source = numbers // blocks_dev
    target = slots // blocks_dev
    joined = source * devices + target
    earlier = (joined[:, None] == joined[None, :]) & (numbers[None, :] < numbers[:, None])
    rank = jnp.sum(earlier.astype(jnp.int32), axis=1)
    held = []
    for device in (me, me ^ (devices // 2)):
        for values in (target, rank):
            held.append(lax.dynamic_slice_in_dim(values, device * blocks_dev, blocks_dev, 0))
    rows = me * blocks_dev + jnp.arange(blocks_dev, dtype=jnp.int32)
    hot = slots[None, :] == rows[:, None]
    row_source = jnp.sum(jnp.where(hot, source[None, :], 0), axis=1)
    row_rank = jnp.sum(jnp.where(hot, rank[None, :], 0), axis=1)
    return held[:2], held[2:], (row_source, row_rank)


def slots_of(steps, ranks, devices, cap):
    held = (steps * cap + ranks)[None, :] == jnp.arange(devices * cap, dtype=jnp.int32)[:, None]
    numbers = jnp.arange(steps.shape[0], dtype=jnp.int32)
    return jnp.max(jnp.where(held, numbers[None, :], -1), axis=1)


def load_kernel(source, ready, target, sem):
    copy = pltpu.make_async_copy(source, target, sem)
    copy.start()
    copy.wait()


def scatter_density_kernel(devices, blocks, cap, table, density, *rest):
    sends, turned = rest[:devices], rest[-1]
    for row in range(blocks):
        turned[row] = density[row].T
    for step in range(devices):
        for rank in range(cap):
            row = jnp.maximum(table[step * cap + rank], 0)
            sends[step][rank] = turned[row]


def gather_density_kernel(steps, cap, table, *rest):
    out = rest[-1]
    for step, piece in zip(steps, rest):
        for rank in range(cap):
            row = table[step * cap + rank]

            @pl.when(row >= 0)
            def _():
                out[row] = piece[rank]


def fit_kernel(bits, blocks, table, factor, density, integrals, *rest):
    keep, send = rest[-2:]
    width = keep.shape[2]
    pairs = integrals.shape[1]
    fitted = jnp.concatenate([density[b] * factor[b] for b in range(blocks)], axis=1)
    for i in range(keep.shape[0]):
        e = sum(bit for j, bit in enumerate(bits[1:]) if i >> j & 1)
        for relative, out in ((e ^ bits[0], send), (e, keep)):
            at = pl.ds(pl.multiple_of(table[relative] * width, width), width)
            out[i] = jnp.dot(
                fitted,
                integrals[:, :, at].reshape(blocks * pairs, width),
                preferred_element_type=jnp.float32,
            ).astype(out.dtype)


def apply_kernel(orders, some, table, integrals, near, far, near_other, far_other, own, other):
    blocks, pairs, half = integrals.shape[0], integrals.shape[1], own.shape[1]
    count, _, width = near.shape
    chunks = []
    for order, low, high in ((orders[0], near, far), (orders[1], near_other, far_other)):
        chunks.append({e: (low, i) if i < count else (high, i - count) for i, e in enumerate(order)})
    for first in range(0, blocks, some):
        total = None
        for e in range(2 * count):
            at = pl.ds(pl.multiple_of(table[e] * width, width), width)
            term = lax.dot_general(
                integrals[first : first + some, :, at].reshape(some * pairs, width),
                jnp.concatenate([piece[e][0][piece[e][1]] for piece in chunks], axis=0),
                (((1,), (1,)), ((), ())),
                preferred_element_type=jnp.float32,
            )
            total = term if total is None else total + term
        for b in range(some):
            value = total[b * pairs : (b + 1) * pairs].T
            own[first + b] = value[:half]
            other[first + b] = value[half:].astype(other.dtype)


def scatter_coulomb_kernel(devices, blocks, cap, table, screen, own, other, *rest):
    near, far, whole, ready = rest[: devices // 2], rest[devices // 2 : devices], rest[-2], rest[-1]
    part = whole.shape[2]
    for b in range(blocks):
        value = (own[b] + other[b].astype(jnp.float32)) * screen[b]
        ready[b] = value.astype(jnp.bfloat16)
        whole[b] = ready[b, :, pl.ds(0, part)]
    for group in range(2):
        for step in range(devices):
            for rank in range(cap):
                b = jnp.maximum(table[(group * devices + step) * cap + rank], 0)
                if step < devices // 2:
                    near[step][group * cap + rank] = ready[b]
                else:
                    far[step - devices // 2][group * cap + rank] = ready[b, :, pl.ds(part, part)]


def pass_on_kernel(devices, cap, table, whole, *rest):
    outs = rest[-(devices // 2) :]
    for group in range(2):
        for step in range(devices // 2):
            for rank in range(cap):
                b = jnp.maximum(table[(group * devices + devices // 2 + step) * cap + rank], 0)
                outs[step][group * cap + rank] = whole[b]


def gather_coulomb_kernel(devices, blocks, shell, cap, table, *rest):
    half = devices // 2
    near, passed, far = rest[:half], rest[half:devices], rest[devices : devices + half]
    rows, cols, landed, done, sems = rest[devices + half :]
    pairs = landed.shape[3]
    part = far[0].shape[2]
    for step in range(devices):
        for group in range(2):
            for rank in range(cap):
                row = table[(group * devices + step) * cap + rank]
                at = group * cap + rank

                @pl.when(row >= 0)
                def _():
                    if step < half:
                        landed[group, row] = near[step][at]
                    else:
                        landed[group, row, :, pl.ds(0, part)] = passed[step - half][at]
                        landed[group, row, :, pl.ds(part, part)] = far[step - half][at]

    to = lax.broadcasted_iota(jnp.int32, (pairs, pairs), 0)
    source = lax.broadcasted_iota(jnp.int32, (pairs, pairs), 1)
    turns = (to, (to % shell) * shell + to // shell)
    copies = []
    for group in range(2):
        turn = (source == turns[group]).astype(jnp.bfloat16)
        for row in range(blocks):
            done[group, row] = lax.dot_general(
                turn,
                landed[group, row],
                (((1,), (1,)), ((), ())),
                preferred_element_type=jnp.float32,
            ).astype(jnp.bfloat16)
            copy = pltpu.make_async_copy(
                done.at[group, row], (rows, cols)[group].at[row], sems.at[group, row]
            )
            copy.start()
            copies.append(copy)
    for copy in copies:
        copy.wait()


def local(three_index, density, screen, pair_shells, home_slot, mirror_slot):
    blocks, pairs, aux_dev = three_index.shape
    ndens = density.shape[2]
    shell = math.isqrt(pairs)
    n = lax.axis_size("pair")
    cores = lax.axis_size("aux")
    me = lax.axis_index("pair")
    core = lax.axis_index("aux")
    half = ndens // cores
    part = pairs // 2
    width = aux_dev // n
    cap = 2 + (blocks - 1) // n
    bf16, f32 = jnp.bfloat16, jnp.float32
    in_vmem = pl.BlockSpec(memory_space=pltpu.VMEM)
    anywhere = pl.BlockSpec(memory_space=pl.ANY)
    ints = functools.partial(jnp.concatenate, axis=0)

    def call(kernel, name, table, args, out_shape, out_specs, ready=(), scratch=()):
        return pl.pallas_call(
            kernel,
            out_shape=out_shape,
            grid_spec=pltpu.PrefetchScalarGridSpec(
                num_scalar_prefetch=1,
                grid=(),
                in_specs=[in_vmem] * len(args) + [anywhere] * len(ready),
                out_specs=out_specs,
                scratch_shapes=list(scratch),
            ),
            compiler_params=pltpu.CompilerParams(vmem_limit_bytes=VMEM_BYTES),
            name=name,
        )(table, *args, *ready)

    def shift(x, d):
        return lax.ppermute(x, "pair", [(s, (s + d) % n) for s in range(n)])

    def flip(x, bit):
        return lax.ppermute(x, "pair", [(s, s ^ bit) for s in range(n)])

    def swap(x):
        return lax.ppermute(x, "aux", [(s, (s + 1) % cores) for s in range(cores)])

    def after(x, *others):
        return lax.optimization_barrier((x, *others))[0]

    def slots(peers, ranks, device):
        return slots_of(peers ^ device, ranks, n, cap)

    home_held, home_passed, home_rows = tables(home_slot, n, blocks, me)
    send_table = ints(
        [slots_of((home_rows[0] - me) % n, home_rows[1], n, cap), core[None].astype(jnp.int32)]
    )
    pick_table = slots_of((me - home_held[0]) % n, home_held[1], n, cap)
    chunk_table = me ^ jnp.arange(n, dtype=jnp.int32)
    weight = jnp.where(pair_shells[:, 0] != pair_shells[:, 1], 2.0, 1.0)
    factor = (screen.astype(f32) * weight[:, None]).astype(bf16)[:, None, :]
    keeping = screen.astype(f32)[:, None, :]

    sends = pl.pallas_call(
        functools.partial(scatter_density_kernel, n, blocks, cap),
        out_shape=[jax.ShapeDtypeStruct((cap, half, pairs), bf16)] * n,
        grid_spec=pltpu.PrefetchScalarGridSpec(
            num_scalar_prefetch=1,
            grid=(1,),
            in_specs=[pl.BlockSpec((blocks, pairs, half), lambda i, t: (0, 0, t[n * cap]))],
            out_specs=[pl.BlockSpec((cap, half, pairs), lambda i, t: (0, 0, 0))] * n,
            scratch_shapes=[pltpu.VMEM((blocks, half, pairs), bf16)],
        ),
        compiler_params=pltpu.CompilerParams(vmem_limit_bytes=VMEM_BYTES),
        name="scatter_density",
    )(send_table, density)
    steps = sorted(range(1, n), key=lambda d: abs(2 * d - n))
    received = [shift(sends[d], d) for d in steps[:-1]]
    integrals = pl.pallas_call(
        load_kernel,
        out_shape=pltpu.VMEM((blocks, pairs, aux_dev), bf16),
        in_specs=[anywhere, anywhere],
        out_specs=in_vmem,
        scratch_shapes=[pltpu.SemaphoreType.DMA],
        compiler_params=pltpu.CompilerParams(vmem_limit_bytes=2 * 1024 * 1024),
        name="load_integrals",
    )(three_index, received[0])
    received += [shift(after(sends[steps[-1]], integrals), steps[-1]), sends[0]]
    steps = (*steps, 0)
    own = call(
        functools.partial(gather_density_kernel, steps, cap),
        "gather_density",
        pick_table,
        received,
        jax.ShapeDtypeStruct((blocks, half, pairs), bf16),
        in_vmem,
    )
    other = swap(own)

    mirror_held, mirror_passed, mirror_rows = tables(after(mirror_slot, own), n, blocks, me)
    out_table = ints([slots(*home_held, me), slots(*mirror_held, me)])
    pass_table = ints([slots(*held, me ^ (n // 2)) for held in (home_passed, mirror_passed)])
    in_table = ints([slots(*home_rows, me), slots(*mirror_rows, me)])

    bits = [1 << j for j in range(n.bit_length() - 1)]
    orders = (bits[1::-1] + bits[2:], bits)

    def fit(value, bits, ready=()):
        return call(
            functools.partial(fit_kernel, bits, blocks),
            "fit",
            chunk_table,
            [factor, value, integrals],
            [
                jax.ShapeDtypeStruct((n // 2, half, width), f32),
                jax.ShapeDtypeStruct((n // 2, half, width), bf16),
            ],
            [in_vmem] * 2,
            ready,
        )

    def step_together(states):
        flat, tree = jax.tree.flatten(states)
        return jax.tree.unflatten(tree, lax.optimization_barrier(flat))

    def totals(states):
        for j in range(len(bits)):
            states = step_together(states)
            found = []
            for (keep, send), order in zip(states, orders):
                value = keep + flip(send, order[j]).astype(f32)
                if j < len(bits) - 1:
                    found.append((value[0::2], value[1::2].astype(bf16)))
                else:
                    found.append(value.astype(bf16))
            states = found
        relative = [[0] for _ in orders]
        for j in reversed(range(len(bits))):
            states = step_together(states)
            fars = [flip(near, order[j]) for near, order in zip(states, orders)]
            relative = [r + [e ^ order[j] for e in r] for r, order in zip(relative, orders)]
            if j == 0:
                return [(*pair, r) for pair, r in zip(zip(states, fars), relative)]
            states = [jnp.concatenate(pair, axis=0) for pair in zip(states, fars)]

    fit_own = fit(own, orders[1])
    fit_other = fit(other, orders[0], fit_own[:1])
    (near_other, far_other, order_other), (near_own, far_own, order_own) = totals(
        [tuple(fit_other), tuple(fit_own)]
    )

    mine, theirs = call(
        functools.partial(apply_kernel, (order_own, order_other), blocks // 2),
        "apply",
        chunk_table,
        [integrals, near_own, far_own, near_other, far_other],
        [
            jax.ShapeDtypeStruct((blocks, half, pairs), f32),
            jax.ShapeDtypeStruct((blocks, half, pairs), bf16),
        ],
        [in_vmem] * 2,
    )
    sends = call(
        functools.partial(scatter_coulomb_kernel, n, blocks, cap),
        "scatter_coulomb",
        out_table,
        [keeping, mine, swap(theirs)],
        [jax.ShapeDtypeStruct((2 * cap, half, pairs), bf16)] * (n // 2)
        + [jax.ShapeDtypeStruct((2 * cap, half, part), bf16)] * (n // 2)
        + [jax.ShapeDtypeStruct((blocks, half, part), bf16)],
        [in_vmem] * (n + 1),
        scratch=[pltpu.VMEM((blocks, half, pairs), bf16)],
    )
    def direct(i, *ready):
        return flip(after(sends[n // 2 + i], *ready), n // 2 + i)

    whole = flip(sends[n], n // 2)
    near = [sends[0], flip(sends[1], 1), flip(sends[2], 2)]
    for d in range(3, n // 2):
        near.append(flip(after(sends[d], near[d - 1]), d))
    far = [direct(0), direct(1, near[1]), direct(2, near[2])]
    passed = call(
        functools.partial(pass_on_kernel, n, cap),
        "pass_on",
        pass_table,
        [whole],
        [jax.ShapeDtypeStruct((2 * cap, half, part), bf16)] * (n // 2),
        [in_vmem] * (n // 2),
        near[1:3],
    )
    passed = [passed[0]] + [flip(passed[d], d) for d in range(1, n // 2)]
    for i in range(3, n // 2):
        far.append(direct(i, passed[i - 2]))
    return call(
        functools.partial(gather_coulomb_kernel, n, blocks, shell, cap),
        "gather_coulomb",
        in_table,
        [*near, *passed, *far],
        [jax.ShapeDtypeStruct((blocks, pairs, half), bf16)] * 2,
        [anywhere] * 2,
        scratch=[
            pltpu.VMEM((2, blocks, half, pairs), bf16),
            pltpu.VMEM((2, blocks, pairs, half), bf16),
            pltpu.SemaphoreType.DMA((2, blocks)),
        ],
    )


def solution(mesh):
    in_specs = (
        P(("mol", "pair"), None, "aux"),
        P(("mol", "pair"), None, None),
        P(("mol", "pair"), None),
        P(("mol", "pair"), None),
        P("mol"),
        P("mol"),
    )
    out_specs = (P(("mol", "pair"), None, "aux"), P(("mol", "pair"), None, "aux"))
    return jax.shard_map(local, mesh=mesh, in_specs=in_specs, out_specs=out_specs, check_vma=False)
```

```python
import functools
import math

import jax
import jax.numpy as jnp
from jax import lax
from jax.experimental import pallas as pl
from jax.experimental.pallas import tpu as pltpu
from jax.sharding import PartitionSpec as P

VMEM_BYTES = 20 * 1024 * 1024


def tables(slots, devices, blocks_dev, me):
    total = slots.shape[0]
    numbers = jnp.arange(total, dtype=jnp.int32)
    source = numbers // blocks_dev
    target = slots // blocks_dev
    joined = source * devices + target
    earlier = (joined[:, None] == joined[None, :]) & (numbers[None, :] < numbers[:, None])
    rank = jnp.sum(earlier.astype(jnp.int32), axis=1)
    held = []
    for device in (me, me ^ (devices // 2)):
        for values in (target, rank):
            held.append(lax.dynamic_slice_in_dim(values, device * blocks_dev, blocks_dev, 0))
    rows = me * blocks_dev + jnp.arange(blocks_dev, dtype=jnp.int32)
    hot = slots[None, :] == rows[:, None]
    row_source = jnp.sum(jnp.where(hot, source[None, :], 0), axis=1)
    row_rank = jnp.sum(jnp.where(hot, rank[None, :], 0), axis=1)
    return held[:2], held[2:], (row_source, row_rank)


def slots_of(steps, ranks, devices, cap):
    held = (steps * cap + ranks)[None, :] == jnp.arange(devices * cap, dtype=jnp.int32)[:, None]
    numbers = jnp.arange(steps.shape[0], dtype=jnp.int32)
    return jnp.max(jnp.where(held, numbers[None, :], -1), axis=1)


def load_kernel(source, ready, target, sem):
    copy = pltpu.make_async_copy(source, target, sem)
    copy.start()
    copy.wait()


def scatter_density_kernel(devices, blocks, cap, table, density, *rest):
    sends, turned = rest[:devices], rest[-1]
    for row in range(blocks):
        turned[row] = density[row].T
    for step in range(devices):
        for rank in range(cap):
            row = jnp.maximum(table[step * cap + rank], 0)
            sends[step][rank] = turned[row]


def gather_density_kernel(steps, cap, table, *rest):
    out = rest[-1]
    for step, piece in zip(steps, rest):
        for rank in range(cap):
            row = table[step * cap + rank]

            @pl.when(row >= 0)
            def _():
                out[row] = piece[rank]


def fit_kernel(bits, blocks, table, factor, density, integrals, *rest):
    keep, send = rest[-2:]
    width = keep.shape[2]
    pairs = integrals.shape[1]
    fitted = jnp.concatenate([density[b] * factor[b] for b in range(blocks)], axis=1)
    for i in range(keep.shape[0]):
        e = sum(bit for j, bit in enumerate(bits[1:]) if i >> j & 1)
        for relative, out in ((e ^ bits[0], send), (e, keep)):
            at = pl.ds(pl.multiple_of(table[relative] * width, width), width)
            out[i] = jnp.dot(
                fitted,
                integrals[:, :, at].reshape(blocks * pairs, width),
                preferred_element_type=jnp.float32,
            ).astype(out.dtype)


def apply_kernel(orders, some, table, integrals, near, far, near_other, far_other, own, other):
    blocks, pairs, half = integrals.shape[0], integrals.shape[1], own.shape[1]
    count, _, width = near.shape
    chunks = []
    for order, low, high in ((orders[0], near, far), (orders[1], near_other, far_other)):
        chunks.append({e: (low, i) if i < count else (high, i - count) for i, e in enumerate(order)})
    for first in range(0, blocks, some):
        total = None
        for e in range(2 * count):
            at = pl.ds(pl.multiple_of(table[e] * width, width), width)
            term = lax.dot_general(
                integrals[first : first + some, :, at].reshape(some * pairs, width),
                jnp.concatenate([piece[e][0][piece[e][1]] for piece in chunks], axis=0),
                (((1,), (1,)), ((), ())),
                preferred_element_type=jnp.float32,
            )
            total = term if total is None else total + term
        for b in range(some):
            value = total[b * pairs : (b + 1) * pairs].T
            own[first + b] = value[:half]
            other[first + b] = value[half:].astype(other.dtype)


def scatter_coulomb_kernel(devices, blocks, cap, table, screen, own, other, *rest):
    near, far, whole, ready = rest[: devices // 2], rest[devices // 2 : devices], rest[-2], rest[-1]
    part = whole.shape[2]
    for b in range(blocks):
        value = (own[b] + other[b].astype(jnp.float32)) * screen[b]
        ready[b] = value.astype(jnp.bfloat16)
        whole[b] = ready[b, :, pl.ds(0, part)]
    for group in range(2):
        for step in range(devices):
            for rank in range(cap):
                b = jnp.maximum(table[(group * devices + step) * cap + rank], 0)
                if step < devices // 2:
                    near[step][group * cap + rank] = ready[b]
                else:
                    far[step - devices // 2][group * cap + rank] = ready[b, :, pl.ds(part, part)]


def pass_on_kernel(devices, cap, table, whole, *rest):
    outs = rest[-(devices // 2) :]
    for group in range(2):
        for step in range(devices // 2):
            for rank in range(cap):
                b = jnp.maximum(table[(group * devices + devices // 2 + step) * cap + rank], 0)
                outs[step][group * cap + rank] = whole[b]


def gather_coulomb_kernel(devices, blocks, shell, cap, table, *rest):
    half = devices // 2
    near, passed, far = rest[:half], rest[half:devices], rest[devices : devices + half]
    rows, cols, landed, done, sems = rest[devices + half :]
    pairs = landed.shape[3]
    part = far[0].shape[2]
    for step in range(devices):
        for group in range(2):
            for rank in range(cap):
                row = table[(group * devices + step) * cap + rank]
                at = group * cap + rank

                @pl.when(row >= 0)
                def _():
                    if step < half:
                        landed[group, row] = near[step][at]
                    else:
                        landed[group, row, :, pl.ds(0, part)] = passed[step - half][at]
                        landed[group, row, :, pl.ds(part, part)] = far[step - half][at]

    to = lax.broadcasted_iota(jnp.int32, (pairs, pairs), 0)
    source = lax.broadcasted_iota(jnp.int32, (pairs, pairs), 1)
    turns = (to, (to % shell) * shell + to // shell)
    copies = []
    for group in range(2):
        turn = (source == turns[group]).astype(jnp.bfloat16)
        for row in range(blocks):
            done[group, row] = lax.dot_general(
                turn,
                landed[group, row],
                (((1,), (1,)), ((), ())),
                preferred_element_type=jnp.float32,
            ).astype(jnp.bfloat16)
            copy = pltpu.make_async_copy(
                done.at[group, row], (rows, cols)[group].at[row], sems.at[group, row]
            )
            copy.start()
            copies.append(copy)
    for copy in copies:
        copy.wait()


def local(three_index, density, screen, pair_shells, home_slot, mirror_slot):
    blocks, pairs, aux_dev = three_index.shape
    ndens = density.shape[2]
    shell = math.isqrt(pairs)
    n = lax.axis_size("pair")
    cores = lax.axis_size("aux")
    me = lax.axis_index("pair")
    core = lax.axis_index("aux")
    half = ndens // cores
    part = pairs // 2
    width = aux_dev // n
    cap = 2 + (blocks - 1) // n
    bf16, f32 = jnp.bfloat16, jnp.float32
    in_vmem = pl.BlockSpec(memory_space=pltpu.VMEM)
    anywhere = pl.BlockSpec(memory_space=pl.ANY)
    ints = functools.partial(jnp.concatenate, axis=0)

    def call(kernel, name, table, args, out_shape, out_specs, ready=(), scratch=()):
        return pl.pallas_call(
            kernel,
            out_shape=out_shape,
            grid_spec=pltpu.PrefetchScalarGridSpec(
                num_scalar_prefetch=1,
                grid=(),
                in_specs=[in_vmem] * len(args) + [anywhere] * len(ready),
                out_specs=out_specs,
                scratch_shapes=list(scratch),
            ),
            compiler_params=pltpu.CompilerParams(vmem_limit_bytes=VMEM_BYTES),
            name=name,
        )(table, *args, *ready)

    def shift(x, d):
        return lax.ppermute(x, "pair", [(s, (s + d) % n) for s in range(n)])

    def flip(x, bit):
        return lax.ppermute(x, "pair", [(s, s ^ bit) for s in range(n)])

    def swap(x):
        return lax.ppermute(x, "aux", [(s, (s + 1) % cores) for s in range(cores)])

    def after(x, *others):
        return lax.optimization_barrier((x, *others))[0]

    def slots(peers, ranks, device):
        return slots_of(peers ^ device, ranks, n, cap)

    home_held, home_passed, home_rows = tables(home_slot, n, blocks, me)
    send_table = ints(
        [slots_of((home_rows[0] - me) % n, home_rows[1], n, cap), core[None].astype(jnp.int32)]
    )
    pick_table = slots_of((me - home_held[0]) % n, home_held[1], n, cap)
    chunk_table = me ^ jnp.arange(n, dtype=jnp.int32)
    weight = jnp.where(pair_shells[:, 0] != pair_shells[:, 1], 2.0, 1.0)
    factor = (screen.astype(f32) * weight[:, None]).astype(bf16)[:, None, :]
    keeping = screen.astype(f32)[:, None, :]

    sends = pl.pallas_call(
        functools.partial(scatter_density_kernel, n, blocks, cap),
        out_shape=[jax.ShapeDtypeStruct((cap, half, pairs), bf16)] * n,
        grid_spec=pltpu.PrefetchScalarGridSpec(
            num_scalar_prefetch=1,
            grid=(1,),
            in_specs=[pl.BlockSpec((blocks, pairs, half), lambda i, t: (0, 0, t[n * cap]))],
            out_specs=[pl.BlockSpec((cap, half, pairs), lambda i, t: (0, 0, 0))] * n,
            scratch_shapes=[pltpu.VMEM((blocks, half, pairs), bf16)],
        ),
        compiler_params=pltpu.CompilerParams(vmem_limit_bytes=VMEM_BYTES),
        name="scatter_density",
    )(send_table, density)
    steps = sorted(range(1, n), key=lambda d: abs(2 * d - n))
    received = [shift(sends[d], d) for d in steps[:-1]]
    integrals = pl.pallas_call(
        load_kernel,
        out_shape=pltpu.VMEM((blocks, pairs, aux_dev), bf16),
        in_specs=[anywhere, anywhere],
        out_specs=in_vmem,
        scratch_shapes=[pltpu.SemaphoreType.DMA],
        compiler_params=pltpu.CompilerParams(vmem_limit_bytes=2 * 1024 * 1024),
        name="load_integrals",
    )(three_index, received[0])
    received += [shift(after(sends[steps[-1]], integrals), steps[-1]), sends[0]]
    steps = (*steps, 0)
    own = call(
        functools.partial(gather_density_kernel, steps, cap),
        "gather_density",
        pick_table,
        received,
        jax.ShapeDtypeStruct((blocks, half, pairs), bf16),
        in_vmem,
    )
    other = swap(own)

    mirror_held, mirror_passed, mirror_rows = tables(after(mirror_slot, own), n, blocks, me)
    out_table = ints([slots(*home_held, me), slots(*mirror_held, me)])
    pass_table = ints([slots(*held, me ^ (n // 2)) for held in (home_passed, mirror_passed)])
    in_table = ints([slots(*home_rows, me), slots(*mirror_rows, me)])

    bits = [1 << j for j in range(n.bit_length() - 1)]
    orders = (bits[1::-1] + bits[2:], bits)

    def fit(value, bits, ready=()):
        return call(
            functools.partial(fit_kernel, bits, blocks),
            "fit",
            chunk_table,
            [factor, value, integrals],
            [
                jax.ShapeDtypeStruct((n // 2, half, width), f32),
                jax.ShapeDtypeStruct((n // 2, half, width), bf16),
            ],
            [in_vmem] * 2,
            ready,
        )

    def step_together(states):
        flat, tree = jax.tree.flatten(states)
        return jax.tree.unflatten(tree, lax.optimization_barrier(flat))

    def totals(states):
        last = len(bits) - 1
        for j in range(last):
            states = step_together(states)
            found = []
            for (keep, send), order in zip(states, orders):
                value = keep + flip(send, order[j]).astype(f32)
                if j < last - 1:
                    found.append((value[0::2], value[1::2].astype(bf16)))
                else:
                    found.append((value, value[::-1].astype(bf16)))
            states = found
        states = step_together(states)
        states = [
            (keep + flip(send, order[last]).astype(f32)).astype(bf16)
            for (keep, send), order in zip(states, orders)
        ]
        relative = [[0, order[last]] for order in orders]
        for j in reversed(range(last)):
            states = step_together(states)
            fars = [flip(near, order[j]) for near, order in zip(states, orders)]
            relative = [r + [e ^ order[j] for e in r] for r, order in zip(relative, orders)]
            if j == 0:
                return [(*pair, r) for pair, r in zip(zip(states, fars), relative)]
            states = [jnp.concatenate(pair, axis=0) for pair in zip(states, fars)]

    fit_own = fit(own, orders[1])
    fit_other = fit(other, orders[0], fit_own[:1])
    (near_other, far_other, order_other), (near_own, far_own, order_own) = totals(
        [tuple(fit_other), tuple(fit_own)]
    )

    mine, theirs = call(
        functools.partial(apply_kernel, (order_own, order_other), blocks // 2),
        "apply",
        chunk_table,
        [integrals, near_own, far_own, near_other, far_other],
        [
            jax.ShapeDtypeStruct((blocks, half, pairs), f32),
            jax.ShapeDtypeStruct((blocks, half, pairs), bf16),
        ],
        [in_vmem] * 2,
    )
    sends = call(
        functools.partial(scatter_coulomb_kernel, n, blocks, cap),
        "scatter_coulomb",
        out_table,
        [keeping, mine, swap(theirs)],
        [jax.ShapeDtypeStruct((2 * cap, half, pairs), bf16)] * (n // 2)
        + [jax.ShapeDtypeStruct((2 * cap, half, part), bf16)] * (n // 2)
        + [jax.ShapeDtypeStruct((blocks, half, part), bf16)],
        [in_vmem] * (n + 1),
        scratch=[pltpu.VMEM((blocks, half, pairs), bf16)],
    )
    def direct(i, *ready):
        return flip(after(sends[n // 2 + i], *ready), n // 2 + i)

    whole = flip(sends[n], n // 2)
    near = [sends[0], flip(sends[1], 1), flip(sends[2], 2)]
    for d in range(3, n // 2):
        near.append(flip(after(sends[d], near[d - 1]), d))
    far = [direct(0), direct(1, near[1]), direct(2, near[2])]
    passed = call(
        functools.partial(pass_on_kernel, n, cap),
        "pass_on",
        pass_table,
        [whole],
        [jax.ShapeDtypeStruct((2 * cap, half, part), bf16)] * (n // 2),
        [in_vmem] * (n // 2),
        near[1:3],
    )
    passed = [passed[0]] + [flip(passed[d], d) for d in range(1, n // 2)]
    for i in range(3, n // 2):
        far.append(direct(i, passed[i - 2]))
    return call(
        functools.partial(gather_coulomb_kernel, n, blocks, shell, cap),
        "gather_coulomb",
        in_table,
        [*near, *passed, *far],
        [jax.ShapeDtypeStruct((blocks, pairs, half), bf16)] * 2,
        [anywhere] * 2,
        scratch=[
            pltpu.VMEM((2, blocks, half, pairs), bf16),
            pltpu.VMEM((2, blocks, pairs, half), bf16),
            pltpu.SemaphoreType.DMA((2, blocks)),
        ],
    )


def solution(mesh):
    in_specs = (
        P(("mol", "pair"), None, "aux"),
        P(("mol", "pair"), None, None),
        P(("mol", "pair"), None),
        P(("mol", "pair"), None),
        P("mol"),
        P("mol"),
    )
    out_specs = (P(("mol", "pair"), None, "aux"), P(("mol", "pair"), None, "aux"))
    return jax.shard_map(local, mesh=mesh, in_specs=in_specs, out_specs=out_specs, check_vma=False)
```

```python
import functools
import math

import jax
import jax.numpy as jnp
from jax import lax
from jax.experimental import pallas as pl
from jax.experimental.pallas import tpu as pltpu
from jax.sharding import PartitionSpec as P

VMEM_BYTES = 20 * 1024 * 1024


def tables(slots, devices, blocks_dev, me):
    total = slots.shape[0]
    numbers = jnp.arange(total, dtype=jnp.int32)
    source = numbers // blocks_dev
    target = slots // blocks_dev
    joined = source * devices + target
    earlier = (joined[:, None] == joined[None, :]) & (numbers[None, :] < numbers[:, None])
    rank = jnp.sum(earlier.astype(jnp.int32), axis=1)
    held = []
    for device in (me, me ^ (devices // 2)):
        for values in (target, rank):
            held.append(lax.dynamic_slice_in_dim(values, device * blocks_dev, blocks_dev, 0))
    rows = me * blocks_dev + jnp.arange(blocks_dev, dtype=jnp.int32)
    hot = slots[None, :] == rows[:, None]
    row_source = jnp.sum(jnp.where(hot, source[None, :], 0), axis=1)
    row_rank = jnp.sum(jnp.where(hot, rank[None, :], 0), axis=1)
    return held[:2], held[2:], (row_source, row_rank)


def slots_of(steps, ranks, devices, cap):
    held = (steps * cap + ranks)[None, :] == jnp.arange(devices * cap, dtype=jnp.int32)[:, None]
    numbers = jnp.arange(steps.shape[0], dtype=jnp.int32)
    return jnp.max(jnp.where(held, numbers[None, :], -1), axis=1)


def load_kernel(source, ready, target, sem):
    copy = pltpu.make_async_copy(source, target, sem)
    copy.start()
    copy.wait()


def scatter_density_kernel(devices, blocks, cap, table, density, *rest):
    sends, turned = rest[:devices], rest[-1]
    for row in range(blocks):
        turned[row] = density[row].T
    for step in range(devices):
        for rank in range(cap):
            row = jnp.maximum(table[step * cap + rank], 0)
            sends[step][rank] = turned[row]


def gather_density_kernel(steps, cap, table, *rest):
    out = rest[-1]
    for step, piece in zip(steps, rest):
        for rank in range(cap):
            row = table[step * cap + rank]

            @pl.when(row >= 0)
            def _():
                out[row] = piece[rank]


def fit_kernel(bits, blocks, table, factor, density, integrals, *rest):
    keep, send = rest[-2:]
    width = keep.shape[2]
    pairs = integrals.shape[1]
    fitted = jnp.concatenate([density[b] * factor[b] for b in range(blocks)], axis=1)
    for i in range(keep.shape[0]):
        e = sum(bit for j, bit in enumerate(bits[1:]) if i >> j & 1)
        for relative, out in ((e ^ bits[0], send), (e, keep)):
            at = pl.ds(pl.multiple_of(table[relative] * width, width), width)
            out[i] = jnp.dot(
                fitted,
                integrals[:, :, at].reshape(blocks * pairs, width),
                preferred_element_type=jnp.float32,
            ).astype(out.dtype)


def apply_kernel(orders, some, table, integrals, near, far, near_other, far_other, own, other):
    blocks, pairs, half = integrals.shape[0], integrals.shape[1], own.shape[1]
    count, _, width = near.shape
    chunks = []
    for order, low, high in ((orders[0], near, far), (orders[1], near_other, far_other)):
        chunks.append({e: (low, i) if i < count else (high, i - count) for i, e in enumerate(order)})
    for first in range(0, blocks, some):
        total = None
        for e in range(2 * count):
            at = pl.ds(pl.multiple_of(table[e] * width, width), width)
            term = lax.dot_general(
                integrals[first : first + some, :, at].reshape(some * pairs, width),
                jnp.concatenate([piece[e][0][piece[e][1]] for piece in chunks], axis=0),
                (((1,), (1,)), ((), ())),
                preferred_element_type=jnp.float32,
            )
            total = term if total is None else total + term
        for b in range(some):
            value = total[b * pairs : (b + 1) * pairs].T
            own[first + b] = value[:half]
            other[first + b] = value[half:].astype(other.dtype)


def scatter_coulomb_kernel(devices, blocks, cap, table, screen, own, other, *rest):
    near, far, whole, ready = rest[: devices // 2], rest[devices // 2 : devices], rest[-2], rest[-1]
    part = whole.shape[2]
    for b in range(blocks):
        value = (own[b] + other[b].astype(jnp.float32)) * screen[b]
        ready[b] = value.astype(jnp.bfloat16)
        whole[b] = ready[b, :, pl.ds(0, part)]
    for group in range(2):
        for step in range(devices):
            for rank in range(cap):
                b = jnp.maximum(table[(group * devices + step) * cap + rank], 0)
                if step < devices // 2:
                    near[step][group * cap + rank] = ready[b]
                else:
                    far[step - devices // 2][group * cap + rank] = ready[b, :, pl.ds(part, part)]


def pass_on_kernel(devices, cap, table, whole, *rest):
    outs = rest[-(devices // 2) :]
    for group in range(2):
        for step in range(devices // 2):
            for rank in range(cap):
                b = jnp.maximum(table[(group * devices + devices // 2 + step) * cap + rank], 0)
                outs[step][group * cap + rank] = whole[b]


def gather_coulomb_kernel(devices, blocks, shell, cap, table, *rest):
    half = devices // 2
    near, passed, far = rest[:half], rest[half:devices], rest[devices : devices + half]
    rows, cols, landed, done, sems = rest[devices + half :]
    pairs = landed.shape[3]
    part = far[0].shape[2]
    for step in range(devices):
        for group in range(2):
            for rank in range(cap):
                row = table[(group * devices + step) * cap + rank]
                at = group * cap + rank

                @pl.when(row >= 0)
                def _():
                    if step < half:
                        landed[group, row] = near[step][at]
                    else:
                        landed[group, row, :, pl.ds(0, part)] = passed[step - half][at]
                        landed[group, row, :, pl.ds(part, part)] = far[step - half][at]

    to = lax.broadcasted_iota(jnp.int32, (pairs, pairs), 0)
    source = lax.broadcasted_iota(jnp.int32, (pairs, pairs), 1)
    turns = (to, (to % shell) * shell + to // shell)
    copies = []
    for group in range(2):
        turn = (source == turns[group]).astype(jnp.bfloat16)
        for row in range(blocks):
            done[group, row] = lax.dot_general(
                turn,
                landed[group, row],
                (((1,), (1,)), ((), ())),
                preferred_element_type=jnp.float32,
            ).astype(jnp.bfloat16)
            copy = pltpu.make_async_copy(
                done.at[group, row], (rows, cols)[group].at[row], sems.at[group, row]
            )
            copy.start()
            copies.append(copy)
    for copy in copies:
        copy.wait()


def local(three_index, density, screen, pair_shells, home_slot, mirror_slot):
    blocks, pairs, aux_dev = three_index.shape
    ndens = density.shape[2]
    shell = math.isqrt(pairs)
    n = lax.axis_size("pair")
    cores = lax.axis_size("aux")
    me = lax.axis_index("pair")
    core = lax.axis_index("aux")
    half = ndens // cores
    part = pairs // 2
    width = aux_dev // n
    cap = 2 + (blocks - 1) // n
    bf16, f32 = jnp.bfloat16, jnp.float32
    in_vmem = pl.BlockSpec(memory_space=pltpu.VMEM)
    anywhere = pl.BlockSpec(memory_space=pl.ANY)
    ints = functools.partial(jnp.concatenate, axis=0)

    def call(kernel, name, table, args, out_shape, out_specs, ready=(), scratch=()):
        return pl.pallas_call(
            kernel,
            out_shape=out_shape,
            grid_spec=pltpu.PrefetchScalarGridSpec(
                num_scalar_prefetch=1,
                grid=(),
                in_specs=[in_vmem] * len(args) + [anywhere] * len(ready),
                out_specs=out_specs,
                scratch_shapes=list(scratch),
            ),
            compiler_params=pltpu.CompilerParams(vmem_limit_bytes=VMEM_BYTES),
            name=name,
        )(table, *args, *ready)

    def shift(x, d):
        return lax.ppermute(x, "pair", [(s, (s + d) % n) for s in range(n)])

    def flip(x, bit):
        return lax.ppermute(x, "pair", [(s, s ^ bit) for s in range(n)])

    def swap(x):
        return lax.ppermute(x, "aux", [(s, (s + 1) % cores) for s in range(cores)])

    def after(x, *others):
        return lax.optimization_barrier((x, *others))[0]

    def slots(peers, ranks, device):
        return slots_of(peers ^ device, ranks, n, cap)

    home_held, home_passed, home_rows = tables(home_slot, n, blocks, me)
    send_table = ints(
        [slots_of((home_rows[0] - me) % n, home_rows[1], n, cap), core[None].astype(jnp.int32)]
    )
    pick_table = slots_of((me - home_held[0]) % n, home_held[1], n, cap)
    chunk_table = me ^ jnp.arange(n, dtype=jnp.int32)
    weight = jnp.where(pair_shells[:, 0] != pair_shells[:, 1], 2.0, 1.0)
    factor = (screen.astype(f32) * weight[:, None]).astype(bf16)[:, None, :]
    keeping = screen.astype(f32)[:, None, :]

    sends = pl.pallas_call(
        functools.partial(scatter_density_kernel, n, blocks, cap),
        out_shape=[jax.ShapeDtypeStruct((cap, half, pairs), bf16)] * n,
        grid_spec=pltpu.PrefetchScalarGridSpec(
            num_scalar_prefetch=1,
            grid=(1,),
            in_specs=[pl.BlockSpec((blocks, pairs, half), lambda i, t: (0, 0, t[n * cap]))],
            out_specs=[pl.BlockSpec((cap, half, pairs), lambda i, t: (0, 0, 0))] * n,
            scratch_shapes=[pltpu.VMEM((blocks, half, pairs), bf16)],
        ),
        compiler_params=pltpu.CompilerParams(vmem_limit_bytes=VMEM_BYTES),
        name="scatter_density",
    )(send_table, density)
    steps = sorted(range(1, n), key=lambda d: abs(2 * d - n))
    received = [shift(sends[d], d) for d in steps[:-1]]
    integrals = pl.pallas_call(
        load_kernel,
        out_shape=pltpu.VMEM((blocks, pairs, aux_dev), bf16),
        in_specs=[anywhere, anywhere],
        out_specs=in_vmem,
        scratch_shapes=[pltpu.SemaphoreType.DMA],
        compiler_params=pltpu.CompilerParams(vmem_limit_bytes=2 * 1024 * 1024),
        name="load_integrals",
    )(three_index, received[0])
    received += [shift(after(sends[steps[-1]], integrals), steps[-1]), sends[0]]
    steps = (*steps, 0)
    own = call(
        functools.partial(gather_density_kernel, steps, cap),
        "gather_density",
        pick_table,
        received,
        jax.ShapeDtypeStruct((blocks, half, pairs), bf16),
        in_vmem,
    )
    other = swap(own)

    mirror_held, mirror_passed, mirror_rows = tables(after(mirror_slot, own), n, blocks, me)
    out_table = ints([slots(*home_held, me), slots(*mirror_held, me)])
    pass_table = ints([slots(*held, me ^ (n // 2)) for held in (home_passed, mirror_passed)])
    in_table = ints([slots(*home_rows, me), slots(*mirror_rows, me)])

    bits = [1 << j for j in range(n.bit_length() - 1)]
    orders = (bits[1::-1] + bits[2:], bits)

    def fit(value, bits, ready=()):
        return call(
            functools.partial(fit_kernel, bits, blocks),
            "fit",
            chunk_table,
            [factor, value, integrals],
            [
                jax.ShapeDtypeStruct((n // 2, half, width), f32),
                jax.ShapeDtypeStruct((n // 2, half, width), bf16),
            ],
            [in_vmem] * 2,
            ready,
        )

    def step_together(states):
        flat, tree = jax.tree.flatten(states)
        return jax.tree.unflatten(tree, lax.optimization_barrier(flat))

    def totals(states):
        last = len(bits) - 1
        for j in range(last):
            states = step_together(states)
            found = []
            for (keep, send), order in zip(states, orders):
                value = keep + flip(send, order[j]).astype(f32)
                if j < last - 1:
                    found.append((value[0::2], value[1::2].astype(bf16)))
                else:
                    turned = jnp.concatenate([value[1:], value[:1]], axis=0)
                    found.append((value, turned.astype(bf16)))
            states = found
        states = step_together(states)
        states = [
            (keep + flip(send, order[last]).astype(f32)).astype(bf16)
            for (keep, send), order in zip(states, orders)
        ]
        relative = [[0, order[last]] for order in orders]
        for j in reversed(range(last)):
            states = step_together(states)
            fars = [flip(near, order[j]) for near, order in zip(states, orders)]
            relative = [r + [e ^ order[j] for e in r] for r, order in zip(relative, orders)]
            if j == 0:
                return [(*pair, r) for pair, r in zip(zip(states, fars), relative)]
            states = [jnp.concatenate(pair, axis=0) for pair in zip(states, fars)]

    fit_own = fit(own, orders[1])
    fit_other = fit(other, orders[0], fit_own[:1])
    (near_other, far_other, order_other), (near_own, far_own, order_own) = totals(
        [tuple(fit_other), tuple(fit_own)]
    )

    mine, theirs = call(
        functools.partial(apply_kernel, (order_own, order_other), blocks // 2),
        "apply",
        chunk_table,
        [integrals, near_own, far_own, near_other, far_other],
        [
            jax.ShapeDtypeStruct((blocks, half, pairs), f32),
            jax.ShapeDtypeStruct((blocks, half, pairs), bf16),
        ],
        [in_vmem] * 2,
    )
    sends = call(
        functools.partial(scatter_coulomb_kernel, n, blocks, cap),
        "scatter_coulomb",
        out_table,
        [keeping, mine, swap(theirs)],
        [jax.ShapeDtypeStruct((2 * cap, half, pairs), bf16)] * (n // 2)
        + [jax.ShapeDtypeStruct((2 * cap, half, part), bf16)] * (n // 2)
        + [jax.ShapeDtypeStruct((blocks, half, part), bf16)],
        [in_vmem] * (n + 1),
        scratch=[pltpu.VMEM((blocks, half, pairs), bf16)],
    )
    def direct(i, *ready):
        return flip(after(sends[n // 2 + i], *ready), n // 2 + i)

    whole = flip(sends[n], n // 2)
    near = [sends[0], flip(sends[1], 1), flip(sends[2], 2)]
    for d in range(3, n // 2):
        near.append(flip(after(sends[d], near[d - 1]), d))
    far = [direct(0), direct(1, near[1]), direct(2, near[2])]
    passed = call(
        functools.partial(pass_on_kernel, n, cap),
        "pass_on",
        pass_table,
        [whole],
        [jax.ShapeDtypeStruct((2 * cap, half, part), bf16)] * (n // 2),
        [in_vmem] * (n // 2),
        near[1:3],
    )
    passed = [passed[0]] + [flip(passed[d], d) for d in range(1, n // 2)]
    for i in range(3, n // 2):
        far.append(direct(i, passed[i - 2]))
    return call(
        functools.partial(gather_coulomb_kernel, n, blocks, shell, cap),
        "gather_coulomb",
        in_table,
        [*near, *passed, *far],
        [jax.ShapeDtypeStruct((blocks, pairs, half), bf16)] * 2,
        [anywhere] * 2,
        scratch=[
            pltpu.VMEM((2, blocks, half, pairs), bf16),
            pltpu.VMEM((2, blocks, pairs, half), bf16),
            pltpu.SemaphoreType.DMA((2, blocks)),
        ],
    )


def solution(mesh):
    in_specs = (
        P(("mol", "pair"), None, "aux"),
        P(("mol", "pair"), None, None),
        P(("mol", "pair"), None),
        P(("mol", "pair"), None),
        P("mol"),
        P("mol"),
    )
    out_specs = (P(("mol", "pair"), None, "aux"), P(("mol", "pair"), None, "aux"))
    return jax.shard_map(local, mesh=mesh, in_specs=in_specs, out_specs=out_specs, check_vma=False)
```

```python
import functools
import math

import jax
import jax.numpy as jnp
from jax import lax
from jax.experimental import pallas as pl
from jax.experimental.pallas import tpu as pltpu
from jax.sharding import PartitionSpec as P

VMEM_BYTES = 20 * 1024 * 1024


def tables(slots, devices, blocks_dev, me):
    total = slots.shape[0]
    numbers = jnp.arange(total, dtype=jnp.int32)
    source = numbers // blocks_dev
    target = slots // blocks_dev
    joined = source * devices + target
    earlier = (joined[:, None] == joined[None, :]) & (numbers[None, :] < numbers[:, None])
    rank = jnp.sum(earlier.astype(jnp.int32), axis=1)
    held = []
    for device in (me, me ^ (devices // 2)):
        for values in (target, rank):
            held.append(lax.dynamic_slice_in_dim(values, device * blocks_dev, blocks_dev, 0))
    rows = me * blocks_dev + jnp.arange(blocks_dev, dtype=jnp.int32)
    hot = slots[None, :] == rows[:, None]
    row_source = jnp.sum(jnp.where(hot, source[None, :], 0), axis=1)
    row_rank = jnp.sum(jnp.where(hot, rank[None, :], 0), axis=1)
    return held[:2], held[2:], (row_source, row_rank)


def slots_of(steps, ranks, devices, cap):
    held = (steps * cap + ranks)[None, :] == jnp.arange(devices * cap, dtype=jnp.int32)[:, None]
    numbers = jnp.arange(steps.shape[0], dtype=jnp.int32)
    return jnp.max(jnp.where(held, numbers[None, :], -1), axis=1)


def load_kernel(source, ready, target, sem):
    copy = pltpu.make_async_copy(source, target, sem)
    copy.start()
    copy.wait()


def scatter_density_kernel(devices, blocks, cap, table, density, *rest):
    sends, turned = rest[:devices], rest[-1]
    for row in range(blocks):
        turned[row] = density[row].T
    for step in range(devices):
        for rank in range(cap):
            row = jnp.maximum(table[step * cap + rank], 0)
            sends[step][rank] = turned[row]


def gather_density_kernel(steps, cap, table, *rest):
    out = rest[-1]
    for step, piece in zip(steps, rest):
        for rank in range(cap):
            row = table[step * cap + rank]

            @pl.when(row >= 0)
            def _():
                out[row] = piece[rank]


def fit_kernel(bits, blocks, table, factor, density, integrals, *rest):
    keep, send = rest[-2:]
    width = keep.shape[2]
    pairs = integrals.shape[1]
    fitted = jnp.concatenate([density[b] * factor[b] for b in range(blocks)], axis=1)
    for i in range(keep.shape[0]):
        e = sum(bit for j, bit in enumerate(bits[1:]) if i >> j & 1)
        for relative, out in ((e ^ bits[0], send), (e, keep)):
            at = pl.ds(pl.multiple_of(table[relative] * width, width), width)
            out[i] = jnp.dot(
                fitted,
                integrals[:, :, at].reshape(blocks * pairs, width),
                preferred_element_type=jnp.float32,
            ).astype(out.dtype)


def apply_kernel(orders, some, table, integrals, near, far, near_other, far_other, own, other):
    blocks, pairs, half = integrals.shape[0], integrals.shape[1], own.shape[1]
    count, _, width = near.shape
    chunks = []
    for order, low, high in ((orders[0], near, far), (orders[1], near_other, far_other)):
        chunks.append({e: (low, i) if i < count else (high, i - count) for i, e in enumerate(order)})
    for first in range(0, blocks, some):
        total = None
        for e in range(2 * count):
            at = pl.ds(pl.multiple_of(table[e] * width, width), width)
            term = lax.dot_general(
                integrals[first : first + some, :, at].reshape(some * pairs, width),
                jnp.concatenate([piece[e][0][piece[e][1]] for piece in chunks], axis=0),
                (((1,), (1,)), ((), ())),
                preferred_element_type=jnp.float32,
            )
            total = term if total is None else total + term
        for b in range(some):
            value = total[b * pairs : (b + 1) * pairs].T
            own[first + b] = value[:half]
            other[first + b] = value[half:].astype(other.dtype)


def scatter_coulomb_kernel(devices, blocks, cap, table, screen, own, other, *rest):
    near, far, whole, ready = rest[: devices // 2], rest[devices // 2 : devices], rest[-2], rest[-1]
    part = whole.shape[2]
    for b in range(blocks):
        value = (own[b] + other[b].astype(jnp.float32)) * screen[b]
        ready[b] = value.astype(jnp.bfloat16)
        whole[b] = ready[b, :, pl.ds(0, part)]
    for group in range(2):
        for step in range(devices):
            for rank in range(cap):
                b = jnp.maximum(table[(group * devices + step) * cap + rank], 0)
                if step < devices // 2:
                    near[step][group * cap + rank] = ready[b]
                else:
                    far[step - devices // 2][group * cap + rank] = ready[b, :, pl.ds(part, part)]


def pass_on_kernel(devices, cap, table, whole, *rest):
    outs = rest[-(devices // 2) :]
    for group in range(2):
        for step in range(devices // 2):
            for rank in range(cap):
                b = jnp.maximum(table[(group * devices + devices // 2 + step) * cap + rank], 0)
                outs[step][group * cap + rank] = whole[b]


def gather_coulomb_kernel(devices, blocks, shell, cap, table, *rest):
    half = devices // 2
    near, passed, far = rest[:half], rest[half:devices], rest[devices : devices + half]
    rows, cols, landed, done, sems = rest[devices + half :]
    pairs = landed.shape[3]
    part = far[0].shape[2]
    for step in range(devices):
        for group in range(2):
            for rank in range(cap):
                row = table[(group * devices + step) * cap + rank]
                at = group * cap + rank

                @pl.when(row >= 0)
                def _():
                    if step < half:
                        landed[group, row] = near[step][at]
                    else:
                        landed[group, row, :, pl.ds(0, part)] = passed[step - half][at]
                        landed[group, row, :, pl.ds(part, part)] = far[step - half][at]

    to = lax.broadcasted_iota(jnp.int32, (pairs, pairs), 0)
    source = lax.broadcasted_iota(jnp.int32, (pairs, pairs), 1)
    turns = (to, (to % shell) * shell + to // shell)
    copies = []
    for group in range(2):
        turn = (source == turns[group]).astype(jnp.bfloat16)
        for row in range(blocks):
            done[group, row] = lax.dot_general(
                turn,
                landed[group, row],
                (((1,), (1,)), ((), ())),
                preferred_element_type=jnp.float32,
            ).astype(jnp.bfloat16)
            copy = pltpu.make_async_copy(
                done.at[group, row], (rows, cols)[group].at[row], sems.at[group, row]
            )
            copy.start()
            copies.append(copy)
    for copy in copies:
        copy.wait()


def local(three_index, density, screen, pair_shells, home_slot, mirror_slot):
    blocks, pairs, aux_dev = three_index.shape
    ndens = density.shape[2]
    shell = math.isqrt(pairs)
    n = lax.axis_size("pair")
    cores = lax.axis_size("aux")
    me = lax.axis_index("pair")
    core = lax.axis_index("aux")
    half = ndens // cores
    part = pairs // 2
    width = aux_dev // n
    cap = 2 + (blocks - 1) // n
    bf16, f32 = jnp.bfloat16, jnp.float32
    in_vmem = pl.BlockSpec(memory_space=pltpu.VMEM)
    anywhere = pl.BlockSpec(memory_space=pl.ANY)
    ints = functools.partial(jnp.concatenate, axis=0)

    def call(kernel, name, table, args, out_shape, out_specs, ready=(), scratch=()):
        return pl.pallas_call(
            kernel,
            out_shape=out_shape,
            grid_spec=pltpu.PrefetchScalarGridSpec(
                num_scalar_prefetch=1,
                grid=(),
                in_specs=[in_vmem] * len(args) + [anywhere] * len(ready),
                out_specs=out_specs,
                scratch_shapes=list(scratch),
            ),
            compiler_params=pltpu.CompilerParams(vmem_limit_bytes=VMEM_BYTES),
            name=name,
        )(table, *args, *ready)

    def shift(x, d):
        return lax.ppermute(x, "pair", [(s, (s + d) % n) for s in range(n)])

    def flip(x, bit):
        return lax.ppermute(x, "pair", [(s, s ^ bit) for s in range(n)])

    def swap(x):
        return lax.ppermute(x, "aux", [(s, (s + 1) % cores) for s in range(cores)])

    def after(x, *others):
        return lax.optimization_barrier((x, *others))[0]

    def slots(peers, ranks, device):
        return slots_of(peers ^ device, ranks, n, cap)

    home_held, home_passed, home_rows = tables(home_slot, n, blocks, me)
    send_table = ints(
        [slots_of((home_rows[0] - me) % n, home_rows[1], n, cap), core[None].astype(jnp.int32)]
    )
    pick_table = slots_of((me - home_held[0]) % n, home_held[1], n, cap)
    chunk_table = me ^ jnp.arange(n, dtype=jnp.int32)
    weight = jnp.where(pair_shells[:, 0] != pair_shells[:, 1], 2.0, 1.0)
    factor = (screen.astype(f32) * weight[:, None]).astype(bf16)[:, None, :]
    keeping = screen.astype(f32)[:, None, :]

    sends = pl.pallas_call(
        functools.partial(scatter_density_kernel, n, blocks, cap),
        out_shape=[jax.ShapeDtypeStruct((cap, half, pairs), bf16)] * n,
        grid_spec=pltpu.PrefetchScalarGridSpec(
            num_scalar_prefetch=1,
            grid=(1,),
            in_specs=[pl.BlockSpec((blocks, pairs, half), lambda i, t: (0, 0, t[n * cap]))],
            out_specs=[pl.BlockSpec((cap, half, pairs), lambda i, t: (0, 0, 0))] * n,
            scratch_shapes=[pltpu.VMEM((blocks, half, pairs), bf16)],
        ),
        compiler_params=pltpu.CompilerParams(vmem_limit_bytes=VMEM_BYTES),
        name="scatter_density",
    )(send_table, density)
    steps = sorted(range(1, n), key=lambda d: (min(d, n - d) > 1, abs(2 * d - n)))
    received = []
    for i, d in enumerate(steps):
        received.append(shift(after(sends[d], *received[: max(i - 4, 0)][-1:]), d))
    integrals = pl.pallas_call(
        load_kernel,
        out_shape=pltpu.VMEM((blocks, pairs, aux_dev), bf16),
        in_specs=[anywhere, anywhere],
        out_specs=in_vmem,
        scratch_shapes=[pltpu.SemaphoreType.DMA],
        compiler_params=pltpu.CompilerParams(vmem_limit_bytes=2 * 1024 * 1024),
        name="load_integrals",
    )(three_index, received[1])
    received.append(sends[0])
    steps = (*steps, 0)
    own = call(
        functools.partial(gather_density_kernel, steps, cap),
        "gather_density",
        pick_table,
        received,
        jax.ShapeDtypeStruct((blocks, half, pairs), bf16),
        in_vmem,
        [integrals],
    )
    other = swap(own)

    mirror_held, mirror_passed, mirror_rows = tables(after(mirror_slot, own), n, blocks, me)
    out_table = ints([slots(*home_held, me), slots(*mirror_held, me)])
    pass_table = ints([slots(*held, me ^ (n // 2)) for held in (home_passed, mirror_passed)])
    in_table = ints([slots(*home_rows, me), slots(*mirror_rows, me)])

    bits = [1 << j for j in range(n.bit_length() - 1)]
    orders = (bits[1::-1] + bits[2:], bits)

    def fit(value, bits, ready=()):
        return call(
            functools.partial(fit_kernel, bits, blocks),
            "fit",
            chunk_table,
            [factor, value, integrals],
            [
                jax.ShapeDtypeStruct((n // 2, half, width), f32),
                jax.ShapeDtypeStruct((n // 2, half, width), bf16),
            ],
            [in_vmem] * 2,
            ready,
        )

    def step_together(states):
        flat, tree = jax.tree.flatten(states)
        return jax.tree.unflatten(tree, lax.optimization_barrier(flat))

    def totals(states):
        last = len(bits) - 1
        for j in range(last):
            states = step_together(states)
            found = []
            for (keep, send), order in zip(states, orders):
                value = keep + flip(send, order[j]).astype(f32)
                if j < last - 1:
                    found.append((value[0::2], value[1::2].astype(bf16)))
                else:
                    turned = jnp.concatenate([value[1:], value[:1]], axis=0)
                    found.append((value, turned.astype(bf16)))
            states = found
        states = step_together(states)
        states = [
            (keep + flip(send, order[last]).astype(f32)).astype(bf16)
            for (keep, send), order in zip(states, orders)
        ]
        relative = [[0, order[last]] for order in orders]
        for j in reversed(range(last)):
            states = step_together(states)
            fars = [flip(near, order[j]) for near, order in zip(states, orders)]
            relative = [r + [e ^ order[j] for e in r] for r, order in zip(relative, orders)]
            if j == 0:
                return [(*pair, r) for pair, r in zip(zip(states, fars), relative)]
            states = [jnp.concatenate(pair, axis=0) for pair in zip(states, fars)]

    fit_own = fit(own, orders[1])
    fit_other = fit(other, orders[0], fit_own[:1])
    (near_other, far_other, order_other), (near_own, far_own, order_own) = totals(
        [tuple(fit_other), tuple(fit_own)]
    )

    mine, theirs = call(
        functools.partial(apply_kernel, (order_own, order_other), blocks // 2),
        "apply",
        chunk_table,
        [integrals, near_own, far_own, near_other, far_other],
        [
            jax.ShapeDtypeStruct((blocks, half, pairs), f32),
            jax.ShapeDtypeStruct((blocks, half, pairs), bf16),
        ],
        [in_vmem] * 2,
    )
    sends = call(
        functools.partial(scatter_coulomb_kernel, n, blocks, cap),
        "scatter_coulomb",
        out_table,
        [keeping, mine, swap(theirs)],
        [jax.ShapeDtypeStruct((2 * cap, half, pairs), bf16)] * (n // 2)
        + [jax.ShapeDtypeStruct((2 * cap, half, part), bf16)] * (n // 2)
        + [jax.ShapeDtypeStruct((blocks, half, part), bf16)],
        [in_vmem] * (n + 1),
        scratch=[pltpu.VMEM((blocks, half, pairs), bf16)],
    )
    def direct(i, *ready):
        return flip(after(sends[n // 2 + i], *ready), n // 2 + i)

    whole = flip(sends[n], n // 2)
    near = [sends[0], flip(sends[1], 1), flip(sends[2], 2)]
    for d in range(3, n // 2):
        near.append(flip(after(sends[d], near[d - 1]), d))
    far = [direct(0), direct(1, near[1]), direct(2, near[2])]
    passed = call(
        functools.partial(pass_on_kernel, n, cap),
        "pass_on",
        pass_table,
        [whole],
        [jax.ShapeDtypeStruct((2 * cap, half, part), bf16)] * (n // 2),
        [in_vmem] * (n // 2),
        near[1:3],
    )
    passed = [passed[0]] + [flip(passed[d], d) for d in range(1, n // 2)]
    for i in range(3, n // 2):
        far.append(direct(i, passed[i - 2]))
    return call(
        functools.partial(gather_coulomb_kernel, n, blocks, shell, cap),
        "gather_coulomb",
        in_table,
        [*near, *passed, *far],
        [jax.ShapeDtypeStruct((blocks, pairs, half), bf16)] * 2,
        [anywhere] * 2,
        scratch=[
            pltpu.VMEM((2, blocks, half, pairs), bf16),
            pltpu.VMEM((2, blocks, pairs, half), bf16),
            pltpu.SemaphoreType.DMA((2, blocks)),
        ],
    )


def solution(mesh):
    in_specs = (
        P(("mol", "pair"), None, "aux"),
        P(("mol", "pair"), None, None),
        P(("mol", "pair"), None),
        P(("mol", "pair"), None),
        P("mol"),
        P("mol"),
    )
    out_specs = (P(("mol", "pair"), None, "aux"), P(("mol", "pair"), None, "aux"))
    return jax.shard_map(local, mesh=mesh, in_specs=in_specs, out_specs=out_specs, check_vma=False)
```

```python
import functools
import math

import jax
import jax.numpy as jnp
from jax import lax
from jax.experimental import pallas as pl
from jax.experimental.pallas import tpu as pltpu
from jax.sharding import PartitionSpec as P

VMEM_BYTES = 20 * 1024 * 1024


def tables(slots, devices, blocks_dev, me):
    total = slots.shape[0]
    numbers = jnp.arange(total, dtype=jnp.int32)
    source = numbers // blocks_dev
    target = slots // blocks_dev
    joined = source * devices + target
    earlier = (joined[:, None] == joined[None, :]) & (numbers[None, :] < numbers[:, None])
    rank = jnp.sum(earlier.astype(jnp.int32), axis=1)
    held = []
    for device in (me, me ^ (devices // 2)):
        for values in (target, rank):
            held.append(lax.dynamic_slice_in_dim(values, device * blocks_dev, blocks_dev, 0))
    rows = me * blocks_dev + jnp.arange(blocks_dev, dtype=jnp.int32)
    hot = slots[None, :] == rows[:, None]
    row_source = jnp.sum(jnp.where(hot, source[None, :], 0), axis=1)
    row_rank = jnp.sum(jnp.where(hot, rank[None, :], 0), axis=1)
    return held[:2], held[2:], (row_source, row_rank)


def slots_of(steps, ranks, devices, cap):
    held = (steps * cap + ranks)[None, :] == jnp.arange(devices * cap, dtype=jnp.int32)[:, None]
    numbers = jnp.arange(steps.shape[0], dtype=jnp.int32)
    return jnp.max(jnp.where(held, numbers[None, :], -1), axis=1)


def load_kernel(source, ready, target, sem):
    copy = pltpu.make_async_copy(source, target, sem)
    copy.start()
    copy.wait()


def scatter_density_kernel(devices, blocks, cap, table, density, *rest):
    sends, turned = rest[:devices], rest[-1]
    for row in range(blocks):
        turned[row] = density[row].T
    for step in range(devices):
        for rank in range(cap):
            row = jnp.maximum(table[step * cap + rank], 0)
            sends[step][rank] = turned[row]


def gather_density_kernel(steps, cap, table, *rest):
    out = rest[-1]
    for step, piece in zip(steps, rest):
        for rank in range(cap):
            row = table[step * cap + rank]

            @pl.when(row >= 0)
            def _():
                out[row] = piece[rank]


def fit_kernel(bits, blocks, table, factor, density, integrals, *rest):
    keep, send = rest[-2:]
    width = keep.shape[2]
    pairs = integrals.shape[1]
    fitted = jnp.concatenate([density[b] * factor[b] for b in range(blocks)], axis=1)
    for i in range(keep.shape[0]):
        e = sum(bit for j, bit in enumerate(bits[1:]) if i >> j & 1)
        for relative, out in ((e ^ bits[0], send), (e, keep)):
            at = pl.ds(pl.multiple_of(table[relative] * width, width), width)
            out[i] = jnp.dot(
                fitted,
                integrals[:, :, at].reshape(blocks * pairs, width),
                preferred_element_type=jnp.float32,
            ).astype(out.dtype)


def apply_kernel(orders, some, table, integrals, near, far, near_other, far_other, own, other):
    blocks, pairs, half = integrals.shape[0], integrals.shape[1], own.shape[1]
    count, _, width = near.shape
    chunks = []
    for order, low, high in ((orders[0], near, far), (orders[1], near_other, far_other)):
        chunks.append({e: (low, i) if i < count else (high, i - count) for i, e in enumerate(order)})
    for first in range(0, blocks, some):
        total = None
        for e in range(2 * count):
            at = pl.ds(pl.multiple_of(table[e] * width, width), width)
            term = lax.dot_general(
                integrals[first : first + some, :, at].reshape(some * pairs, width),
                jnp.concatenate([piece[e][0][piece[e][1]] for piece in chunks], axis=0),
                (((1,), (1,)), ((), ())),
                preferred_element_type=jnp.float32,
            )
            total = term if total is None else total + term
        for b in range(some):
            value = total[b * pairs : (b + 1) * pairs].T
            own[first + b] = value[:half]
            other[first + b] = value[half:].astype(other.dtype)


def scatter_coulomb_kernel(devices, blocks, cap, table, screen, own, other, *rest):
    near, far, whole, ready = rest[: devices // 2], rest[devices // 2 : devices], rest[-2], rest[-1]
    part = whole.shape[2]
    for b in range(blocks):
        value = (own[b] + other[b].astype(jnp.float32)) * screen[b]
        ready[b] = value.astype(jnp.bfloat16)
        whole[b] = ready[b, :, pl.ds(0, part)]
    for group in range(2):
        for step in range(devices):
            for rank in range(cap):
                b = jnp.maximum(table[(group * devices + step) * cap + rank], 0)
                if step < devices // 2:
                    near[step][group * cap + rank] = ready[b]
                else:
                    far[step - devices // 2][group * cap + rank] = ready[b, :, pl.ds(part, part)]


def pass_on_kernel(devices, cap, table, whole, *rest):
    outs = rest[-(devices // 2) :]
    for group in range(2):
        for step in range(devices // 2):
            for rank in range(cap):
                b = jnp.maximum(table[(group * devices + devices // 2 + step) * cap + rank], 0)
                outs[step][group * cap + rank] = whole[b]


def gather_coulomb_kernel(devices, blocks, shell, cap, table, *rest):
    half = devices // 2
    near, passed, far = rest[:half], rest[half:devices], rest[devices : devices + half]
    rows, cols, landed, done, sems = rest[devices + half :]
    pairs = landed.shape[3]
    part = far[0].shape[2]
    for step in range(devices):
        for group in range(2):
            for rank in range(cap):
                row = table[(group * devices + step) * cap + rank]
                at = group * cap + rank

                @pl.when(row >= 0)
                def _():
                    if step < half:
                        landed[group, row] = near[step][at]
                    else:
                        landed[group, row, :, pl.ds(0, part)] = passed[step - half][at]
                        landed[group, row, :, pl.ds(part, part)] = far[step - half][at]

    to = lax.broadcasted_iota(jnp.int32, (pairs, pairs), 0)
    source = lax.broadcasted_iota(jnp.int32, (pairs, pairs), 1)
    turns = (to, (to % shell) * shell + to // shell)
    copies = []
    for group in range(2):
        turn = (source == turns[group]).astype(jnp.bfloat16)
        for row in range(blocks):
            done[group, row] = lax.dot_general(
                turn,
                landed[group, row],
                (((1,), (1,)), ((), ())),
                preferred_element_type=jnp.float32,
            ).astype(jnp.bfloat16)
            copy = pltpu.make_async_copy(
                done.at[group, row], (rows, cols)[group].at[row], sems.at[group, row]
            )
            copy.start()
            copies.append(copy)
    for copy in copies:
        copy.wait()


def local(three_index, density, screen, pair_shells, home_slot, mirror_slot):
    blocks, pairs, aux_dev = three_index.shape
    ndens = density.shape[2]
    shell = math.isqrt(pairs)
    n = lax.axis_size("pair")
    cores = lax.axis_size("aux")
    me = lax.axis_index("pair")
    core = lax.axis_index("aux")
    half = ndens // cores
    part = pairs // 2
    width = aux_dev // n
    cap = 2 + (blocks - 1) // n
    bf16, f32 = jnp.bfloat16, jnp.float32
    in_vmem = pl.BlockSpec(memory_space=pltpu.VMEM)
    anywhere = pl.BlockSpec(memory_space=pl.ANY)
    ints = functools.partial(jnp.concatenate, axis=0)

    def call(kernel, name, table, args, out_shape, out_specs, ready=(), scratch=()):
        return pl.pallas_call(
            kernel,
            out_shape=out_shape,
            grid_spec=pltpu.PrefetchScalarGridSpec(
                num_scalar_prefetch=1,
                grid=(),
                in_specs=[in_vmem] * len(args) + [anywhere] * len(ready),
                out_specs=out_specs,
                scratch_shapes=list(scratch),
            ),
            compiler_params=pltpu.CompilerParams(vmem_limit_bytes=VMEM_BYTES),
            name=name,
        )(table, *args, *ready)

    def shift(x, d):
        return lax.ppermute(x, "pair", [(s, (s + d) % n) for s in range(n)])

    def flip(x, bit):
        return lax.ppermute(x, "pair", [(s, s ^ bit) for s in range(n)])

    def swap(x):
        return lax.ppermute(x, "aux", [(s, (s + 1) % cores) for s in range(cores)])

    def after(x, *others):
        return lax.optimization_barrier((x, *others))[0]

    def slots(peers, ranks, device):
        return slots_of(peers ^ device, ranks, n, cap)

    home_held, home_passed, home_rows = tables(home_slot, n, blocks, me)
    send_table = ints(
        [slots_of((home_rows[0] - me) % n, home_rows[1], n, cap), core[None].astype(jnp.int32)]
    )
    pick_table = slots_of((me - home_held[0]) % n, home_held[1], n, cap)
    chunk_table = me ^ jnp.arange(n, dtype=jnp.int32)
    weight = jnp.where(pair_shells[:, 0] != pair_shells[:, 1], 2.0, 1.0)
    factor = (screen.astype(f32) * weight[:, None]).astype(bf16)[:, None, :]
    keeping = screen.astype(f32)[:, None, :]

    sends = pl.pallas_call(
        functools.partial(scatter_density_kernel, n, blocks, cap),
        out_shape=[jax.ShapeDtypeStruct((cap, half, pairs), bf16)] * n,
        grid_spec=pltpu.PrefetchScalarGridSpec(
            num_scalar_prefetch=1,
            grid=(1,),
            in_specs=[pl.BlockSpec((blocks, pairs, half), lambda i, t: (0, 0, t[n * cap]))],
            out_specs=[pl.BlockSpec((cap, half, pairs), lambda i, t: (0, 0, 0))] * n,
            scratch_shapes=[pltpu.VMEM((blocks, half, pairs), bf16)],
        ),
        compiler_params=pltpu.CompilerParams(vmem_limit_bytes=VMEM_BYTES),
        name="scatter_density",
    )(send_table, density)
    steps = sorted(range(1, n), key=lambda d: (min(d, n - d) > 1, abs(2 * d - n)))
    received = []
    for i, d in enumerate(steps):
        received.append(shift(after(sends[d], *received[: max(i - 4, 0)][-1:]), d))
    integrals = pl.pallas_call(
        load_kernel,
        out_shape=pltpu.VMEM((blocks, pairs, aux_dev), bf16),
        in_specs=[anywhere, anywhere],
        out_specs=in_vmem,
        scratch_shapes=[pltpu.SemaphoreType.DMA],
        compiler_params=pltpu.CompilerParams(vmem_limit_bytes=2 * 1024 * 1024),
        name="load_integrals",
    )(three_index, received[1])
    received.append(sends[0])
    steps = (*steps, 0)
    own = call(
        functools.partial(gather_density_kernel, steps, cap),
        "gather_density",
        pick_table,
        received,
        jax.ShapeDtypeStruct((blocks, half, pairs), bf16),
        in_vmem,
        [integrals],
    )
    other = swap(own)

    mirror_held, mirror_passed, mirror_rows = tables(after(mirror_slot, own), n, blocks, me)
    out_table = ints([slots(*home_held, me), slots(*mirror_held, me)])
    pass_table = ints([slots(*held, me ^ (n // 2)) for held in (home_passed, mirror_passed)])
    in_table = ints([slots(*home_rows, me), slots(*mirror_rows, me)])

    bits = [1 << j for j in range(n.bit_length() - 1)]
    orders = (bits, bits[1::-1] + bits[2:])

    def fit(value, bits, ready=()):
        return call(
            functools.partial(fit_kernel, bits, blocks),
            "fit",
            chunk_table,
            [factor, value, integrals],
            [
                jax.ShapeDtypeStruct((n // 2, half, width), f32),
                jax.ShapeDtypeStruct((n // 2, half, width), bf16),
            ],
            [in_vmem] * 2,
            ready,
        )

    def totals(parts):
        last = len(bits) - 1
        parts, marks = list(parts), ([], [])
        relative = [[0, order[last]] for order in orders]
        for j in range(2 * last + 1):
            for c, order in enumerate(orders):
                lag = j - 2 + c
                bit = order[min(j, 2 * last - j)]
                ready = [marks[1 - c][lag]] if lag >= 0 else [parts[1][1]] if lag == -1 and j else []
                if j <= last:
                    keep, send = parts[c]
                    value = keep + flip(after(send, *ready), bit).astype(f32)
                if j < last - 1:
                    parts[c] = (value[0::2], value[1::2].astype(bf16))
                elif j == last - 1:
                    turned = jnp.concatenate([value[1:], value[:1]], axis=0)
                    parts[c] = (value, turned.astype(bf16))
                elif j == last:
                    parts[c] = (None, value.astype(bf16))
                else:
                    near = after(parts[c][1], *ready)
                    far = flip(near, bit)
                    relative[c] = relative[c] + [e ^ bit for e in relative[c]]
                    both = (near, far) if j == 2 * last else (jnp.concatenate([near, far], axis=0),)
                    parts[c] = (both[0], both[-1])
                marks[c].append(parts[c][1])
        return [(*pair, order) for pair, order in zip(parts, relative)]

    fit_own = fit(own, orders[0])
    fit_other = fit(other, orders[1], fit_own[:1])
    (near_own, far_own, order_own), (near_other, far_other, order_other) = totals(
        [tuple(fit_own), tuple(fit_other)]
    )

    mine, theirs = call(
        functools.partial(apply_kernel, (order_own, order_other), blocks // 2),
        "apply",
        chunk_table,
        [integrals, near_own, far_own, near_other, far_other],
        [
            jax.ShapeDtypeStruct((blocks, half, pairs), f32),
            jax.ShapeDtypeStruct((blocks, half, pairs), bf16),
        ],
        [in_vmem] * 2,
    )
    sends = call(
        functools.partial(scatter_coulomb_kernel, n, blocks, cap),
        "scatter_coulomb",
        out_table,
        [keeping, mine, swap(theirs)],
        [jax.ShapeDtypeStruct((2 * cap, half, pairs), bf16)] * (n // 2)
        + [jax.ShapeDtypeStruct((2 * cap, half, part), bf16)] * (n // 2)
        + [jax.ShapeDtypeStruct((blocks, half, part), bf16)],
        [in_vmem] * (n + 1),
        scratch=[pltpu.VMEM((blocks, half, pairs), bf16)],
    )
    def direct(i, *ready):
        return flip(after(sends[n // 2 + i], *ready), n // 2 + i)

    whole = flip(sends[n], n // 2)
    near = [sends[0], flip(sends[1], 1), flip(sends[2], 2)]
    for d in range(3, n // 2):
        near.append(flip(after(sends[d], near[d - 1]), d))
    far = [direct(0), direct(1, near[1]), direct(2, near[2])]
    passed = call(
        functools.partial(pass_on_kernel, n, cap),
        "pass_on",
        pass_table,
        [whole],
        [jax.ShapeDtypeStruct((2 * cap, half, part), bf16)] * (n // 2),
        [in_vmem] * (n // 2),
        near[1:3],
    )
    passed = [passed[0]] + [flip(passed[d], d) for d in range(1, n // 2)]
    for i in range(3, n // 2):
        far.append(direct(i, passed[i - 2]))
    return call(
        functools.partial(gather_coulomb_kernel, n, blocks, shell, cap),
        "gather_coulomb",
        in_table,
        [*near, *passed, *far],
        [jax.ShapeDtypeStruct((blocks, pairs, half), bf16)] * 2,
        [anywhere] * 2,
        scratch=[
            pltpu.VMEM((2, blocks, half, pairs), bf16),
            pltpu.VMEM((2, blocks, pairs, half), bf16),
            pltpu.SemaphoreType.DMA((2, blocks)),
        ],
    )


def solution(mesh):
    in_specs = (
        P(("mol", "pair"), None, "aux"),
        P(("mol", "pair"), None, None),
        P(("mol", "pair"), None),
        P(("mol", "pair"), None),
        P("mol"),
        P("mol"),
    )
    out_specs = (P(("mol", "pair"), None, "aux"), P(("mol", "pair"), None, "aux"))
    return jax.shard_map(local, mesh=mesh, in_specs=in_specs, out_specs=out_specs, check_vma=False)
```

```python
import functools
import math

import jax
import jax.numpy as jnp
from jax import lax
from jax.experimental import pallas as pl
from jax.experimental.pallas import tpu as pltpu
from jax.sharding import PartitionSpec as P

VMEM_BYTES = 20 * 1024 * 1024


def tables(slots, devices, blocks_dev, me):
    total = slots.shape[0]
    numbers = jnp.arange(total, dtype=jnp.int32)
    source = numbers // blocks_dev
    target = slots // blocks_dev
    joined = source * devices + target
    earlier = (joined[:, None] == joined[None, :]) & (numbers[None, :] < numbers[:, None])
    rank = jnp.sum(earlier.astype(jnp.int32), axis=1)
    held = []
    for device in (me, me ^ (devices // 2)):
        for values in (target, rank):
            held.append(lax.dynamic_slice_in_dim(values, device * blocks_dev, blocks_dev, 0))
    rows = me * blocks_dev + jnp.arange(blocks_dev, dtype=jnp.int32)
    hot = slots[None, :] == rows[:, None]
    row_source = jnp.sum(jnp.where(hot, source[None, :], 0), axis=1)
    row_rank = jnp.sum(jnp.where(hot, rank[None, :], 0), axis=1)
    return held[:2], held[2:], (row_source, row_rank)


def slots_of(steps, ranks, devices, cap):
    held = (steps * cap + ranks)[None, :] == jnp.arange(devices * cap, dtype=jnp.int32)[:, None]
    numbers = jnp.arange(steps.shape[0], dtype=jnp.int32)
    return jnp.max(jnp.where(held, numbers[None, :], -1), axis=1)


def load_kernel(source, ready, target, sem):
    copy = pltpu.make_async_copy(source, target, sem)
    copy.start()
    copy.wait()


def scatter_density_kernel(devices, blocks, cap, table, density, *rest):
    sends, turned = rest[:devices], rest[-1]
    for row in range(blocks):
        turned[row] = density[row].T
    for step in range(devices):
        for rank in range(cap):
            row = jnp.maximum(table[step * cap + rank], 0)
            sends[step][rank] = turned[row]


def gather_density_kernel(steps, cap, table, *rest):
    out = rest[-1]
    for step, piece in zip(steps, rest):
        for rank in range(cap):
            row = table[step * cap + rank]

            @pl.when(row >= 0)
            def _():
                out[row] = piece[rank]


def fit_kernel(bits, blocks, table, factor, density, integrals, *rest):
    keep, send = rest[-2:]
    width = keep.shape[2]
    pairs = integrals.shape[1]
    fitted = jnp.concatenate([density[b] * factor[b] for b in range(blocks)], axis=1)
    for i in range(keep.shape[0]):
        e = sum(bit for j, bit in enumerate(bits[1:]) if i >> j & 1)
        for relative, out in ((e ^ bits[0], send), (e, keep)):
            at = pl.ds(pl.multiple_of(table[relative] * width, width), width)
            out[i] = jnp.dot(
                fitted,
                integrals[:, :, at].reshape(blocks * pairs, width),
                preferred_element_type=jnp.float32,
            ).astype(out.dtype)


def apply_kernel(orders, some, table, integrals, near, far, near_other, far_other, own, other):
    blocks, pairs, half = integrals.shape[0], integrals.shape[1], own.shape[1]
    count, _, width = near.shape
    chunks = []
    for order, low, high in ((orders[0], near, far), (orders[1], near_other, far_other)):
        chunks.append({e: (low, i) if i < count else (high, i - count) for i, e in enumerate(order)})
    for first in range(0, blocks, some):
        total = None
        for e in range(2 * count):
            at = pl.ds(pl.multiple_of(table[e] * width, width), width)
            term = lax.dot_general(
                integrals[first : first + some, :, at].reshape(some * pairs, width),
                jnp.concatenate([piece[e][0][piece[e][1]] for piece in chunks], axis=0),
                (((1,), (1,)), ((), ())),
                preferred_element_type=jnp.float32,
            )
            total = term if total is None else total + term
        for b in range(some):
            value = total[b * pairs : (b + 1) * pairs].T
            own[first + b] = value[:half]
            other[first + b] = value[half:].astype(other.dtype)


def scatter_coulomb_kernel(devices, blocks, cap, table, screen, own, other, *rest):
    near, far, whole, ready = rest[: devices // 2], rest[devices // 2 : devices], rest[-2], rest[-1]
    part = whole.shape[2]
    for b in range(blocks):
        value = (own[b] + other[b].astype(jnp.float32)) * screen[b]
        ready[b] = value.astype(jnp.bfloat16)
        whole[b] = ready[b, :, pl.ds(0, part)]
    for group in range(2):
        for step in range(devices):
            for rank in range(cap):
                b = jnp.maximum(table[(group * devices + step) * cap + rank], 0)
                if step < devices // 2:
                    near[step][group * cap + rank] = ready[b]
                else:
                    far[step - devices // 2][group * cap + rank] = ready[b, :, pl.ds(part, part)]


def pass_on_kernel(devices, cap, table, whole, *rest):
    outs = rest[-(devices // 2) :]
    for group in range(2):
        for step in range(devices // 2):
            for rank in range(cap):
                b = jnp.maximum(table[(group * devices + devices // 2 + step) * cap + rank], 0)
                outs[step][group * cap + rank] = whole[b]


def gather_coulomb_kernel(devices, blocks, shell, cap, table, *rest):
    half = devices // 2
    near, passed, far = rest[:half], rest[half:devices], rest[devices : devices + half]
    rows, cols, landed, done, sems = rest[devices + half :]
    pairs = landed.shape[3]
    part = far[0].shape[2]
    for step in range(devices):
        for group in range(2):
            for rank in range(cap):
                row = table[(group * devices + step) * cap + rank]
                at = group * cap + rank

                @pl.when(row >= 0)
                def _():
                    if step < half:
                        landed[group, row] = near[step][at]
                    else:
                        landed[group, row, :, pl.ds(0, part)] = passed[step - half][at]
                        landed[group, row, :, pl.ds(part, part)] = far[step - half][at]

    to = lax.broadcasted_iota(jnp.int32, (pairs, pairs), 0)
    source = lax.broadcasted_iota(jnp.int32, (pairs, pairs), 1)
    turns = (to, (to % shell) * shell + to // shell)
    copies = []
    for group in range(2):
        turn = (source == turns[group]).astype(jnp.bfloat16)
        for row in range(blocks):
            done[group, row] = lax.dot_general(
                turn,
                landed[group, row],
                (((1,), (1,)), ((), ())),
                preferred_element_type=jnp.float32,
            ).astype(jnp.bfloat16)
            copy = pltpu.make_async_copy(
                done.at[group, row], (rows, cols)[group].at[row], sems.at[group, row]
            )
            copy.start()
            copies.append(copy)
    for copy in copies:
        copy.wait()


def local(three_index, density, screen, pair_shells, home_slot, mirror_slot):
    blocks, pairs, aux_dev = three_index.shape
    ndens = density.shape[2]
    shell = math.isqrt(pairs)
    n = lax.axis_size("pair")
    cores = lax.axis_size("aux")
    me = lax.axis_index("pair")
    core = lax.axis_index("aux")
    half = ndens // cores
    part = pairs // 2
    width = aux_dev // n
    cap = 2 + (blocks - 1) // n
    bf16, f32 = jnp.bfloat16, jnp.float32
    in_vmem = pl.BlockSpec(memory_space=pltpu.VMEM)
    anywhere = pl.BlockSpec(memory_space=pl.ANY)
    ints = functools.partial(jnp.concatenate, axis=0)

    def call(kernel, name, table, args, out_shape, out_specs, ready=(), scratch=()):
        return pl.pallas_call(
            kernel,
            out_shape=out_shape,
            grid_spec=pltpu.PrefetchScalarGridSpec(
                num_scalar_prefetch=1,
                grid=(),
                in_specs=[in_vmem] * len(args) + [anywhere] * len(ready),
                out_specs=out_specs,
                scratch_shapes=list(scratch),
            ),
            compiler_params=pltpu.CompilerParams(vmem_limit_bytes=VMEM_BYTES),
            name=name,
        )(table, *args, *ready)

    def shift(x, d):
        return lax.ppermute(x, "pair", [(s, (s + d) % n) for s in range(n)])

    def flip(x, bit):
        return lax.ppermute(x, "pair", [(s, s ^ bit) for s in range(n)])

    def swap(x):
        return lax.ppermute(x, "aux", [(s, (s + 1) % cores) for s in range(cores)])

    def after(x, *others):
        return lax.optimization_barrier((x, *others))[0]

    def slots(peers, ranks, device):
        return slots_of(peers ^ device, ranks, n, cap)

    home_held, home_passed, home_rows = tables(home_slot, n, blocks, me)
    send_table = ints(
        [slots_of((home_rows[0] - me) % n, home_rows[1], n, cap), core[None].astype(jnp.int32)]
    )
    pick_table = slots_of((me - home_held[0]) % n, home_held[1], n, cap)
    chunk_table = me ^ jnp.arange(n, dtype=jnp.int32)
    weight = jnp.where(pair_shells[:, 0] != pair_shells[:, 1], 2.0, 1.0)
    factor = (screen.astype(f32) * weight[:, None]).astype(bf16)[:, None, :]
    keeping = screen.astype(f32)[:, None, :]

    sends = pl.pallas_call(
        functools.partial(scatter_density_kernel, n, blocks, cap),
        out_shape=[jax.ShapeDtypeStruct((cap, half, pairs), bf16)] * n,
        grid_spec=pltpu.PrefetchScalarGridSpec(
            num_scalar_prefetch=1,
            grid=(1,),
            in_specs=[pl.BlockSpec((blocks, pairs, half), lambda i, t: (0, 0, t[n * cap]))],
            out_specs=[pl.BlockSpec((cap, half, pairs), lambda i, t: (0, 0, 0))] * n,
            scratch_shapes=[pltpu.VMEM((blocks, half, pairs), bf16)],
        ),
        compiler_params=pltpu.CompilerParams(vmem_limit_bytes=VMEM_BYTES),
        name="scatter_density",
    )(send_table, density)
    steps = sorted(range(1, n), key=lambda d: (min(d, n - d) > 1, abs(2 * d - n)))
    received = []
    for i, d in enumerate(steps):
        received.append(shift(after(sends[d], *received[: max(i - 4, 0)][-1:]), d))
    integrals = pl.pallas_call(
        load_kernel,
        out_shape=pltpu.VMEM((blocks, pairs, aux_dev), bf16),
        in_specs=[anywhere, anywhere],
        out_specs=in_vmem,
        scratch_shapes=[pltpu.SemaphoreType.DMA],
        compiler_params=pltpu.CompilerParams(vmem_limit_bytes=2 * 1024 * 1024),
        name="load_integrals",
    )(three_index, received[1])
    received.append(sends[0])
    steps = (*steps, 0)
    own = call(
        functools.partial(gather_density_kernel, steps, cap),
        "gather_density",
        pick_table,
        received,
        jax.ShapeDtypeStruct((blocks, half, pairs), bf16),
        in_vmem,
        [integrals],
    )
    other = swap(own)

    mirror_held, mirror_passed, mirror_rows = tables(after(mirror_slot, own), n, blocks, me)
    out_table = ints([slots(*home_held, me), slots(*mirror_held, me)])
    pass_table = ints([slots(*held, me ^ (n // 2)) for held in (home_passed, mirror_passed)])
    in_table = ints([slots(*home_rows, me), slots(*mirror_rows, me)])

    bits = [1 << j for j in range(n.bit_length() - 1)]
    orders = (bits, bits[1::-1] + bits[2:])

    def fit(value, bits, ready=()):
        return call(
            functools.partial(fit_kernel, bits, blocks),
            "fit",
            chunk_table,
            [factor, value, integrals],
            [
                jax.ShapeDtypeStruct((n // 2, half, width), f32),
                jax.ShapeDtypeStruct((n // 2, half, width), bf16),
            ],
            [in_vmem] * 2,
            ready,
        )

    def totals(parts):
        last = len(bits) - 1
        parts, marks = list(parts), ([], [])
        relative = [[0, order[last]] for order in orders]
        for j in range(2 * last + 1):
            for c, order in enumerate(orders):
                lag = j - 2 + c
                bit = order[min(j, 2 * last - j)]
                ready = [marks[1 - c][lag]] if lag >= 0 else [parts[1][1]] if lag == -1 and j else []
                if j <= last:
                    keep, send = parts[c]
                    value = keep + flip(after(send, *ready), bit).astype(f32)
                if j < last - 1:
                    parts[c] = (value[0::2], value[1::2].astype(bf16))
                elif j == last - 1:
                    turned = jnp.concatenate([value[1:], value[:1]], axis=0)
                    parts[c] = (value, turned.astype(bf16))
                elif j == last:
                    parts[c] = (None, value.astype(bf16))
                else:
                    near = after(parts[c][1], *ready)
                    far = flip(near, bit)
                    relative[c] = relative[c] + [e ^ bit for e in relative[c]]
                    both = (near, far) if j == 2 * last else (jnp.concatenate([near, far], axis=0),)
                    parts[c] = (both[0], both[-1])
                marks[c].append(parts[c][1])
        return [(*pair, order) for pair, order in zip(parts, relative)]

    fit_own = fit(own, orders[0])
    fit_other = fit(other, orders[1], fit_own[:1])
    (near_own, far_own, order_own), (near_other, far_other, order_other) = totals(
        [tuple(fit_own), tuple(fit_other)]
    )

    mine, theirs = call(
        functools.partial(apply_kernel, (order_own, order_other), blocks // 2),
        "apply",
        chunk_table,
        [integrals, near_own, far_own, near_other, far_other],
        [
            jax.ShapeDtypeStruct((blocks, half, pairs), f32),
            jax.ShapeDtypeStruct((blocks, half, pairs), bf16),
        ],
        [in_vmem] * 2,
    )
    sends = call(
        functools.partial(scatter_coulomb_kernel, n, blocks, cap),
        "scatter_coulomb",
        out_table,
        [keeping, mine, swap(theirs)],
        [jax.ShapeDtypeStruct((2 * cap, half, pairs), bf16)] * (n // 2)
        + [jax.ShapeDtypeStruct((2 * cap, half, part), bf16)] * (n // 2)
        + [jax.ShapeDtypeStruct((blocks, half, part), bf16)],
        [in_vmem] * (n + 1),
        scratch=[pltpu.VMEM((blocks, half, pairs), bf16)],
    )
    def direct(i, *ready):
        return flip(after(sends[n // 2 + i], *ready), n // 2 + i)

    whole = flip(sends[n], n // 2)
    near = [sends[0], flip(sends[1], 1), flip(sends[2], 2)]
    for d in range(3, n // 2):
        near.append(flip(after(sends[d], near[d - 1]), d))
    far = [direct(0), direct(1, near[1]), direct(2, near[2])]
    passed = call(
        functools.partial(pass_on_kernel, n, cap),
        "pass_on",
        pass_table,
        [whole],
        [jax.ShapeDtypeStruct((2 * cap, half, part), bf16)] * (n // 2),
        [in_vmem] * (n // 2),
        near[1:3],
    )
    passed = [passed[0], flip(passed[1], 1)] + [
        flip(after(passed[d], far[min(d - 2, 1)]), d) for d in range(2, n // 2)
    ]
    for i in range(3, n // 2):
        far.append(direct(i, passed[i - 2]))
    return call(
        functools.partial(gather_coulomb_kernel, n, blocks, shell, cap),
        "gather_coulomb",
        in_table,
        [*near, *passed, *far],
        [jax.ShapeDtypeStruct((blocks, pairs, half), bf16)] * 2,
        [anywhere] * 2,
        scratch=[
            pltpu.VMEM((2, blocks, half, pairs), bf16),
            pltpu.VMEM((2, blocks, pairs, half), bf16),
            pltpu.SemaphoreType.DMA((2, blocks)),
        ],
    )


def solution(mesh):
    in_specs = (
        P(("mol", "pair"), None, "aux"),
        P(("mol", "pair"), None, None),
        P(("mol", "pair"), None),
        P(("mol", "pair"), None),
        P("mol"),
        P("mol"),
    )
    out_specs = (P(("mol", "pair"), None, "aux"), P(("mol", "pair"), None, "aux"))
    return jax.shard_map(local, mesh=mesh, in_specs=in_specs, out_specs=out_specs, check_vma=False)
```

```python
import functools
import math

import jax
import jax.numpy as jnp
from jax import lax
from jax.experimental import pallas as pl
from jax.experimental.pallas import tpu as pltpu
from jax.sharding import PartitionSpec as P

VMEM_BYTES = 20 * 1024 * 1024


def tables(slots, devices, blocks_dev, me):
    total = slots.shape[0]
    numbers = jnp.arange(total, dtype=jnp.int32)
    source = numbers // blocks_dev
    target = slots // blocks_dev
    joined = source * devices + target
    earlier = (joined[:, None] == joined[None, :]) & (numbers[None, :] < numbers[:, None])
    rank = jnp.sum(earlier.astype(jnp.int32), axis=1)
    held = []
    for device in (me, me ^ (devices // 2)):
        for values in (target, rank):
            held.append(lax.dynamic_slice_in_dim(values, device * blocks_dev, blocks_dev, 0))
    rows = me * blocks_dev + jnp.arange(blocks_dev, dtype=jnp.int32)
    hot = slots[None, :] == rows[:, None]
    row_source = jnp.sum(jnp.where(hot, source[None, :], 0), axis=1)
    row_rank = jnp.sum(jnp.where(hot, rank[None, :], 0), axis=1)
    return held[:2], held[2:], (row_source, row_rank)


def slots_of(steps, ranks, devices, cap):
    held = (steps * cap + ranks)[None, :] == jnp.arange(devices * cap, dtype=jnp.int32)[:, None]
    numbers = jnp.arange(steps.shape[0], dtype=jnp.int32)
    return jnp.max(jnp.where(held, numbers[None, :], -1), axis=1)


def load_kernel(source, ready, target, sem):
    copy = pltpu.make_async_copy(source, target, sem)
    copy.start()
    copy.wait()


def scatter_density_kernel(devices, blocks, cap, table, density, *rest):
    sends, turned = rest[:devices], rest[-1]
    for row in range(blocks):
        turned[row] = density[row].T
    for step in range(devices):
        for rank in range(cap):
            row = jnp.maximum(table[step * cap + rank], 0)
            sends[step][rank] = turned[row]


def gather_density_kernel(steps, cap, table, *rest):
    out = rest[-1]
    for step, piece in zip(steps, rest):
        for rank in range(cap):
            row = table[step * cap + rank]

            @pl.when(row >= 0)
            def _():
                out[row] = piece[rank]


def fit_kernel(bits, blocks, table, factor, density, integrals, *rest):
    keep, send = rest[-2:]
    width = keep.shape[2]
    pairs = integrals.shape[1]
    fitted = jnp.concatenate([density[b] * factor[b] for b in range(blocks)], axis=1)
    for i in range(keep.shape[0]):
        e = sum(bit for j, bit in enumerate(bits[1:]) if i >> j & 1)
        for relative, out in ((e ^ bits[0], send), (e, keep)):
            at = pl.ds(pl.multiple_of(table[relative] * width, width), width)
            out[i] = jnp.dot(
                fitted,
                integrals[:, :, at].reshape(blocks * pairs, width),
                preferred_element_type=jnp.float32,
            ).astype(out.dtype)


def apply_kernel(orders, first, table, integrals, near, far, near_other, far_other, *rest):
    own, other = rest[-2:]
    pairs, (some, half) = integrals.shape[1], own.shape[:2]
    count, _, width = near.shape
    chunks = []
    for order, low, high in ((orders[0], near, far), (orders[1], near_other, far_other)):
        chunks.append({e: (low, i) if i < count else (high, i - count) for i, e in enumerate(order)})
    total = None
    for e in range(2 * count):
        at = pl.ds(pl.multiple_of(table[e] * width, width), width)
        term = lax.dot_general(
            integrals[first : first + some, :, at].reshape(some * pairs, width),
            jnp.concatenate([piece[e][0][piece[e][1]] for piece in chunks], axis=0),
            (((1,), (1,)), ((), ())),
            preferred_element_type=jnp.float32,
        )
        total = term if total is None else total + term
    for b in range(some):
        value = total[b * pairs : (b + 1) * pairs].T
        own[b] = value[:half]
        other[b] = value[half:].astype(other.dtype)


def scatter_coulomb_kernel(devices, blocks, cap, table, screen, *rest):
    sums, rest = rest[:4], rest[4:]
    some = sums[0].shape[0]
    near, far, whole, ready = rest[: devices // 2], rest[devices // 2 : devices], rest[-2], rest[-1]
    part = whole.shape[2]
    for b in range(blocks):
        own, other = sums[b // some * 2 : b // some * 2 + 2]
        value = (own[b % some] + other[b % some].astype(jnp.float32)) * screen[b]
        ready[b] = value.astype(jnp.bfloat16)
        whole[b] = ready[b, :, pl.ds(0, part)]
    for group in range(2):
        for step in range(devices):
            for rank in range(cap):
                b = jnp.maximum(table[(group * devices + step) * cap + rank], 0)
                if step < devices // 2:
                    near[step][group * cap + rank] = ready[b]
                else:
                    far[step - devices // 2][group * cap + rank] = ready[b, :, pl.ds(part, part)]


def pass_on_kernel(devices, cap, table, whole, *rest):
    outs = rest[-(devices // 2) :]
    for group in range(2):
        for step in range(devices // 2):
            for rank in range(cap):
                b = jnp.maximum(table[(group * devices + devices // 2 + step) * cap + rank], 0)
                outs[step][group * cap + rank] = whole[b]


def gather_coulomb_kernel(devices, blocks, shell, cap, table, *rest):
    half = devices // 2
    near, passed, far = rest[:half], rest[half:devices], rest[devices : devices + half]
    rows, cols, landed, done, sems = rest[devices + half :]
    pairs = landed.shape[3]
    part = far[0].shape[2]
    for step in range(devices):
        for group in range(2):
            for rank in range(cap):
                row = table[(group * devices + step) * cap + rank]
                at = group * cap + rank

                @pl.when(row >= 0)
                def _():
                    if step < half:
                        landed[group, row] = near[step][at]
                    else:
                        landed[group, row, :, pl.ds(0, part)] = passed[step - half][at]
                        landed[group, row, :, pl.ds(part, part)] = far[step - half][at]

    to = lax.broadcasted_iota(jnp.int32, (pairs, pairs), 0)
    source = lax.broadcasted_iota(jnp.int32, (pairs, pairs), 1)
    turns = (to, (to % shell) * shell + to // shell)
    copies = []
    for group in range(2):
        turn = (source == turns[group]).astype(jnp.bfloat16)
        for row in range(blocks):
            done[group, row] = lax.dot_general(
                turn,
                landed[group, row],
                (((1,), (1,)), ((), ())),
                preferred_element_type=jnp.float32,
            ).astype(jnp.bfloat16)
            copy = pltpu.make_async_copy(
                done.at[group, row], (rows, cols)[group].at[row], sems.at[group, row]
            )
            copy.start()
            copies.append(copy)
    for copy in copies:
        copy.wait()


def local(three_index, density, screen, pair_shells, home_slot, mirror_slot):
    blocks, pairs, aux_dev = three_index.shape
    ndens = density.shape[2]
    shell = math.isqrt(pairs)
    n = lax.axis_size("pair")
    cores = lax.axis_size("aux")
    me = lax.axis_index("pair")
    core = lax.axis_index("aux")
    half = ndens // cores
    part = pairs // 2
    width = aux_dev // n
    cap = 2 + (blocks - 1) // n
    bf16, f32 = jnp.bfloat16, jnp.float32
    in_vmem = pl.BlockSpec(memory_space=pltpu.VMEM)
    anywhere = pl.BlockSpec(memory_space=pl.ANY)
    ints = functools.partial(jnp.concatenate, axis=0)

    def call(kernel, name, table, args, out_shape, out_specs, ready=(), scratch=()):
        return pl.pallas_call(
            kernel,
            out_shape=out_shape,
            grid_spec=pltpu.PrefetchScalarGridSpec(
                num_scalar_prefetch=1,
                grid=(),
                in_specs=[in_vmem] * len(args) + [anywhere] * len(ready),
                out_specs=out_specs,
                scratch_shapes=list(scratch),
            ),
            compiler_params=pltpu.CompilerParams(vmem_limit_bytes=VMEM_BYTES),
            name=name,
        )(table, *args, *ready)

    def shift(x, d):
        return lax.ppermute(x, "pair", [(s, (s + d) % n) for s in range(n)])

    def flip(x, bit):
        return lax.ppermute(x, "pair", [(s, s ^ bit) for s in range(n)])

    def swap(x):
        return lax.ppermute(x, "aux", [(s, (s + 1) % cores) for s in range(cores)])

    def after(x, *others):
        return lax.optimization_barrier((x, *others))[0]

    def slots(peers, ranks, device):
        return slots_of(peers ^ device, ranks, n, cap)

    home_held, home_passed, home_rows = tables(home_slot, n, blocks, me)
    send_table = ints(
        [slots_of((home_rows[0] - me) % n, home_rows[1], n, cap), core[None].astype(jnp.int32)]
    )
    pick_table = slots_of((me - home_held[0]) % n, home_held[1], n, cap)
    chunk_table = me ^ jnp.arange(n, dtype=jnp.int32)
    weight = jnp.where(pair_shells[:, 0] != pair_shells[:, 1], 2.0, 1.0)
    factor = (screen.astype(f32) * weight[:, None]).astype(bf16)[:, None, :]
    keeping = screen.astype(f32)[:, None, :]

    sends = pl.pallas_call(
        functools.partial(scatter_density_kernel, n, blocks, cap),
        out_shape=[jax.ShapeDtypeStruct((cap, half, pairs), bf16)] * n,
        grid_spec=pltpu.PrefetchScalarGridSpec(
            num_scalar_prefetch=1,
            grid=(1,),
            in_specs=[pl.BlockSpec((blocks, pairs, half), lambda i, t: (0, 0, t[n * cap]))],
            out_specs=[pl.BlockSpec((cap, half, pairs), lambda i, t: (0, 0, 0))] * n,
            scratch_shapes=[pltpu.VMEM((blocks, half, pairs), bf16)],
        ),
        compiler_params=pltpu.CompilerParams(vmem_limit_bytes=VMEM_BYTES),
        name="scatter_density",
    )(send_table, density)
    steps = sorted(range(1, n), key=lambda d: (min(d, n - d) > 1, abs(2 * d - n)))
    received = []
    for i, d in enumerate(steps):
        received.append(shift(after(sends[d], *received[: max(i - 4, 0)][-1:]), d))
    integrals = pl.pallas_call(
        load_kernel,
        out_shape=pltpu.VMEM((blocks, pairs, aux_dev), bf16),
        in_specs=[anywhere, anywhere],
        out_specs=in_vmem,
        scratch_shapes=[pltpu.SemaphoreType.DMA],
        compiler_params=pltpu.CompilerParams(vmem_limit_bytes=2 * 1024 * 1024),
        name="load_integrals",
    )(three_index, received[1])
    received.append(sends[0])
    steps = (*steps, 0)
    own = call(
        functools.partial(gather_density_kernel, steps, cap),
        "gather_density",
        pick_table,
        received,
        jax.ShapeDtypeStruct((blocks, half, pairs), bf16),
        in_vmem,
        [integrals],
    )
    other = swap(own)

    mirror_held, mirror_passed, mirror_rows = tables(after(mirror_slot, own), n, blocks, me)
    out_table = ints([slots(*home_held, me), slots(*mirror_held, me)])
    pass_table = ints([slots(*held, me ^ (n // 2)) for held in (home_passed, mirror_passed)])
    in_table = ints([slots(*home_rows, me), slots(*mirror_rows, me)])

    bits = [1 << j for j in range(n.bit_length() - 1)]
    orders = (bits, bits[1::-1] + bits[2:])

    def fit(value, bits, ready=()):
        return call(
            functools.partial(fit_kernel, bits, blocks),
            "fit",
            chunk_table,
            [factor, value, integrals],
            [
                jax.ShapeDtypeStruct((n // 2, half, width), f32),
                jax.ShapeDtypeStruct((n // 2, half, width), bf16),
            ],
            [in_vmem] * 2,
            ready,
        )

    def totals(parts):
        last = len(bits) - 1
        parts, marks = list(parts), ([], [])
        relative = [[0, order[last]] for order in orders]
        for j in range(2 * last + 1):
            for c, order in enumerate(orders):
                lag = j - 2 + c
                bit = order[min(j, 2 * last - j)]
                ready = [marks[1 - c][lag]] if lag >= 0 else [parts[1][1]] if lag == -1 and j else []
                if j <= last:
                    keep, send = parts[c]
                    value = keep + flip(after(send, *ready), bit).astype(f32)
                if j < last - 1:
                    parts[c] = (value[0::2], value[1::2].astype(bf16))
                elif j == last - 1:
                    turned = jnp.concatenate([value[1:], value[:1]], axis=0)
                    parts[c] = (value, turned.astype(bf16))
                elif j == last:
                    parts[c] = (None, value.astype(bf16))
                else:
                    near = after(parts[c][1], *ready)
                    far = flip(near, bit)
                    relative[c] = relative[c] + [e ^ bit for e in relative[c]]
                    both = (near, far) if j == 2 * last else (jnp.concatenate([near, far], axis=0),)
                    parts[c] = (both[0], both[-1])
                marks[c].append(parts[c][1])
        return [(*pair, order) for pair, order in zip(parts, relative)]

    fit_own = fit(own, orders[0])
    fit_other = fit(other, orders[1], fit_own[:1])
    (near_own, far_own, order_own), (near_other, far_other, order_other) = totals(
        [tuple(fit_own), tuple(fit_other)]
    )

    sums = []
    for first in (0, blocks // 2):
        mine, theirs = call(
            functools.partial(apply_kernel, (order_own, order_other), first),
            "apply",
            chunk_table,
            [integrals, near_own, far_own, near_other, far_other],
            [
                jax.ShapeDtypeStruct((blocks // 2, half, pairs), f32),
                jax.ShapeDtypeStruct((blocks // 2, half, pairs), bf16),
            ],
            [in_vmem] * 2,
            sums[:1],
        )
        sums += [mine, swap(after(theirs, *sums[1:2]))]
    sends = call(
        functools.partial(scatter_coulomb_kernel, n, blocks, cap),
        "scatter_coulomb",
        out_table,
        [keeping, *sums],
        [jax.ShapeDtypeStruct((2 * cap, half, pairs), bf16)] * (n // 2)
        + [jax.ShapeDtypeStruct((2 * cap, half, part), bf16)] * (n // 2)
        + [jax.ShapeDtypeStruct((blocks, half, part), bf16)],
        [in_vmem] * (n + 1),
        scratch=[pltpu.VMEM((blocks, half, pairs), bf16)],
    )
    def direct(i, *ready):
        return flip(after(sends[n // 2 + i], *ready), n // 2 + i)

    whole = flip(sends[n], n // 2)
    near = [sends[0], flip(sends[1], 1), flip(sends[2], 2)]
    for d in range(3, n // 2):
        near.append(flip(after(sends[d], near[d - 1]), d))
    far = [direct(0), direct(1, near[1]), direct(2, near[2])]
    passed = call(
        functools.partial(pass_on_kernel, n, cap),
        "pass_on",
        pass_table,
        [whole],
        [jax.ShapeDtypeStruct((2 * cap, half, part), bf16)] * (n // 2),
        [in_vmem] * (n // 2),
        near[1:3],
    )
    passed = [passed[0], flip(passed[1], 1)] + [
        flip(after(passed[d], far[min(d - 2, 1)]), d) for d in range(2, n // 2)
    ]
    for i in range(3, n // 2):
        far.append(direct(i, passed[i - 2]))
    return call(
        functools.partial(gather_coulomb_kernel, n, blocks, shell, cap),
        "gather_coulomb",
        in_table,
        [*near, *passed, *far],
        [jax.ShapeDtypeStruct((blocks, pairs, half), bf16)] * 2,
        [anywhere] * 2,
        scratch=[
            pltpu.VMEM((2, blocks, half, pairs), bf16),
            pltpu.VMEM((2, blocks, pairs, half), bf16),
            pltpu.SemaphoreType.DMA((2, blocks)),
        ],
    )


def solution(mesh):
    in_specs = (
        P(("mol", "pair"), None, "aux"),
        P(("mol", "pair"), None, None),
        P(("mol", "pair"), None),
        P(("mol", "pair"), None),
        P("mol"),
        P("mol"),
    )
    out_specs = (P(("mol", "pair"), None, "aux"), P(("mol", "pair"), None, "aux"))
    return jax.shard_map(local, mesh=mesh, in_specs=in_specs, out_specs=out_specs, check_vma=False)
```

```python
import functools
import math

import jax
import jax.numpy as jnp
from jax import lax
from jax.experimental import pallas as pl
from jax.experimental.pallas import tpu as pltpu
from jax.sharding import PartitionSpec as P

VMEM_BYTES = 20 * 1024 * 1024


def tables(slots, devices, blocks_dev, me):
    total = slots.shape[0]
    numbers = jnp.arange(total, dtype=jnp.int32)
    source = numbers // blocks_dev
    target = slots // blocks_dev
    joined = source * devices + target
    earlier = (joined[:, None] == joined[None, :]) & (numbers[None, :] < numbers[:, None])
    rank = jnp.sum(earlier.astype(jnp.int32), axis=1)
    held = []
    for device in (me, me ^ (devices // 2)):
        for values in (target, rank):
            held.append(lax.dynamic_slice_in_dim(values, device * blocks_dev, blocks_dev, 0))
    rows = me * blocks_dev + jnp.arange(blocks_dev, dtype=jnp.int32)
    hot = slots[None, :] == rows[:, None]
    row_source = jnp.sum(jnp.where(hot, source[None, :], 0), axis=1)
    row_rank = jnp.sum(jnp.where(hot, rank[None, :], 0), axis=1)
    return held[:2], held[2:], (row_source, row_rank)


def slots_of(steps, ranks, devices, cap):
    held = (steps * cap + ranks)[None, :] == jnp.arange(devices * cap, dtype=jnp.int32)[:, None]
    numbers = jnp.arange(steps.shape[0], dtype=jnp.int32)
    return jnp.max(jnp.where(held, numbers[None, :], -1), axis=1)


def load_kernel(source, ready, target, sem):
    copy = pltpu.make_async_copy(source, target, sem)
    copy.start()
    copy.wait()


def scatter_density_kernel(devices, blocks, cap, table, density, *rest):
    sends, turned = rest[:devices], rest[-1]
    for row in range(blocks):
        turned[row] = density[row].T
    for step in range(devices):
        for rank in range(cap):
            row = jnp.maximum(table[step * cap + rank], 0)
            sends[step][rank] = turned[row]


def gather_density_kernel(steps, cap, table, *rest):
    out = rest[-1]
    for step, piece in zip(steps, rest):
        for rank in range(cap):
            row = table[step * cap + rank]

            @pl.when(row >= 0)
            def _():
                out[row] = piece[rank]


def fit_kernel(bits, blocks, table, factor, density, integrals, *rest):
    keep, send = rest[-2:]
    width = keep.shape[2]
    pairs = integrals.shape[1]
    fitted = jnp.concatenate([density[b] * factor[b] for b in range(blocks)], axis=1)
    for i in range(keep.shape[0]):
        e = sum(bit for j, bit in enumerate(bits[1:]) if i >> j & 1)
        for relative, out in ((e ^ bits[0], send), (e, keep)):
            at = pl.ds(pl.multiple_of(table[relative] * width, width), width)
            out[i] = jnp.dot(
                fitted,
                integrals[:, :, at].reshape(blocks * pairs, width),
                preferred_element_type=jnp.float32,
            ).astype(out.dtype)


def apply_kernel(orders, some, table, integrals, near, far, near_other, far_other, own, other):
    blocks, pairs, half = integrals.shape[0], integrals.shape[1], own.shape[1]
    count, _, width = near.shape
    chunks = []
    for order, low, high in ((orders[0], near, far), (orders[1], near_other, far_other)):
        chunks.append({e: (low, i) if i < count else (high, i - count) for i, e in enumerate(order)})
    for first in range(0, blocks, some):
        total = None
        for e in range(2 * count):
            at = pl.ds(pl.multiple_of(table[e] * width, width), width)
            term = lax.dot_general(
                integrals[first : first + some, :, at].reshape(some * pairs, width),
                jnp.concatenate([piece[e][0][piece[e][1]] for piece in chunks], axis=0),
                (((1,), (1,)), ((), ())),
                preferred_element_type=jnp.float32,
            )
            total = term if total is None else total + term
        for b in range(some):
            value = total[b * pairs : (b + 1) * pairs].T
            own[first + b] = value[:half]
            other[first + b] = value[half:].astype(other.dtype)


def scatter_coulomb_kernel(devices, blocks, cap, table, screen, own, other, *rest):
    near, far, whole, ready = rest[: devices // 2], rest[devices // 2 : devices], rest[-2], rest[-1]
    part = whole.shape[2]
    for b in range(blocks):
        value = (own[b] + other[b].astype(jnp.float32)) * screen[b]
        ready[b] = value.astype(jnp.bfloat16)
        whole[b] = ready[b, :, pl.ds(0, part)]
    for group in range(2):
        for step in range(devices):
            for rank in range(cap):
                b = jnp.maximum(table[(group * devices + step) * cap + rank], 0)
                if step < devices // 2:
                    near[step][group * cap + rank] = ready[b]
                else:
                    far[step - devices // 2][group * cap + rank] = ready[b, :, pl.ds(part, part)]


def pass_on_kernel(devices, cap, table, whole, *rest):
    outs = rest[-(devices // 2) :]
    for group in range(2):
        for step in range(devices // 2):
            for rank in range(cap):
                b = jnp.maximum(table[(group * devices + devices // 2 + step) * cap + rank], 0)
                outs[step][group * cap + rank] = whole[b]


def gather_coulomb_kernel(devices, blocks, shell, cap, table, *rest):
    half = devices // 2
    near, passed, far = rest[:half], rest[half:devices], rest[devices : devices + half]
    rows, cols, landed, done, sems = rest[devices + half :]
    pairs = landed.shape[3]
    part = far[0].shape[2]
    for step in range(devices):
        for group in range(2):
            for rank in range(cap):
                row = table[(group * devices + step) * cap + rank]
                at = group * cap + rank

                @pl.when(row >= 0)
                def _():
                    if step < half:
                        landed[group, row] = near[step][at]
                    else:
                        landed[group, row, :, pl.ds(0, part)] = passed[step - half][at]
                        landed[group, row, :, pl.ds(part, part)] = far[step - half][at]

    to = lax.broadcasted_iota(jnp.int32, (pairs, pairs), 0)
    source = lax.broadcasted_iota(jnp.int32, (pairs, pairs), 1)
    turns = (to, (to % shell) * shell + to // shell)
    copies = []
    for group in range(2):
        turn = (source == turns[group]).astype(jnp.bfloat16)
        for row in range(blocks):
            done[group, row] = lax.dot_general(
                turn,
                landed[group, row],
                (((1,), (1,)), ((), ())),
                preferred_element_type=jnp.float32,
            ).astype(jnp.bfloat16)
            copy = pltpu.make_async_copy(
                done.at[group, row], (rows, cols)[group].at[row], sems.at[group, row]
            )
            copy.start()
            copies.append(copy)
    for copy in copies:
        copy.wait()


def local(three_index, density, screen, pair_shells, home_slot, mirror_slot):
    blocks, pairs, aux_dev = three_index.shape
    ndens = density.shape[2]
    shell = math.isqrt(pairs)
    n = lax.axis_size("pair")
    cores = lax.axis_size("aux")
    me = lax.axis_index("pair")
    core = lax.axis_index("aux")
    half = ndens // cores
    part = pairs // 2
    width = aux_dev // n
    cap = 2 + (blocks - 1) // n
    bf16, f32 = jnp.bfloat16, jnp.float32
    in_vmem = pl.BlockSpec(memory_space=pltpu.VMEM)
    anywhere = pl.BlockSpec(memory_space=pl.ANY)
    ints = functools.partial(jnp.concatenate, axis=0)

    def call(kernel, name, table, args, out_shape, out_specs, ready=(), scratch=()):
        return pl.pallas_call(
            kernel,
            out_shape=out_shape,
            grid_spec=pltpu.PrefetchScalarGridSpec(
                num_scalar_prefetch=1,
                grid=(),
                in_specs=[in_vmem] * len(args) + [anywhere] * len(ready),
                out_specs=out_specs,
                scratch_shapes=list(scratch),
            ),
            compiler_params=pltpu.CompilerParams(vmem_limit_bytes=VMEM_BYTES),
            name=name,
        )(table, *args, *ready)

    def shift(x, d):
        return lax.ppermute(x, "pair", [(s, (s + d) % n) for s in range(n)])

    def flip(x, bit):
        return lax.ppermute(x, "pair", [(s, s ^ bit) for s in range(n)])

    def swap(x):
        return lax.ppermute(x, "aux", [(s, (s + 1) % cores) for s in range(cores)])

    def after(x, *others):
        return lax.optimization_barrier((x, *others))[0]

    def slots(peers, ranks, device):
        return slots_of(peers ^ device, ranks, n, cap)

    home_held, home_passed, home_rows = tables(home_slot, n, blocks, me)
    send_table = ints(
        [slots_of((home_rows[0] - me) % n, home_rows[1], n, cap), core[None].astype(jnp.int32)]
    )
    pick_table = slots_of((me - home_held[0]) % n, home_held[1], n, cap)
    chunk_table = me ^ jnp.arange(n, dtype=jnp.int32)
    weight = jnp.where(pair_shells[:, 0] != pair_shells[:, 1], 2.0, 1.0)
    factor = (screen.astype(f32) * weight[:, None]).astype(bf16)[:, None, :]
    keeping = screen.astype(f32)[:, None, :]

    sends = pl.pallas_call(
        functools.partial(scatter_density_kernel, n, blocks, cap),
        out_shape=[jax.ShapeDtypeStruct((cap, half, pairs), bf16)] * n,
        grid_spec=pltpu.PrefetchScalarGridSpec(
            num_scalar_prefetch=1,
            grid=(1,),
            in_specs=[pl.BlockSpec((blocks, pairs, half), lambda i, t: (0, 0, t[n * cap]))],
            out_specs=[pl.BlockSpec((cap, half, pairs), lambda i, t: (0, 0, 0))] * n,
            scratch_shapes=[pltpu.VMEM((blocks, half, pairs), bf16)],
        ),
        compiler_params=pltpu.CompilerParams(vmem_limit_bytes=VMEM_BYTES),
        name="scatter_density",
    )(send_table, density)
    steps = sorted(range(1, n), key=lambda d: (min(d, n - d) > 1, abs(2 * d - n)))
    received = []
    for i, d in enumerate(steps):
        received.append(shift(after(sends[d], *received[: max(i - 4, 0)][-1:]), d))
    integrals = pl.pallas_call(
        load_kernel,
        out_shape=pltpu.VMEM((blocks, pairs, aux_dev), bf16),
        in_specs=[anywhere, anywhere],
        out_specs=in_vmem,
        scratch_shapes=[pltpu.SemaphoreType.DMA],
        compiler_params=pltpu.CompilerParams(vmem_limit_bytes=2 * 1024 * 1024),
        name="load_integrals",
    )(three_index, received[1])
    received.append(sends[0])
    steps = (*steps, 0)
    own = call(
        functools.partial(gather_density_kernel, steps, cap),
        "gather_density",
        pick_table,
        received,
        jax.ShapeDtypeStruct((blocks, half, pairs), bf16),
        in_vmem,
        [integrals],
    )
    other = swap(own)

    mirror_held, mirror_passed, mirror_rows = tables(after(mirror_slot, own), n, blocks, me)
    out_table = ints([slots(*home_held, me), slots(*mirror_held, me)])
    pass_table = ints([slots(*held, me ^ (n // 2)) for held in (home_passed, mirror_passed)])
    in_table = ints([slots(*home_rows, me), slots(*mirror_rows, me)])

    bits = [1 << j for j in range(n.bit_length() - 1)]
    orders = (bits, bits[1::-1] + bits[2:])

    def fit(value, bits, ready=()):
        return call(
            functools.partial(fit_kernel, bits, blocks),
            "fit",
            chunk_table,
            [factor, value, integrals],
            [
                jax.ShapeDtypeStruct((n // 2, half, width), f32),
                jax.ShapeDtypeStruct((n // 2, half, width), bf16),
            ],
            [in_vmem] * 2,
            ready,
        )

    def totals(parts):
        last = len(bits) - 1
        parts, marks = list(parts), ([], [])
        relative = [[0, order[last]] for order in orders]
        for j in range(2 * last + 1):
            for c, order in enumerate(orders):
                lag = j - 2 + c
                bit = order[min(j, 2 * last - j)]
                ready = [marks[1 - c][lag]] if lag >= 0 else [parts[1][1]] if lag == -1 and j else []
                if j <= last:
                    keep, send = parts[c]
                    value = keep + flip(after(send, *ready), bit).astype(f32)
                if j < last - 1:
                    parts[c] = (value[0::2], value[1::2].astype(bf16))
                elif j == last - 1:
                    turned = jnp.concatenate([value[1:], value[:1]], axis=0)
                    parts[c] = (value, turned.astype(bf16))
                elif j == last:
                    parts[c] = (None, value.astype(bf16))
                else:
                    near = after(parts[c][1], *ready)
                    far = flip(near, bit)
                    relative[c] = relative[c] + [e ^ bit for e in relative[c]]
                    both = (near, far) if j == 2 * last else (jnp.concatenate([near, far], axis=0),)
                    parts[c] = (both[0], both[-1])
                marks[c].append(parts[c][1])
        return [(*pair, order) for pair, order in zip(parts, relative)]

    fit_own = fit(own, orders[0])
    fit_other = fit(other, orders[1], fit_own[:1])
    (near_own, far_own, order_own), (near_other, far_other, order_other) = totals(
        [tuple(fit_own), tuple(fit_other)]
    )

    mine, theirs = call(
        functools.partial(apply_kernel, (order_own, order_other), blocks // 2),
        "apply",
        chunk_table,
        [integrals, near_own, far_own, near_other, far_other],
        [
            jax.ShapeDtypeStruct((blocks, half, pairs), f32),
            jax.ShapeDtypeStruct((blocks, half, pairs), bf16),
        ],
        [in_vmem] * 2,
    )
    sends = call(
        functools.partial(scatter_coulomb_kernel, n, blocks, cap),
        "scatter_coulomb",
        out_table,
        [keeping, mine, swap(theirs)],
        [jax.ShapeDtypeStruct((2 * cap, half, pairs), bf16)] * (n // 2)
        + [jax.ShapeDtypeStruct((2 * cap, half, part), bf16)] * (n // 2)
        + [jax.ShapeDtypeStruct((blocks, half, part), bf16)],
        [in_vmem] * (n + 1),
        scratch=[pltpu.VMEM((blocks, half, pairs), bf16)],
    )
    def direct(i, *ready):
        return flip(after(sends[n // 2 + i], *ready), n // 2 + i)

    whole = flip(sends[n], n // 2)
    near = [sends[0], flip(sends[1], 1), flip(sends[2], 2)]
    for d in range(3, n // 2):
        near.append(flip(after(sends[d], near[d - 1]), d))
    far = [direct(0), direct(1, near[2]), direct(2, near[2])]
    passed = call(
        functools.partial(pass_on_kernel, n, cap),
        "pass_on",
        pass_table,
        [whole],
        [jax.ShapeDtypeStruct((2 * cap, half, part), bf16)] * (n // 2),
        [in_vmem] * (n // 2),
        near[1:3],
    )
    passed = [passed[0], flip(passed[1], 1)] + [
        flip(after(passed[d], far[min(d - 2, 1)]), d) for d in range(2, n // 2)
    ]
    for i in range(3, n // 2):
        far.append(direct(i, passed[i - 2]))
    return call(
        functools.partial(gather_coulomb_kernel, n, blocks, shell, cap),
        "gather_coulomb",
        in_table,
        [*near, *passed, *far],
        [jax.ShapeDtypeStruct((blocks, pairs, half), bf16)] * 2,
        [anywhere] * 2,
        scratch=[
            pltpu.VMEM((2, blocks, half, pairs), bf16),
            pltpu.VMEM((2, blocks, pairs, half), bf16),
            pltpu.SemaphoreType.DMA((2, blocks)),
        ],
    )


def solution(mesh):
    in_specs = (
        P(("mol", "pair"), None, "aux"),
        P(("mol", "pair"), None, None),
        P(("mol", "pair"), None),
        P(("mol", "pair"), None),
        P("mol"),
        P("mol"),
    )
    out_specs = (P(("mol", "pair"), None, "aux"), P(("mol", "pair"), None, "aux"))
    return jax.shard_map(local, mesh=mesh, in_specs=in_specs, out_specs=out_specs, check_vma=False)
```
